32 devices in a mesh: seq: 16 (over z, x, core), rows: 2 (over y).
Axes of the slice: x: 2, y: 2, z: 4, core: 2. Of those that a mesh axis runs over, the one named last changes fastest.
Arguments:
- tokens: bfloat16 [2048, 4, 512], P('seq', 'rows'), may hold values from -6 to 6
- memory: bfloat16 [1024, 4, 512], P('seq', 'rows'), may hold values from -6 to 6
- segments: int32 [4, 2048], P('rows', 'seq'), may hold values from 0 to 1023, as said below
- padding: int32 [4, 2048], P('rows', 'seq'), may hold values from 0 to 1, as said below
- cotangent: bfloat16 [2048, 4, 512], P('seq', 'rows'), may hold values from -6 to 6
- self_project: bfloat16 [512, 1536], replicated, may hold values from -0.25 to 0.25
- self_output: bfloat16 [512, 512], replicated, may hold values from -1 to 1
- cross_query: bfloat16 [512, 512], replicated, may hold values from -0.25 to 0.25
- cross_memory: bfloat16 [512, 1024], replicated, may hold values from -0.25 to 0.25
- cross_output: bfloat16 [512, 512], replicated, may hold values from -1 to 1
- feed_in: bfloat16 [512, 2048], replicated, may hold values from -0.25 to 0.25
- feed_in_bias: float32 [2048], replicated, may hold values from -3 to 3
- feed_out: bfloat16 [2048, 512], replicated, may hold values from -0.125 to 0.125
- feed_out_bias: float32 [512], replicated, may hold values from -3 to 3
- norm_gain: float32 [3, 512], replicated, may hold values from 0.25 to 1.75
- norm_bias: float32 [3, 512], replicated, may hold values from -3 to 3
- residual_scale: float32 [3, 512], replicated, may hold values from 0.6 to 2.5
Outputs:
- output: bfloat16 [2048, 4, 512], P('seq', 'rows')
- tokens_grad: float32 [2048, 4, 512], P('seq', 'rows')
- memory_grad: float32 [1024, 4, 512], P('seq', 'rows')
- self_project_grad: float32 [512, 1536], P('seq')
- self_output_grad: float32 [512, 512], P('seq')
- cross_query_grad: float32 [512, 512], P('seq')
- cross_memory_grad: float32 [512, 1024], P('seq')
- cross_output_grad: float32 [512, 512], P('seq')
- feed_in_grad: float32 [512, 2048], P('seq')
- feed_in_bias_grad: float32 [2048], P('seq')
- feed_out_grad: float32 [2048, 512], P('seq')
- feed_out_bias_grad: float32 [512], P('seq')
- norm_gain_grad: float32 [3, 512], P(None, 'seq')
- norm_bias_grad: float32 [3, 512], P(None, 'seq')
- residual_scale_grad: float32 [3, 512], P(None, 'seq')
The draws below stay inside these ranges and needn't reach their ends.
Inputs may be any that keep to these rules, and one draw needn't show every extreme that they name: `segments`: rows come in aligned pairs. In each pair one row, which one drawn from the seed, is a document row: segment 0 at every position. The other is packed: its ids never fall, change only at even positions, each id covers 2 to 62 positions (the last one possibly fewer, at least 2), and the id of its last segment is exactly 1023. `padding`: 1 on every position of document rows. On a packed row it is 0 exactly on the positions of its last segment, in some packed rows, and 1 elsewhere.
All inputs are finite; a program needn't handle non-finite values.
Results may differ from the reference program's by a relative error of at most 0.025.
Values may be sent and summed in bfloat16 or wider, within the bound.
A program may use at most 256 MiB of HBM per device.

```python
import math
import jax
import jax.numpy as jnp
from jax import lax

D = 512
HEADS = 8
FF = 2048
SENT = 64
LEN = 2048
MEMLEN = 1024
ROWS = 4


def packed_layout(key):
    units = LEN // 2
    choose = jax.random.randint(jax.random.fold_in(key, 101), (ROWS // 2,), 0, 2)
    first_kind = (choose == 0).astype(jnp.int32)
    document = jnp.stack([first_kind, 1 - first_kind], 1).reshape(ROWS)
    spans = jax.random.randint(jax.random.fold_in(key, 102), (ROWS, units), 1, SENT // 2)
    ends = jnp.cumsum(spans, 1)
    flags = jnp.zeros((ROWS, units), jnp.int32).at[jnp.arange(ROWS)[:, None], ends].set(1, mode='drop')
    unit_ids = jnp.cumsum(flags, 1)
    shifted = unit_ids + (units - 1 - unit_ids[:, -1:])
    identities = jnp.repeat(shifted, 2, axis=1)
    return (identities * (1 - document)[:, None], document)


def draw_segments(key, part):
    identities, document = packed_layout(key)
    return identities.astype(jnp.int32)


def draw_padding(key, part):
    identities, document = packed_layout(key)
    key = jax.random.fold_in(key, 2)
    marked = jax.random.randint(key, (ROWS,), 0, 4)
    final_ids = identities[:, -1:]
    tail = (identities == final_ids) & (document[:, None] == 0) & (marked[:, None] != 0)
    return (1 - tail.astype(jnp.int32)).astype(jnp.int32)


def block_scale(key, shape, shards, low, high):
    def one(axis_at, parts):
        steps = jax.random.uniform(jax.random.fold_in(jax.random.fold_in(key, 6), axis_at), (parts,), jnp.float32, low / len(shards), high / len(shards))
        return jnp.repeat(jnp.exp(steps), shape[axis_at] // parts).reshape((-1,) + (1,) * (len(shape) - axis_at - 1))

    loudness = one(*shards[0])
    for cut in shards[1:]:
        loudness = loudness * one(*cut)
    return loudness


def bell_draw(stream_key, dims, spread, limit, shards=(), held_as=jnp.bfloat16):
    loudness = block_scale(stream_key, dims, shards, -0.22, 0.18) if shards else 1.0
    result = jax.random.normal(stream_key, dims, jnp.float32) * spread * loudness
    return jnp.minimum(jnp.maximum(result, -limit), limit).astype(held_as)


def setup_inputs(seed: int = 0) -> dict:
    streams_of = jax.random.split(jax.random.key(seed), 18)
    tokens = bell_draw(streams_of[0], (LEN, ROWS, D), 1.0, 6.0, ((0, 16), (1, 2)))
    memory = bell_draw(streams_of[1], (MEMLEN, ROWS, D), 1.0, 6.0, ((0, 16), (1, 2)))
    segments = draw_segments(jax.random.fold_in(streams_of[17], 71), 0)
    padding = draw_padding(jax.random.fold_in(streams_of[17], 71), 0)
    cotangent = bell_draw(streams_of[4], (LEN, ROWS, D), 1.0, 6.0, ((0, 16), (1, 2)))
    self_project = bell_draw(streams_of[5], (D, 3 * D), D ** -0.5, 0.25)
    self_output = bell_draw(streams_of[6], (D, D), (D // 16) ** -0.5, 1.0)
    cross_query = bell_draw(streams_of[7], (D, D), D ** -0.5, 0.25)
    cross_memory = bell_draw(streams_of[8], (D, 2 * D), D ** -0.5, 0.25)
    cross_output = bell_draw(streams_of[9], (D, D), (D // 16) ** -0.5, 1.0)
    feed_in = bell_draw(streams_of[10], (D, FF), D ** -0.5, 0.25)
    feed_in_bias = bell_draw(streams_of[11], (FF,), 0.5, 3.0, (), jnp.float32)
    feed_out = bell_draw(streams_of[12], (FF, D), FF ** -0.5, 0.125)
    feed_out_bias = bell_draw(streams_of[13], (D,), 0.3, 3.0, (), jnp.float32)
    norm_gain = jnp.clip(1.0 + 0.15 * jax.random.normal(streams_of[14], (3, D), jnp.float32), 0.25, 1.75)
    norm_bias = bell_draw(streams_of[15], (3, D), 0.3, 3.0, (), jnp.float32)
    residual_scale = jnp.clip(jnp.exp(jax.random.uniform(streams_of[16], (3, D), jnp.float32, math.log(0.6), math.log(2.5))), 0.6, 2.5)
    return dict(tokens=tokens, memory=memory, segments=segments, padding=padding, cotangent=cotangent, self_project=self_project, self_output=self_output, cross_query=cross_query, cross_memory=cross_memory, cross_output=cross_output, feed_in=feed_in, feed_in_bias=feed_in_bias, feed_out=feed_out, feed_out_bias=feed_out_bias, norm_gain=norm_gain, norm_bias=norm_bias, residual_scale=residual_scale)


EPSILON = 1e-05
NEGATIVE = -1e+30
HIGHEST = lax.Precision.HIGHEST

@jax.custom_vjp
def low(v):
    return lax.optimization_barrier(v.astype(jnp.bfloat16)).astype(jnp.float32)

@jax.custom_vjp
def low_back(v):
    return v

def low_keep(v):
    return (low(v), None)

def low_pass(kept, grad):
    return (grad,)

def back_keep(v):
    return (v, None)

def back_low(kept, grad):
    return (low(grad),)
low.defvjp(low_keep, low_pass)
low_back.defvjp(back_keep, back_low)

def layer_norm(summed, gain_row, shift_row):
    centre = lax.optimization_barrier(jnp.mean(summed, -1, keepdims=True))
    centred = summed - centre
    inverse_std = lax.rsqrt(lax.optimization_barrier(jnp.mean(centred * centred, -1, keepdims=True)) + EPSILON)
    return centred * inverse_std * gain_row + shift_row

def matmul(left, right):
    return jnp.dot(left, right, precision=HIGHEST, preferred_element_type=jnp.float32)

def attend(queries, key_heads, value_heads, allowed_at):
    length, head_count, head_width = queries.shape
    extent = math.gcd(length, 512)
    score_scale = 1.0 / math.sqrt(head_width)
    blocks = queries.reshape(length // extent, extent, head_count, head_width)
    offsets = jnp.arange(length // extent, dtype=jnp.int32) * extent

    def one_block(element):
        portion, offset = element
        raw_scores = low_back(jnp.einsum('qhd,khd->hqk', portion, key_heads, precision=HIGHEST) * score_scale)
        allowed = allowed_at(offset, extent)[None]
        masked = jnp.where(allowed, raw_scores, NEGATIVE)
        highest = lax.optimization_barrier(jnp.max(masked, -1, keepdims=True))
        weights = jnp.where(allowed, jnp.exp(masked - highest), 0.0)
        probabilities = low(weights / lax.optimization_barrier(jnp.sum(weights, -1, keepdims=True)))
        return jnp.einsum('hqk,khd->qhd', probabilities, value_heads, precision=HIGHEST)
    outcome = lax.map(jax.checkpoint(one_block), (blocks, offsets))
    return outcome.reshape(length, head_count * head_width)

def layer_row(token_row, memory_row, segment_row, padding_row, params):
    self_project, self_output, cross_query, cross_memory, cross_output, feed_in, feed_in_bias, feed_out, feed_out_bias, norm_gain, norm_bias, residual_scale = params
    length = token_row.shape[0]
    mem_length = memory_row.shape[0]
    model_width = self_project.shape[0]
    head_width = model_width // HEADS
    projected = low(low_back(matmul(token_row, self_project)))
    queries = projected[:, :model_width].reshape(length, HEADS, head_width)
    key_heads = projected[:, model_width:2 * model_width].reshape(length, HEADS, head_width)
    value_heads = projected[:, 2 * model_width:].reshape(length, HEADS, head_width)
    positions = jnp.arange(length, dtype=jnp.int32)
    memory_segments = segment_row[::2]

    def self_allowed(offset, extent):
        query_places = offset + jnp.arange(extent, dtype=jnp.int32)
        query_segments = lax.dynamic_slice_in_dim(segment_row, offset, extent)
        same_segment = query_segments[:, None] == segment_row[None, :]
        causal = positions[None, :] <= query_places[:, None]
        itself = positions[None, :] == query_places[:, None]
        return same_segment & causal & ((padding_row[None, :] == 1) | itself)

    def cross_allowed(offset, extent):
        query_segments = lax.dynamic_slice_in_dim(segment_row, offset, extent)
        return query_segments[:, None] == memory_segments[None, :]
    self_attended = low(low_back(attend(queries, key_heads, value_heads, self_allowed)))
    first_branch = low_back(matmul(self_attended, self_output))
    hidden1 = layer_norm(token_row * residual_scale[0] + first_branch, norm_gain[0], norm_bias[0])
    cross_queries = low(low_back(matmul(low(hidden1), cross_query))).reshape(length, HEADS, head_width)
    memory_projected = low(low_back(matmul(memory_row, cross_memory)))
    memory_keys = memory_projected[:, :model_width].reshape(mem_length, HEADS, head_width)
    memory_values = memory_projected[:, model_width:].reshape(mem_length, HEADS, head_width)
    cross_attended = low(low_back(attend(cross_queries, memory_keys, memory_values, cross_allowed)))
    second_branch = low_back(matmul(cross_attended, cross_output))
    hidden2 = layer_norm(hidden1 * residual_scale[1] + second_branch, norm_gain[1], norm_bias[1])
    pre_active = low_back(matmul(low(hidden2), feed_in) + feed_in_bias)
    active = low(jax.nn.gelu(pre_active))
    third_branch = low_back(matmul(active, feed_out) + feed_out_bias)
    return layer_norm(hidden2 * residual_scale[2] + third_branch, norm_gain[2], norm_bias[2])

def reference(tokens, memory, segments, padding, cotangent, self_project, self_output, cross_query, cross_memory, cross_output, feed_in, feed_in_bias, feed_out, feed_out_bias, norm_gain, norm_bias, residual_scale):
    params = tuple((weight.astype(jnp.float32) for weight in (self_project, self_output, cross_query, cross_memory, cross_output, feed_in, feed_in_bias, feed_out, feed_out_bias, norm_gain, norm_bias, residual_scale)))
    zeros_start = tuple((jnp.zeros_like(weight) for weight in params))
    streams = (jnp.transpose(tokens.astype(jnp.float32), (1, 0, 2)), jnp.transpose(memory.astype(jnp.float32), (1, 0, 2)), segments, padding, jnp.transpose(cotangent.astype(jnp.float32), (1, 0, 2)))

    def per_row(running, element):
        token_row, memory_row, segment_row, padding_row, cotangent_row = element

        def forward(first_arg, second_arg, weights):
            return layer_row(first_arg, second_arg, segment_row, padding_row, weights)
        outcome, backward = jax.vjp(forward, token_row, memory_row, params)
        token_grad, memory_grad, weight_grads = backward(cotangent_row)
        running = jax.tree.map(lambda left, right: left + right, running, weight_grads)
        return (running, (outcome.astype(jnp.bfloat16), token_grad, memory_grad))
    running, (outcomes, token_grads, memory_grads) = lax.scan(per_row, zeros_start, streams)
    return (jnp.transpose(outcomes, (1, 0, 2)), jnp.transpose(token_grads, (1, 0, 2)), jnp.transpose(memory_grads, (1, 0, 2)), running[0], running[1], running[2], running[3], running[4], running[5], running[6], running[7], running[8], running[9], running[10], running[11])
```

```python
import functools
import math

import jax
import jax.numpy as jnp
from jax import lax
from jax.experimental import pallas as pl
from jax.experimental.pallas import tpu as pltpu
from jax.sharding import PartitionSpec as P

HEADS = 8
EPSILON = 1e-05
NEGATIVE = -1e30
BF = jnp.bfloat16
F32 = jnp.float32
I32 = jnp.int32
MESH = pl.DeviceIdType.MESH
GELU_A = math.sqrt(2.0 / math.pi)
GELU_B = 0.044715


def nn(a, b):
    return jnp.dot(a, b, preferred_element_type=F32)


def nt(a, b):
    return lax.dot_general(a, b, (((1,), (1,)), ((), ())), preferred_element_type=F32)


def tn(a, b):
    return lax.dot_general(a, b, (((0,), (0,)), ((), ())), preferred_element_type=F32)


def log2(value):
    return int(value).bit_length() - 1


def reverse_static(index, bits):
    return sum(((index >> k) & 1) << (bits - 1 - k) for k in range(bits))


class Sizes:
    def __init__(self, n, rows, t, mt, d, ff):
        self.n, self.rows, self.t, self.mt, self.d, self.ff = n, rows, t, mt, d, ff
        self.bits, self.row_bits = log2(n), log2(rows)
        self.split = n // HEADS
        self.hd = d // HEADS
        self.halo = t // 2
        self.mhalo = mt // 2
        self.sums = {
            "fo": (ff // n, d, True),
            "fi": (d // n, ff, True),
            "co": (d // n, d, True),
            "cq": (d // n, d, True),
            "mk": (mt, 2 * d, False),
            "cm": (d // n, 2 * d, True),
            "so": (d // n, d, True),
            "sp": (d // n, 3 * d, True),
        }

    def scratch(self):
        n, t, mt, d, ff, hd = self.n, self.t, self.mt, self.d, self.ff, self.hd
        v, dma = pltpu.VMEM, pltpu.SemaphoreType.DMA
        steps = self.bits + self.row_bits
        spec = dict(
            w_sp=v((d, 3 * d), BF), w_so=v((d, d), BF), w_cq=v((d, d), BF), w_cm=v((d, 2 * d), BF),
            w_co=v((d, d), BF), w_fi=v((d, ff), BF), w_fo=v((ff, d), BF),
            qkvt=v((HEADS, 3 * hd, t), BF), kv=v((n, 2 * hd, t), BF), qt=v((HEADS, hd, t), BF),
            kts=v((hd, n * t), BF), vts=v((hd, n * t), BF),
            ots=v((HEADS, hd, t), BF), otr=v((HEADS, hd, t), BF),
            of=v((HEADS, t, hd), F32), lse=v((HEADS, t, 1), F32),
            dos=v((HEADS, hd, t), BF), dor=v((HEADS, hd, t), BF),
            dqr=v((HEADS, hd, t), BF),
            dkt=v((hd, n * t), F32), dvt=v((hd, n * t), F32),
            dkvr=v((self.split, HEADS, 2 * hd, t), BF),
            qp=v((t, d), BF), ps=v((t + self.halo, 2 * d), BF), pm=v((2 * mt, 2 * d), BF),
            cp=v((8, t), I32), cn=v((8, t), I32),
            lsep=v((HEADS, t, 1), F32), lsec=v((HEADS, t, 1), F32), lsed=v((HEADS, t, 1), F32),
            op=v((t, d), F32), co32=v((2 * t, d), F32),
            dps=v((t + self.halo, 2 * d), F32), dpm=v((2 * mt, 2 * d), F32),
            hss=v((self.halo, 2 * d), BF), hsr=v((self.halo, 2 * d), BF),
            hms=v((mt, 2 * d), BF), hmr=v((mt, 2 * d), BF),
            ag=v((n, mt, 2 * d), BF),
            att=v((2 * t, d), BF), catt=v((2 * t, d), BF), cqv=v((2 * t, d), BF),
            tmp=v((2 * t, d), F32), n1=v((2 * t, d), F32), n2=v((2 * t, d), F32),
            i1=v((2 * t, 1), F32), i2=v((2 * t, 1), F32),
            h1b=v((2 * t, d), BF), h2b=v((2 * t, d), BF),
            act=v((2 * t, ff), BF), dg=v((2 * t, ff), F32),
            dtb=v((2 * t, d), BF), dc=v((2 * t, d), BF), dcq=v((2 * t, d), BF),
            dself=v((t, d), BF), dproj=v((2 * t, 3 * d), BF), dmem=v((2 * mt, 2 * d), BF),
            sm=v((16, d), F32), smr=v((steps, 16, d), F32),
        )
        for name, (r, c, over_rows) in self.sums.items():
            if name != "mk":
                spec["a_" + name] = v((n, r, c), BF)
            spec["r_" + name] = v((n - 1 + (self.row_bits if over_rows else 0), r, c), BF)
            spec["ss_" + name] = dma((steps,))
            spec["rs_" + name] = dma((steps,))
        spec.update(
            sms=dma((steps,)), smrs=dma((steps,)),
            wsem=dma((7,)), ags=dma((self.bits,)), agr=dma((self.bits,)),
            hs=dma((8,)), hr=dma((8,)),
            kvs_s=dma((n,)), kvs_r=dma, q_s=dma((HEADS,)), q_r=dma,
            o_s=dma((HEADS,)), o_r=dma, do_s=dma((HEADS,)), do_r=dma,
            dq_s=dma((HEADS,)), dq_r=dma, dkv_s=dma((n,)), dkv_r=dma,
        )
        return spec


class Refs:
    def __init__(self, names, refs):
        for name, ref in zip(names, refs):
            setattr(self, name, ref)


INPUTS = (
    "x", "mem", "cot", "codes", "segcol",
    "h_sp", "h_so", "h_cq", "h_cm", "h_co", "h_fi", "h_fo",
    "fi_b", "fo_b", "gain", "bias", "scale",
)
OUTPUTS = (
    "out", "dx", "dm", "g_sp", "g_so", "g_cq", "g_cm", "g_co", "g_fi", "g_fo", "g_small",
)


def layer_kernel(z, names, *refs):
    g = Refs(names, refs)
    n, t, mt, d, ff, hd, split = z.n, z.t, z.mt, z.d, z.ff, z.hd, z.split
    half = d // HEADS * 2
    pairs = d // half
    softmax_scale = 1.0 / math.sqrt(hd)
    s = lax.axis_index("seq")
    r = lax.axis_index("rows")
    here = lax.rem(s, n)

    def bit_of(index, k):
        return lax.rem(lax.div(index, 2 ** k), 2)

    def seq_partner(k):
        return s + (1 - 2 * bit_of(s, k)) * 2 ** k

    def row_partner(k):
        return r + (1 - 2 * bit_of(r, k)) * 2 ** k

    nxt = lax.rem(s + 1, n)
    prv = lax.rem(s + n - 1, n)
    place = sum(bit_of(s, k) * 2 ** (z.bits - 1 - k) for k in range(z.bits))
    my_head = lax.div(s, split)
    my_part = lax.rem(s, split)
    own_turn = lax.div(s, split)
    own_rest = lax.rem(s, split)
    own_part = own_rest + lax.rem(own_turn, 2) * (split - 1 - 2 * own_rest)

    barrier = pltpu.get_barrier_semaphore()
    for step in range(1, n):
        pl.semaphore_signal(barrier, inc=1, device_id=(lax.rem(s + step, n), r), device_id_type=MESH)
    for k in range(z.row_bits):
        pl.semaphore_signal(barrier, inc=1, device_id=(s, row_partner(k)), device_id_type=MESH)

    weight_names = ("sp", "cm", "so", "cq", "co", "fi", "fo")
    loads = {}
    for j, name in enumerate(weight_names):
        loads[name] = pltpu.make_async_copy(
            getattr(g, "h_" + name), getattr(g, "w_" + name), g.wsem.at[j]
        )
        loads[name].start()

    def remote(src, dst, ssem, rsem, dev):
        return pltpu.make_async_remote_copy(
            src_ref=src, dst_ref=dst, send_sem=ssem, recv_sem=rsem,
            device_id=dev, device_id_type=MESH,
        )

    class Spread:
        def __init__(self, src, dst, ssem, rsem, dest):
            self.dest = dest
            self.far = remote(src, dst, ssem, rsem, (dest, r))
            self.near = pltpu.make_async_copy(src, dst, rsem)

        def start(self):
            @pl.when(self.dest != s)
            def _():
                self.far.start()

            @pl.when(self.dest == s)
            def _():
                self.near.start()

        def wait_send(self):
            @pl.when(self.dest != s)
            def _():
                self.far.wait_send()

    def wait_whole(ref, sem):
        pltpu.make_async_copy(ref, ref, sem).wait()

    class Sum:
        def __init__(self, name):
            share_rows, columns, over_rows = z.sums[name]
            self.a = g.ag if name == "mk" else getattr(g, "a_" + name)
            self.r = getattr(g, "r_" + name)
            self.ss, self.rs = getattr(g, "ss_" + name), getattr(g, "rs_" + name)
            self.steps = z.bits + (z.row_bits if over_rows else 0)
            self.copies = {}

        def held(self, k):
            if k == 0:
                return self.a, 0, n
            if k <= z.bits:
                first = n - n // 2 ** (k - 1)
                return self.r, first, n // 2 ** k
            return self.r, n - 1 + k - z.bits - 1, 1

        def start(self, k):
            ref, first, blocks = self.held(k)
            into, into_first, into_blocks = self.held(k + 1)
            if k < z.bits:
                count = blocks // 2
                b = bit_of(s, k)
                src = ref.at[pl.ds(first + (1 - b) * count, count)]
                dst = into.at[pl.ds(into_first, count)]
                dev = (seq_partner(k), r)
            else:
                src = ref.at[pl.ds(first, 1)]
                dst = into.at[pl.ds(into_first, 1)]
                dev = (s, row_partner(k - z.bits))
            copy = remote(src, dst, self.ss.at[k], self.rs.at[k], dev)
            copy.start()
            self.copies[k] = copy

        def finish(self, k, out=None):
            self.copies[k].wait()
            ref, first, blocks = self.held(k)
            into, into_first, into_blocks = self.held(k + 1)
            base = first
            if k < z.bits:
                base = first + bit_of(s, k) * (blocks // 2)
            if out is not None:
                out[...] = into[into_first].astype(F32) + ref[base].astype(F32)
                return
            if into_blocks <= 2:
                for j in range(into_blocks):
                    into[into_first + j] = into[into_first + j] + ref[base + j]
            else:
                def add(j, carry):
                    into[into_first + j] = into[into_first + j] + ref[base + j]
                    return carry
                lax.fori_loop(0, into_blocks, add, 0)

        def put(self, owner, value, columns=None):
            where = reverse_static(owner, z.bits)
            if columns is None:
                self.a[where] = value
            else:
                self.a[where, :, columns] = value

    sums = {name: Sum(name) for name in z.sums}

    def put_rows(name, value, columns=None, first_owner=0):
        share = z.sums[name][0]
        value = value.astype(BF)
        for j in range(value.shape[0] // share):
            sums[name].put(first_owner + j, value[j * share:(j + 1) * share], columns)

    def over_rows(count, size, step):
        def one(j, carry):
            step(pl.ds(pl.multiple_of(j * size, size), size))
            return carry
        lax.fori_loop(0, count // size, one, 0)

    def mean(value):
        return jnp.sum(value, -1, keepdims=True) * (1.0 / d)

    def norm_forward(total):
        centred = total - mean(total)
        inverse = lax.rsqrt(mean(centred * centred) + EPSILON)
        return centred * inverse, inverse

    def norm_backward(grad, normed, inverse, gain_row, which):
        scaled = grad * gain_row
        result = inverse * (scaled - mean(scaled) - normed * mean(scaled * normed))
        g.sm[which:which + 1, :] += jnp.sum(grad * normed, 0, keepdims=True)
        g.sm[3 + which:4 + which, :] += jnp.sum(grad, 0, keepdims=True)
        return result

    lane = lax.broadcasted_iota(I32, (t, half), 1)

    def only(value, which):
        keep = (lane < hd) if which == 0 else (lane >= hd)
        return jnp.where(keep, value, jnp.zeros_like(value))

    def both(first, second):
        return jnp.where(lane < hd, first, second)

    def pair_cols(p, offset=0):
        return slice(offset + p * half, offset + (p + 1) * half)

    g.sm[...] = jnp.zeros_like(g.sm)

    loads["sp"].wait()
    for part in range(3):
        cols = slice(part * d, (part + 1) * d)
        doc = nn(g.x[0:t, :], g.w_sp[:, cols]).astype(BF)
        g.qkvt[:, part * hd:(part + 1) * hd, :] = doc.T.reshape(HEADS, hd, t)
    pl.semaphore_wait(barrier, n - 1 + z.row_bits)

    kv_copies = []
    for h in range(HEADS):
        for f in range(split):
            dest = h * split + f
            kv_copies.append(Spread(
                g.qkvt.at[h, pl.ds(hd, 2 * hd)], g.kv.at[here], g.kvs_s.at[dest], g.kvs_r, dest))
    q_copies = [
        Spread(g.qkvt.at[h, pl.ds(0, hd)], g.qt.at[own_turn], g.q_s.at[h], g.q_r, h * split + own_part)
        for h in range(HEADS)
    ]
    for copy in kv_copies + q_copies:
        copy.start()

    packed = nn(g.x[t:, :], g.w_sp[...]).astype(BF)
    g.qp[...] = packed[:, :d]
    g.ps[0:t, :] = packed[:, d:]
    loads["cm"].wait()
    mem_kv = nn(g.mem[...], g.w_cm[...]).astype(BF)
    g.ag[place] = mem_kv[:mt]
    g.pm[z.mhalo:z.mhalo + mt, :] = mem_kv[mt:]

    halo_copies = [
        remote(g.codes, g.cn, g.hs.at[0], g.hr.at[0], (prv, r)),
        remote(g.codes, g.cp, g.hs.at[1], g.hr.at[1], (nxt, r)),
        remote(g.ps.at[pl.ds(t - z.halo, z.halo)], g.ps.at[pl.ds(t, z.halo)],
               g.hs.at[2], g.hr.at[2], (nxt, r)),
        remote(g.pm.at[pl.ds(z.mhalo, z.mhalo)], g.pm.at[pl.ds(z.mhalo + mt, z.mhalo)],
               g.hs.at[3], g.hr.at[3], (prv, r)),
        remote(g.pm.at[pl.ds(mt, z.mhalo)], g.pm.at[pl.ds(0, z.mhalo)],
               g.hs.at[4], g.hr.at[4], (nxt, r)),
    ]
    for copy in halo_copies:
        copy.start()

    class Gather:
        def __init__(self):
            self.copies = {}

        def start(self, k):
            count = 2 ** k
            first = lax.div(place, count) * count
            part = g.ag.at[pl.ds(first, count)]
            self.copies[k] = remote(
                part, part, g.ags.at[k], g.agr.at[k], (seq_partner(z.bits - 1 - k), r))
            self.copies[k].start()

        def finish(self, k):
            self.copies[k].wait()

    gather = Gather()
    gather.start(0)

    for copy in halo_copies[0:3]:
        copy.wait()
    q_at = lax.broadcasted_iota(I32, (t, t), 0)
    k_at = lax.broadcasted_iota(I32, (t, t), 1)
    seg_q = g.segcol[...]

    def self_mask():
        seg_k, pad_k = g.codes[0:1, :], g.codes[1:2, :]
        own = (seg_q == seg_k) & (k_at <= q_at) & ((pad_k == 1) | (k_at == q_at))
        prev = (seg_q == g.cp[2:3, :]) & (g.cp[3:4, :] == 1)
        return own, prev[:, :z.halo]

    def cross_mask():
        at = lax.broadcasted_iota(I32, (1, 2 * mt), 1)
        seg_k = jnp.where(
            at < z.mhalo, g.cp[5:6, :],
            jnp.where(at < z.mhalo + mt, g.codes[4:5, :], g.cn[6:7, :]))
        return seg_q == seg_k

    def softmax_parts(scores):
        top = functools.reduce(jnp.maximum, [jnp.max(b, -1, keepdims=True) for b in scores])
        weights = [jnp.exp(b - top) for b in scores]
        total = functools.reduce(jnp.add, [jnp.sum(w, -1, keepdims=True) for w in weights])
        return weights, total, top + jnp.log(total)

    own_mask, prev_mask = self_mask()
    for p in range(pairs):
        q, k, v = g.qp[:, pair_cols(p)], g.ps[:, pair_cols(p)], g.ps[:, pair_cols(p, d)]
        outs = []
        for w in range(2):
            sc = nt(only(q, w), k) * softmax_scale
            blocks = [jnp.where(own_mask, sc[:, :t], NEGATIVE), jnp.where(prev_mask, sc[:, t:], NEGATIVE)]
            weights, total, lse = softmax_parts(blocks)
            g.lsep[2 * p + w] = lse
            o = nn(weights[0].astype(BF), v[:t]) + nn(weights[1].astype(BF), v[t:])
            outs.append(o / total)
        o = both(*outs)
        g.op[:, pair_cols(p)] = o
        g.att[t:, pair_cols(p)] = o.astype(BF)

    wait_whole(g.kv, g.kvs_r)
    wait_whole(g.qt, g.q_r)
    for j in range(n):
        g.kts[:, j * t:(j + 1) * t] = g.kv[j, 0:hd]
        g.vts[:, j * t:(j + 1) * t] = g.kv[j, hd:]

    wide = split * t
    diag_q = lax.broadcasted_iota(I32, (t, wide), 0)
    diag_k = lax.broadcasted_iota(I32, (t, wide), 1)

    def turn_rest(i):
        return my_part if i % 2 == 0 else split - 1 - my_part

    def diag_mask(i):
        return diag_k <= diag_q + turn_rest(i) * t

    o_copies = []
    for i in range(HEADS):
        q = g.qt[i].T
        low = i * wide
        blocks = []
        if low:
            blocks.append(nn(q, g.kts[:, :low]) * softmax_scale)
        blocks.append(jnp.where(
            diag_mask(i), nn(q, g.kts[:, low:low + wide]) * softmax_scale, NEGATIVE))
        weights, total, lse = softmax_parts(blocks)
        g.lse[i] = lse
        o = nt(weights[-1].astype(BF), g.vts[:, low:low + wide])
        if low:
            o = o + nt(weights[0].astype(BF), g.vts[:, :low])
        o = o / total
        g.of[i] = o
        g.ots[i] = o.T.astype(BF)
        copy = Spread(g.ots.at[i], g.otr.at[my_head], g.o_s.at[i], g.o_r, i * split + turn_rest(i))
        copy.start()
        o_copies.append(copy)
        if i % 2 == 1 and i // 2 < z.bits:
            gather.finish(i // 2)
            if i // 2 + 1 < z.bits:
                gather.start(i // 2 + 1)
    for k in range(HEADS // 2, z.bits):
        gather.finish(k)
        if k + 1 < z.bits:
            gather.start(k + 1)
    for copy in kv_copies + q_copies:
        copy.wait_send()

    loads["so"].wait()
    wait_whole(g.otr, g.o_r)
    g.att[0:t, :] = g.otr[...].reshape(d, t).T
    g.tmp[...] = nn(g.att[...], g.w_so[...])

    def first_norm(rows):
        total = g.x[rows, :].astype(F32) * g.scale[0:1, :] + g.tmp[rows, :]
        normed, inverse = norm_forward(total)
        g.n1[rows, :] = normed
        g.i1[rows, :] = inverse
        g.h1b[rows, :] = (normed * g.gain[0:1, :] + g.bias[0:1, :]).astype(BF)

    over_rows(2 * t, 64, first_norm)
    loads["cq"].wait()
    g.cqv[...] = nn(g.h1b[...], g.w_cq[...]).astype(BF)

    for copy in halo_copies[3:]:
        copy.wait()
    seen = cross_mask()
    for p in range(pairs):
        q, k, v = g.cqv[t:, pair_cols(p)], g.pm[:, pair_cols(p)], g.pm[:, pair_cols(p, d)]
        outs = []
        for w in range(2):
            sc = jnp.where(seen, nt(only(q, w), k) * softmax_scale, NEGATIVE)
            (weights,), total, lse = softmax_parts([sc])
            g.lsec[2 * p + w] = lse
            outs.append(nn(weights.astype(BF), v) / total)
        o = both(*outs)
        g.co32[t:, pair_cols(p)] = o
        g.catt[t:, pair_cols(p)] = o.astype(BF)
    for p in range(pairs):
        q = g.cqv[0:t, pair_cols(p)]
        k = g.ag[:, :, pair_cols(p)].reshape(n * mt, half)
        v = g.ag[:, :, pair_cols(p, d)].reshape(n * mt, half)
        outs = []
        for w in range(2):
            sc = nt(only(q, w), k) * softmax_scale
            (weights,), total, lse = softmax_parts([sc])
            g.lsed[2 * p + w] = lse
            outs.append(nn(weights.astype(BF), v) / total)
        o = both(*outs)
        g.co32[0:t, pair_cols(p)] = o
        g.catt[0:t, pair_cols(p)] = o.astype(BF)
    for copy in o_copies:
        copy.wait_send()

    loads["co"].wait()
    g.tmp[...] = nn(g.catt[...], g.w_co[...])

    def second_norm(rows):
        hidden1 = g.n1[rows, :] * g.gain[0:1, :] + g.bias[0:1, :]
        normed, inverse = norm_forward(hidden1 * g.scale[1:2, :] + g.tmp[rows, :])
        g.n2[rows, :] = normed
        g.i2[rows, :] = inverse
        g.h2b[rows, :] = (normed * g.gain[1:2, :] + g.bias[1:2, :]).astype(BF)

    over_rows(2 * t, 64, second_norm)

    loads["fi"].wait()
    chunks = ff // d
    for c in range(chunks):
        cols = slice(c * d, (c + 1) * d)
        pre = nn(g.h2b[...], g.w_fi[:, cols]) + g.fi_b[0:1, cols]
        square = pre * pre
        bent = jnp.tanh(GELU_A * pre * (1.0 + GELU_B * square))
        g.act[:, cols] = (0.5 * pre * (1.0 + bent)).astype(BF)
        g.dg[:, cols] = 0.5 * (1.0 + bent) + 0.5 * pre * (1.0 - bent * bent) * (
            GELU_A * (1.0 + 3.0 * GELU_B * square))
    loads["fo"].wait()
    g.tmp[...] = nn(g.act[...], g.w_fo[...])

    def third_norm(rows):
        hidden2 = g.n2[rows, :] * g.gain[1:2, :] + g.bias[1:2, :]
        total = hidden2 * g.scale[2:3, :] + (g.tmp[rows, :] + g.fo_b[0:1, :])
        normed, inverse = norm_forward(total)
        g.out[rows, :] = (normed * g.gain[2:3, :] + g.bias[2:3, :]).astype(BF)
        grad = g.cot[rows, :].astype(F32)
        back = norm_backward(grad, normed, inverse, g.gain[2:3, :], 2)
        g.sm[8:9, :] += jnp.sum(back * hidden2, 0, keepdims=True)
        g.dx[rows, :] = back
        low = back.astype(BF)
        g.dtb[rows, :] = low
        g.sm[9:10, :] += jnp.sum(low.astype(F32), 0, keepdims=True)

    over_rows(2 * t, 64, third_norm)

    for c in range(chunks):
        cols = slice(c * d, (c + 1) * d)
        put_rows("fo", nn(g.act[:, cols].T, g.dtb[...]), None, c * d // z.sums["fo"][0])
    sums["fo"].start(0)
    for c in range(chunks):
        cols = slice(c * d, (c + 1) * d)
        back = (nt(g.dtb[...], g.w_fo[cols, :]) * g.dg[:, cols]).astype(BF)
        g.act[:, cols] = back
        g.sm[10 + c:11 + c, :] = jnp.sum(back.astype(F32), 0, keepdims=True)
    sums["fo"].finish(0)
    sums["fo"].start(1)
    h2t = g.h2b[...].T
    for c in range(chunks):
        cols = slice(c * d, (c + 1) * d)
        put_rows("fi", nn(h2t, g.act[:, cols]), cols)
    sums["fi"].start(0)
    g.tmp[...] = nt(g.act[...], g.w_fi[...])

    def second_back(rows):
        grad = g.dx[rows, :] * g.scale[2:3, :] + g.tmp[rows, :]
        back = norm_backward(grad, g.n2[rows, :], g.i2[rows, :], g.gain[1:2, :], 1)
        hidden1 = g.n1[rows, :] * g.gain[0:1, :] + g.bias[0:1, :]
        g.sm[7:8, :] += jnp.sum(back * hidden1, 0, keepdims=True)
        g.dx[rows, :] = back
        g.dtb[rows, :] = back.astype(BF)

    over_rows(2 * t, 64, second_back)
    sums["fo"].finish(1)
    sums["fo"].start(2)
    g.dc[...] = nt(g.dtb[...], g.w_co[...]).astype(BF)
    sums["fi"].finish(0)
    sums["fi"].start(1)

    for p in range(pairs):
        q, k, v = g.cqv[t:, pair_cols(p)], g.pm[:, pair_cols(p)], g.pm[:, pair_cols(p, d)]
        go, o = g.dc[t:, pair_cols(p)], g.co32[t:, pair_cols(p)]
        dqs, dk, dv = [], 0.0, 0.0
        for w in range(2):
            qm, gm = only(q, w), only(go, w)
            weights = jnp.where(seen, jnp.exp(nt(qm, k) * softmax_scale - g.lsec[2 * p + w]), 0.0)
            delta = jnp.sum(gm.astype(F32) * o, -1, keepdims=True)
            ds = (weights * (nt(gm, v) - delta)).astype(BF)
            dqs.append(nn(ds, k))
            dk = dk + tn(ds, qm)
            dv = dv + tn(weights.astype(BF), gm)
        g.dcq[t:, pair_cols(p)] = (both(*dqs) * softmax_scale).astype(BF)
        g.dpm[:, pair_cols(p)] = dk * softmax_scale
        g.dpm[:, pair_cols(p, d)] = dv
    g.hms[0:z.mhalo, :] = g.dpm[0:z.mhalo, :].astype(BF)
    g.hms[z.mhalo:, :] = g.dpm[z.mhalo + mt:, :].astype(BF)
    mem_halo = [
        remote(g.hms.at[pl.ds(0, z.mhalo)], g.hmr.at[pl.ds(z.mhalo, z.mhalo)],
               g.hs.at[5], g.hr.at[5], (prv, r)),
        remote(g.hms.at[pl.ds(z.mhalo, z.mhalo)], g.hmr.at[pl.ds(0, z.mhalo)],
               g.hs.at[6], g.hr.at[6], (nxt, r)),
    ]
    for copy in mem_halo:
        copy.start()
    sums["fo"].finish(2)
    sums["fo"].start(3)

    for p in range(pairs):
        q, go, o = g.cqv[0:t, pair_cols(p)], g.dc[0:t, pair_cols(p)], g.co32[0:t, pair_cols(p)]
        qt, gt = q.T, go.T
        k = g.ag[:, :, pair_cols(p)].reshape(n * mt, half)
        v = g.ag[:, :, pair_cols(p, d)].reshape(n * mt, half)
        dqs, dks, dvs = [], [], []
        for w in range(2):
            qm, gm = only(q, w), only(go, w)
            weights = jnp.exp(nt(qm, k) * softmax_scale - g.lsed[2 * p + w])
            delta = jnp.sum(gm.astype(F32) * o, -1, keepdims=True)
            ds = (weights * (nt(gm, v) - delta)).astype(BF)
            dqs.append(nn(ds, k))
            dks.append(nn(qt[w * hd:(w + 1) * hd], ds))
            dvs.append(nn(gt[w * hd:(w + 1) * hd], weights.astype(BF)))
        g.dcq[0:t, pair_cols(p)] = (both(*dqs) * softmax_scale).astype(BF)
        dk = (jnp.concatenate(dks, 0) * softmax_scale).astype(BF).T
        dv = jnp.concatenate(dvs, 0).astype(BF).T
        g.ag[:, :, pair_cols(p)] = dk.reshape(n, mt, half)
        g.ag[:, :, pair_cols(p, d)] = dv.reshape(n, mt, half)
        if p == 1:
            sums["fi"].finish(1)
            sums["fi"].start(2)
    sums["mk"].start(0)

    put_rows("co", nn(g.catt[...].T, g.dtb[...]))
    put_rows("cq", nn(g.h1b[...].T, g.dcq[...]))
    sums["co"].start(0)
    sums["cq"].start(0)
    g.tmp[...] = nt(g.dcq[...], g.w_cq[...])

    def first_back(rows):
        grad = g.dx[rows, :] * g.scale[1:2, :] + g.tmp[rows, :]
        back = norm_backward(grad, g.n1[rows, :], g.i1[rows, :], g.gain[0:1, :], 0)
        g.sm[6:7, :] += jnp.sum(back * g.x[rows, :].astype(F32), 0, keepdims=True)
        g.dx[rows, :] = back
        g.dtb[rows, :] = back.astype(BF)

    over_rows(2 * t, 64, first_back)
    d_self = nt(g.dtb[...], g.w_so[...]).astype(BF)
    g.dself[...] = d_self[t:]
    g.dos[...] = d_self[:t].T.reshape(HEADS, hd, t)
    do_copies = [
        Spread(g.dos.at[h], g.dor.at[own_turn], g.do_s.at[h], g.do_r, h * split + own_part)
        for h in range(HEADS)
    ]
    for copy in do_copies:
        copy.start()
    put_rows("so", nn(g.att[...].T, g.dtb[...]))
    sums["so"].start(0)
    sums["mk"].finish(0)
    sums["mk"].start(1)
    sums["fo"].finish(3)
    sums["fo"].start(4)
    for name in ("co", "cq"):
        sums[name].finish(0)
        sums[name].start(1)

    for p in range(pairs):
        q, k, v = g.qp[:, pair_cols(p)], g.ps[:, pair_cols(p)], g.ps[:, pair_cols(p, d)]
        go, o = g.dself[:, pair_cols(p)], g.op[:, pair_cols(p)]
        dqs, dk, dv = [], 0.0, 0.0
        for w in range(2):
            qm, gm = only(q, w), only(go, w)
            sc = nt(qm, k) * softmax_scale - g.lsep[2 * p + w]
            weights = jnp.concatenate(
                [jnp.where(own_mask, jnp.exp(sc[:, :t]), 0.0),
                 jnp.where(prev_mask, jnp.exp(sc[:, t:]), 0.0)], 1)
            delta = jnp.sum(gm.astype(F32) * o, -1, keepdims=True)
            ds = (weights * (nt(gm, v) - delta)).astype(BF)
            dqs.append(nn(ds, k))
            dk = dk + tn(ds, qm)
            dv = dv + tn(weights.astype(BF), gm)
        g.dproj[t:, pair_cols(p)] = (both(*dqs) * softmax_scale).astype(BF)
        g.dps[:, pair_cols(p)] = dk * softmax_scale
        g.dps[:, pair_cols(p, d)] = dv
    g.hss[...] = g.dps[t:, :].astype(BF)
    self_halo = remote(g.hss, g.hsr, g.hs.at[7], g.hr.at[7], (prv, r))
    self_halo.start()
    sums["fi"].finish(2)
    sums["fi"].start(3)
    sums["mk"].finish(1)
    sums["mk"].start(2)

    wait_whole(g.dor, g.do_r)
    g.dkt[...] = jnp.zeros_like(g.dkt)
    g.dvt[...] = jnp.zeros_like(g.dvt)
    dq_copies, dkv_copies = [], []
    chunk = min(512, n * t)
    for i in reversed(range(HEADS)):
        qt, gt = g.qt[i], g.dor[i]
        q, go = qt.T, gt.T
        delta = jnp.sum(go.astype(F32) * g.of[i], -1, keepdims=True)
        lse = g.lse[i]
        low = i * wide
        spans = [(a, min(a + chunk, low), False) for a in range(0, low, chunk)]
        spans.append((low, low + wide, True))
        dq = 0.0
        for first, last, masked in spans:
            k, v = g.kts[:, first:last], g.vts[:, first:last]
            weights = jnp.exp(nn(q, k) * softmax_scale - lse)
            if masked:
                weights = jnp.where(diag_mask(i), weights, 0.0)
            ds = (weights * (nn(go, v) - delta)).astype(BF)
            dq = dq + nt(ds, k)
            g.dkt[:, first:last] += nn(qt, ds)
            g.dvt[:, first:last] += nn(gt, weights.astype(BF))
        g.ots[i] = (dq * softmax_scale).T.astype(BF)
        copy = Spread(g.ots.at[i], g.dqr.at[my_head], g.dq_s.at[i], g.dq_r, i * split + turn_rest(i))
        copy.start()
        dq_copies.append(copy)
        for j in range(i * split, (i + 1) * split):
            g.kv[j, 0:hd] = (g.dkt[:, j * t:(j + 1) * t] * softmax_scale).astype(BF)
            g.kv[j, hd:] = g.dvt[:, j * t:(j + 1) * t].astype(BF)
            copy = Spread(g.kv.at[j], g.dkvr.at[my_part, my_head], g.dkv_s.at[j], g.dkv_r, j)
            copy.start()
            dkv_copies.append(copy)
        if i == 6:
            sums["mk"].finish(2)
            sums["mk"].start(3)
        if i == 4:
            sums["fi"].finish(3)
            sums["fi"].start(4)
            for name in ("co", "cq"):
                sums[name].finish(1)
                sums[name].start(2)
            sums["so"].finish(0)
            sums["so"].start(1)
        if i == 2:
            for name in ("co", "cq"):
                sums[name].finish(2)
                sums[name].start(3)
            sums["so"].finish(1)
            sums["so"].start(2)

    for k in range(3, z.bits):
        sums["mk"].finish(k)
        if k + 1 < z.bits:
            sums["mk"].start(k + 1)
    for copy in mem_halo:
        copy.wait()
    ref, first, blocks = sums["mk"].held(z.bits)
    g.dmem[0:mt, :] = ref[first]
    g.dmem[mt:, :] = (g.dpm[z.mhalo:z.mhalo + mt, :] + g.hmr[...].astype(F32)).astype(BF)
    g.dm[...] = nt(g.dmem[...], g.w_cm[...])
    put_rows("cm", nn(g.mem[...].T, g.dmem[...]))
    sums["cm"].start(0)

    self_halo.wait()
    wait_whole(g.dqr, g.dq_r)
    g.dproj[0:t, 0:d] = g.dqr[...].reshape(d, t).T
    wait_whole(g.dkvr, g.dkv_r)
    for part in range(2):
        total = g.dkvr[0, :, part * hd:(part + 1) * hd, :].astype(F32)
        for f in range(1, split):
            total = total + g.dkvr[f, :, part * hd:(part + 1) * hd, :].astype(F32)
        g.dproj[0:t, (part + 1) * d:(part + 2) * d] = total.astype(BF).reshape(d, t).T
    g.dproj[t:2 * t - z.halo, d:] = g.dps[0:t - z.halo, :].astype(BF)
    g.dproj[2 * t - z.halo:, d:] = (g.dps[t - z.halo:t, :] + g.hsr[...].astype(F32)).astype(BF)
    put_rows("sp", nn(g.x[...].T, g.dproj[...]))
    sums["sp"].start(0)

    def small(k):
        dev = (seq_partner(k), r) if k < z.bits else (s, row_partner(k - z.bits))
        return remote(g.sm, g.smr.at[k], g.sms.at[k], g.smrs.at[k], dev)

    g.tmp[...] = nt(g.dproj[...], g.w_sp[...])

    def last(rows):
        g.dx[rows, :] = g.dx[rows, :] * g.scale[0:1, :] + g.tmp[rows, :]

    over_rows(2 * t, 64, last)
    order = ("fo", "fi", "co", "cq", "so", "cm", "sp")
    done = {"fo": 4, "fi": 4, "co": 3, "cq": 3, "so": 2, "cm": 0, "sp": 0}
    for step in range(z.bits + z.row_bits):
        tiny = small(step)
        tiny.start()
        for name in order:
            k = done[name]
            if k >= sums[name].steps:
                continue
            finished = k + 1 == sums[name].steps
            sums[name].finish(k, getattr(g, "g_" + name) if finished else None)
            if not finished:
                sums[name].start(k + 1)
            done[name] = k + 1
        tiny.wait()
        g.sm[...] = g.sm[...] + g.smr[step]
    g.g_small[...] = g.sm[...]
    for copy in do_copies + dq_copies + dkv_copies:
        copy.wait_send()


def on_device(
    mesh_shape,
    tokens, memory, segments, padding, cotangent,
    self_project, self_output, cross_query, cross_memory, cross_output,
    feed_in, feed_in_bias, feed_out, feed_out_bias, norm_gain, norm_bias, residual_scale,
):
    t, _, d = tokens.shape
    mt = memory.shape[0]
    ff = feed_in.shape[1]
    n, rows = mesh_shape
    z = Sizes(n, rows, t, mt, d, ff)

    swap = segments[1, 0] == segments[1, t - 1]

    def ordered(array):
        first, second = array[:, 0], array[:, 1]
        return jnp.concatenate(
            [jnp.where(swap, second, first), jnp.where(swap, first, second)], 0)

    def restored(array):
        first, second = array[:array.shape[0] // 2], array[array.shape[0] // 2:]
        return jnp.stack([jnp.where(swap, second, first), jnp.where(swap, first, second)], 1)

    seg = jnp.where(swap, segments[0], segments[1])
    pad = jnp.where(swap, padding[0], padding[1])
    mem_seg = seg[::2]
    gap = jnp.full((t,), -1, I32)
    tail = jnp.full((t - z.halo,), -1, I32)
    codes = jnp.stack([
        seg, pad,
        jnp.concatenate([seg[t - z.halo:], tail]),
        jnp.concatenate([pad[t - z.halo:], tail]),
        jnp.concatenate([gap[:z.mhalo], mem_seg, gap[:t - z.mhalo - mt]]),
        jnp.concatenate([mem_seg[mt - z.mhalo:], gap[:t - z.mhalo]]),
        jnp.concatenate([gap[:t - z.mhalo], mem_seg[:z.mhalo]]),
        gap,
    ])

    scratch = z.scratch()
    names = INPUTS + OUTPUTS + tuple(scratch)
    vmem, anywhere = pl.BlockSpec(memory_space=pltpu.VMEM), pl.BlockSpec(memory_space=pl.ANY)
    outcome = pl.pallas_call(
        functools.partial(layer_kernel, z, names),
        out_shape=[
            jax.ShapeDtypeStruct((2 * t, d), BF),
            jax.ShapeDtypeStruct((2 * t, d), F32),
            jax.ShapeDtypeStruct((2 * mt, d), F32),
        ] + [
            jax.ShapeDtypeStruct(z.sums[name][:2], F32)
            for name in ("sp", "so", "cq", "cm", "co", "fi", "fo")
        ] + [jax.ShapeDtypeStruct((16, d), F32)],
        in_specs=[vmem] * 5 + [anywhere] * 7 + [vmem] * 5,
        out_specs=[vmem] * len(OUTPUTS),
        scratch_shapes=list(scratch.values()),
        compiler_params=pltpu.CompilerParams(
            collective_id=0, has_side_effects=True, vmem_limit_bytes=62 * 2 ** 20),
        name="layer",
    )(
        ordered(tokens), ordered(memory), ordered(cotangent), codes, seg.reshape(t, 1),
        self_project, self_output, cross_query, cross_memory, cross_output, feed_in, feed_out,
        feed_in_bias.reshape(1, ff), feed_out_bias.reshape(1, d), norm_gain, norm_bias, residual_scale,
    )
    out, dx, dm, g_sp, g_so, g_cq, g_cm, g_co, g_fi, g_fo, small = outcome
    at = lax.axis_index("seq")
    in_bias = lax.dynamic_slice(small[10:10 + ff // d].reshape(ff), (at * (ff // n),), (ff // n,))
    share = lax.dynamic_slice(small, (0, at * (d // n)), (16, d // n))
    return (
        restored(out), restored(dx), restored(dm),
        g_sp, g_so, g_cq, g_cm, g_co, g_fi, in_bias, g_fo, share[9],
        share[0:3], share[3:6], share[6:9],
    )


def solution(mesh):
    in_specs = (
        P("seq", "rows", None), P("seq", "rows", None), P("rows", "seq"), P("rows", "seq"),
        P("seq", "rows", None),
    ) + (P(),) * 12
    out_specs = (P("seq", "rows", None),) * 3 + (
        P("seq", None), P("seq", None), P("seq", None), P("seq", None), P("seq", None),
        P("seq", None), P("seq"), P("seq", None), P("seq"),
        P(None, "seq"), P(None, "seq"), P(None, "seq"),
    )
    shape = (mesh.shape["seq"], mesh.shape["rows"])
    return jax.shard_map(
        functools.partial(on_device, shape),
        mesh=mesh, in_specs=in_specs, out_specs=out_specs, check_vma=False,
    )
```

```python
import functools
import math

import jax
import jax.numpy as jnp
from jax import lax
from jax.experimental import pallas as pl
from jax.experimental.pallas import tpu as pltpu
from jax.sharding import PartitionSpec as P

HEADS = 8
EPSILON = 1e-05
NEGATIVE = -1e30
BF = jnp.bfloat16
F32 = jnp.float32
I32 = jnp.int32
MESH = pl.DeviceIdType.MESH
GELU_A = math.sqrt(2.0 / math.pi)
GELU_B = 0.044715


def nn(a, b):
    return jnp.dot(a, b, preferred_element_type=F32)


def nt(a, b):
    return lax.dot_general(a, b, (((1,), (1,)), ((), ())), preferred_element_type=F32)


def tn(a, b):
    return lax.dot_general(a, b, (((0,), (0,)), ((), ())), preferred_element_type=F32)


def log2(value):
    return int(value).bit_length() - 1


def reverse_static(index, bits):
    return sum(((index >> k) & 1) << (bits - 1 - k) for k in range(bits))


class Sizes:
    def __init__(self, n, rows, t, mt, d, ff):
        self.n, self.rows, self.t, self.mt, self.d, self.ff = n, rows, t, mt, d, ff
        self.bits, self.row_bits = log2(n), log2(rows)
        self.split = n // HEADS
        self.hd = d // HEADS
        self.halo = t // 2
        self.mhalo = mt // 2
        self.sums = {
            "fo": (ff // n, d, "rows first"),
            "fi": (d // n, ff, "rows last"),
            "co": (d // n, d, "rows first"),
            "cq": (d // n, d, "rows first"),
            "mk": (mt, d, "seq alone"),
            "cm": (d // n, 2 * d, "rows last"),
            "so": (d // n, d, "rows last"),
            "sp": (d // n, 3 * d, "rows first"),
        }

    def steps(self, name):
        order = self.sums[name][2]
        seq = [("seq", k) for k in range(self.bits)]
        rows = [("exchange", k) for k in range(self.row_bits)]
        if order == "seq alone":
            return seq
        if order == "rows last":
            return seq + rows
        return seq[:1] + [("halve", 0)] + seq[1:] + rows[1:] + [("gather", 0)]

    def parts(self, name):
        return 2 if self.sums[name][2] == "rows first" else 1

    def received(self, name):
        held, first, spans = self.n * self.parts(name), 0, []
        for kind, _ in self.steps(name):
            held = held // 2 if kind in ("seq", "halve") else held
            spans.append((first, held))
            first += held
        return spans, first

    def scratch(self):
        n, t, mt, d, ff, hd, split = self.n, self.t, self.mt, self.d, self.ff, self.hd, self.split
        v, dma = pltpu.VMEM, pltpu.SemaphoreType.DMA
        small_steps = self.bits + self.row_bits
        spec = dict(
            w_sp=v((d, 3 * d), BF), w_so=v((d, d), BF), w_cq=v((d, d), BF), w_cm=v((d, 2 * d), BF),
            w_co=v((d, d), BF), w_fi=v((d, ff), BF), w_fo=v((ff, d), BF),
            xg=v((n, t, d), BF), mg=v((n, mt, d), BF), mkv=v((n, mt, 2 * d), BF),
            wtp=v((3, 2 * hd, d), BF), wt=v((3 * hd, d), BF),
            qta=v((n, hd, t), BF), kts=v((hd, n * t), BF), vts=v((hd, n * t), BF),
            ots=v((HEADS, hd, t), BF), otr=v((HEADS, hd, t), BF), of=v((HEADS, t, hd), F32),
            dos=v((HEADS, hd, t), BF), dor=v((HEADS, hd, t), BF), dqr=v((HEADS, hd, t), BF),
            dwt=v((3 * hd, d), F32),
            kvst=v((HEADS, split, 2 * hd, t), BF), kvsib=v((HEADS, split, 2 * hd, t), BF),
            kvfin=v((HEADS, 2 * hd, t), BF), dkvr=v((HEADS, 2 * hd, t), BF),
            dws=v((n, d // n, 4 * hd), BF), dwr=v((n, d // n, 4 * hd), BF),
            dsh=v((d // n, 3 * d), BF), dshr=v((self.row_bits, d // n, 3 * d), BF),
            xw=v((t + self.halo, d), BF), mw=v((2 * mt, d), BF),
            qp=v((t, d), BF), ps=v((t + self.halo, 2 * d), BF), pm=v((2 * mt, 2 * d), BF),
            cp=v((8, t), I32), cn=v((8, t), I32),
            lse=v((t, 4 * HEADS), F32),
            op=v((t, d), F32), co32=v((2 * t, d), F32),
            dmp=v((2 * mt, d), F32), dxp=v((t + self.halo, d), F32),
            hss=v((self.halo, d), BF), hsr=v((self.halo, d), BF),
            hms=v((mt, d), BF), hmr=v((mt, d), BF),
            att=v((2 * t, d), BF), catt=v((2 * t, d), BF), cqv=v((2 * t, d), BF),
            tmp=v((2 * t, d), F32), n1=v((2 * t, d), F32), n2=v((2 * t, d), F32),
            i1=v((2 * t, 1), F32), i2=v((2 * t, 1), F32),
            h1b=v((2 * t, d), BF), h2b=v((2 * t, d), BF),
            act=v((2 * t, ff), BF), dg=v((2 * t, ff), F32),
            dtb=v((2 * t, d), BF), dc=v((2 * t, d), BF), dcq=v((2 * t, d), BF),
            dself=v((t, d), BF), dproj=v((t, 3 * d), BF),
            sm=v((16, d), F32), smr=v((small_steps, 16, d), F32),
        )
        for name, (r, c, order) in self.sums.items():
            parts = self.parts(name)
            if name != "mk":
                spec["a_" + name] = v((n * parts, r, c // parts), BF)
            spec["r_" + name] = v((self.received(name)[1], r, c // parts), BF)
            spec["ss_" + name] = dma((len(self.steps(name)),))
            spec["rs_" + name] = dma((len(self.steps(name)),))
        spec.update(
            sms=dma((small_steps,)), smrs=dma((small_steps,)),
            wsem=dma((7,)), xgs=dma((4, n)), xgr=dma((n,)), mgs=dma((4, n)), mgr=dma((n,)),
            hs=dma((8,)), hr=dma((8,)),
            o_s=dma((HEADS,)), o_r=dma, do_s=dma((HEADS,)), do_r=dma,
            dq_s=dma((HEADS,)), dq_r=dma, kf_s=dma((HEADS,)), kf_r=dma,
            sib_s=dma((HEADS, split)), sib_r=dma((HEADS, split)),
            dw_s=dma((n,)), dw_r=dma, dy_s=dma((self.row_bits,)), dy_r=dma((self.row_bits,)),
        )
        return spec


class Refs:
    def __init__(self, names, refs):
        for name, ref in zip(names, refs):
            setattr(self, name, ref)


INPUTS = (
    "x", "mem", "cot", "codes", "segcol",
    "h_sp", "h_so", "h_cq", "h_cm", "h_co", "h_fi", "h_fo",
    "fi_b", "fo_b", "gain", "bias", "scale",
)
OUTPUTS = (
    "out", "dx", "dm", "g_sp", "g_so", "g_cq", "g_cm", "g_co", "g_fi", "g_fo", "g_small",
)


def layer_kernel(z, names, *refs):
    g = Refs(names, refs)
    n, t, mt, d, ff, hd, split = z.n, z.t, z.mt, z.d, z.ff, z.hd, z.split
    half = 2 * hd
    pairs = d // half
    softmax_scale = 1.0 / math.sqrt(hd)
    s = lax.axis_index("seq")
    r = lax.axis_index("rows")

    def bit_of(index, k):
        return lax.rem(lax.div(index, 2 ** k), 2)

    def seq_partner(k):
        return s + (1 - 2 * bit_of(s, k)) * 2 ** k

    def row_partner(k):
        return r + (1 - 2 * bit_of(r, k)) * 2 ** k

    def place_of(index):
        return sum(bit_of(index, k) * 2 ** (z.bits - 1 - k) for k in range(z.bits))

    nxt = lax.rem(s + 1, n)
    prv = lax.rem(s + n - 1, n)
    my_head = lax.div(s, split)
    my_part = lax.rem(s, split)
    own_turn = lax.div(s, split)
    own_rest = lax.rem(s, split)
    own_part = own_rest + lax.rem(own_turn, 2) * (split - 1 - 2 * own_rest)

    barrier = pltpu.get_barrier_semaphore()
    for step in range(1, n):
        pl.semaphore_signal(barrier, inc=1, device_id=(lax.rem(s + step, n), r), device_id_type=MESH)
    for k in range(z.row_bits):
        pl.semaphore_signal(barrier, inc=1, device_id=(s, row_partner(k)), device_id_type=MESH)

    loads = {
        name: pltpu.make_async_copy(getattr(g, "h_" + name), getattr(g, "w_" + name), g.wsem.at[j])
        for j, name in enumerate(("sp", "cm", "so", "cq", "co", "fi", "fo"))
    }
    loads["sp"].start()

    def remote(src, dst, ssem, rsem, dev):
        return pltpu.make_async_remote_copy(
            src_ref=src, dst_ref=dst, send_sem=ssem, recv_sem=rsem,
            device_id=dev, device_id_type=MESH,
        )

    class Spread:
        def __init__(self, src, dst, ssem, rsem, dest):
            self.dest = dest
            self.far = remote(src, dst, ssem, rsem, (dest, r))
            self.near = pltpu.make_async_copy(src, dst, rsem)

        def start(self):
            @pl.when(self.dest != s)
            def _():
                self.far.start()

            @pl.when(self.dest == s)
            def _():
                self.near.start()

        def wait_send(self):
            @pl.when(self.dest != s)
            def _():
                self.far.wait_send()

    def wait_whole(ref, sem):
        pltpu.make_async_copy(ref, ref, sem).wait()

    class Chain:
        def __init__(self, buf, send, recv):
            self.buf, self.send, self.recv = buf, send, recv
            self.line = n // 4
            self.zz, self.xx, self.core = lax.div(s, 4), bit_of(s, 1), bit_of(s, 0)

        def copy(self, way, origin):
            dev = (s + 4, s - 4, s + 2 - 4 * self.xx, s + 1 - 2 * self.core)[way]
            at = place_of(origin)
            block = self.buf.at[at]
            return remote(block, block, self.send.at[way, at], self.recv.at[at], (dev, r))

        def arrive(self, origin):
            at = place_of(origin)
            wait_whole(self.buf.at[at], self.recv.at[at])

        def pass_on(self, action, zz, ahead, back):
            origin = s + 4 * (zz - self.zz)
            if ahead:
                @pl.when(self.zz < self.line - 1)
                def _():
                    action(self.copy(0, origin))
            if back:
                @pl.when(self.zz > 0)
                def _():
                    action(self.copy(1, origin))
            action(self.copy(2, origin))
            action(self.copy(3, origin))

        def start(self):
            self.pass_on(lambda c: c.start(), self.zz, True, True)

        def line_step(self, j, action, wait):
            low, high = self.zz - 1 - j, self.zz + 1 + j

            @pl.when(low >= 0)
            def _():
                if wait:
                    self.arrive(s + 4 * (low - self.zz))
                self.pass_on(action, low, True, False)

            @pl.when(high < self.line)
            def _():
                if wait:
                    self.arrive(s + 4 * (high - self.zz))
                self.pass_on(action, high, False, True)

        def step(self, j):
            self.line_step(j, lambda c: c.start(), True)

        def across(self, j, action, wait):
            other = s + 2 - 4 * self.xx
            for sign in ((1,) if j == 0 else (-1, 1)):
                zz = self.zz + sign * j

                @pl.when((zz >= 0) & (zz < self.line))
                def _():
                    origin = other + 4 * (zz - self.zz)
                    if wait:
                        self.arrive(origin)
                    action(self.copy(3, origin))

        def cross_step(self, j):
            self.across(j, lambda c: c.start(), True)

        def finish(self):
            other = s + 1 - 2 * self.core
            for k in range(2 * self.line):
                self.arrive(lax.rem(other, 2) + 2 * k)

        def drain(self):
            done = lambda c: c.wait_send()
            self.pass_on(done, self.zz, True, True)
            for j in range(self.line - 1):
                self.line_step(j, done, False)
            for j in range(self.line):
                self.across(j, done, False)

    class Sum:
        def __init__(self, name):
            self.name, self.out = name, getattr(g, "g_" + name, None)
            self.a = g.mg if name == "mk" else getattr(g, "a_" + name)
            self.r = getattr(g, "r_" + name)
            self.ss, self.rs = getattr(g, "ss_" + name), getattr(g, "rs_" + name)
            self.steps, self.parts = z.steps(name), z.parts(name)
            self.spans = z.received(name)[0]
            self.share, self.columns = z.sums[name][:2]
            self.copies = {}
            self.at = -1

        def held(self, i):
            if i == 0:
                return self.a, 0, n * self.parts
            return (self.r,) + self.spans[i - 1]

        def bit(self, i):
            kind, k = self.steps[i]
            return bit_of(s, k) if kind == "seq" else bit_of(r, k)

        def start(self, i):
            ref, first, blocks = self.held(i)
            into, into_first, count = self.held(i + 1)
            kind, k = self.steps[i]
            src = ref.at[pl.ds(first + (1 - self.bit(i)) * count, count)] if blocks > count else (
                ref.at[pl.ds(first, count)])
            dev = (seq_partner(k), r) if kind == "seq" else (s, row_partner(k))
            self.copies[i] = remote(src, into.at[pl.ds(into_first, count)], self.ss.at[i], self.rs.at[i], dev)
            self.copies[i].start()

        def finish(self, i):
            self.copies[i].wait()
            ref, first, blocks = self.held(i)
            into, into_first, count = self.held(i + 1)
            kind, k = self.steps[i]
            last = i + 1 == len(self.steps)
            if kind == "gather":
                width = self.columns // 2
                mine, theirs = bit_of(r, 0) * width, (1 - bit_of(r, 0)) * width
                self.out[:, pl.ds(pl.multiple_of(mine, width), width)] = ref[first].astype(F32)
                self.out[:, pl.ds(pl.multiple_of(theirs, width), width)] = into[into_first].astype(F32)
                return
            if last and self.out is not None:
                self.out[...] = into[into_first].astype(F32) + ref[first].astype(F32)
                return
            base = first + self.bit(i) * count if blocks > count else first
            if count <= 2:
                for j in range(count):
                    into[into_first + j] = into[into_first + j] + ref[base + j]
            else:
                def add(j, carry):
                    into[into_first + j] = into[into_first + j] + ref[base + j]
                    return carry
                lax.fori_loop(0, count, add, 0)

        def advance(self):
            if self.at == len(self.steps):
                return
            if self.at >= 0:
                self.finish(self.at)
            self.at += 1
            if self.at < len(self.steps):
                self.start(self.at)

        def result(self):
            ref, first, _ = self.held(len(self.steps))
            return ref[first]

        def put(self, owner, value, first_column):
            width = self.columns // self.parts
            core, rest = owner % 2, reverse_static(owner // 2, z.bits - 1)
            for part in range(self.parts):
                low = max(first_column, part * width)
                high = min(first_column + value.shape[1], (part + 1) * width)
                if low < high:
                    where = (core * self.parts + part) * (n // 2) + rest
                    self.a[where, :, low - part * width:high - part * width] = (
                        value[:, low - first_column:high - first_column])

    sums = {name: Sum(name) for name in z.sums}

    def advance(*which):
        for name in which:
            sums[name].advance()

    def put_rows(name, value, first_column=0, first_owner=0):
        share = z.sums[name][0]
        value = value.astype(BF)
        for j in range(value.shape[0] // share):
            sums[name].put(first_owner + j, value[j * share:(j + 1) * share], first_column)

    def over_rows(count, size, step):
        def one(j, carry):
            step(pl.ds(pl.multiple_of(j * size, size), size))
            return carry
        lax.fori_loop(0, count // size, one, 0)

    def mean(value):
        return jnp.sum(value, -1, keepdims=True) * (1.0 / d)

    def norm_forward(total):
        centred = total - mean(total)
        inverse = lax.rsqrt(mean(centred * centred) + EPSILON)
        return centred * inverse, inverse

    def norm_backward(grad, normed, inverse, gain_row, which):
        scaled = grad * gain_row
        result = inverse * (scaled - mean(scaled) - normed * mean(scaled * normed))
        g.sm[which:which + 1, :] += jnp.sum(grad * normed, 0, keepdims=True)
        g.sm[3 + which:4 + which, :] += jnp.sum(grad, 0, keepdims=True)
        return result

    lane = lax.broadcasted_iota(I32, (t, half), 1)

    def only(value, which):
        keep = (lane < hd) if which == 0 else (lane >= hd)
        return jnp.where(keep, value, jnp.zeros_like(value))

    def both(first, second):
        return jnp.where(lane < hd, first, second)

    def pair_cols(p, offset=0):
        return slice(offset + p * half, offset + (p + 1) * half)

    def keep_lse(index, value):
        g.lse[:, index:index + 1] = value

    def kept_lse(index):
        return g.lse[:, index:index + 1]

    SELF_PACKED, CROSS_PACKED, CROSS_DOC, SELF_DOC = (k * HEADS for k in range(4))

    tokens_all = Chain(g.xg, g.xgs, g.xgr)
    memory_all = Chain(g.mg, g.mgs, g.mgr)
    place = place_of(s)
    g.xg[place] = g.x[0:t, :]
    g.mg[place] = g.mem[0:mt, :]
    g.xw[0:t, :] = g.x[t:, :]
    g.mw[z.mhalo:z.mhalo + mt, :] = g.mem[mt:, :]
    g.sm[...] = jnp.zeros_like(g.sm)
    pl.semaphore_wait(barrier, n - 1 + z.row_bits)
    tokens_all.start()
    halo_copies = [
        remote(g.codes, g.cn, g.hs.at[0], g.hr.at[0], (prv, r)),
        remote(g.codes, g.cp, g.hs.at[1], g.hr.at[1], (nxt, r)),
        remote(g.x.at[pl.ds(2 * t - z.halo, z.halo)], g.xw.at[pl.ds(t, z.halo)],
               g.hs.at[2], g.hr.at[2], (nxt, r)),
        remote(g.mem.at[pl.ds(mt, z.mhalo)], g.mw.at[pl.ds(z.mhalo + mt, z.mhalo)],
               g.hs.at[3], g.hr.at[3], (prv, r)),
        remote(g.mem.at[pl.ds(2 * mt - z.mhalo, z.mhalo)], g.mw.at[pl.ds(0, z.mhalo)],
               g.hs.at[4], g.hr.at[4], (nxt, r)),
    ]
    for copy in halo_copies:
        copy.start()

    loads["sp"].wait()
    for name in ("cm", "so", "cq", "co", "fi", "fo"):
        loads[name].start()
    for part in range(3):
        first = pl.multiple_of(part * d + lax.div(my_head, 2) * half, half)
        g.wtp[part] = g.w_sp[:, pl.ds(first, half)].T
        g.wt[part * hd:(part + 1) * hd, :] = g.wtp[
            part, pl.ds(pl.multiple_of(lax.rem(my_head, 2) * hd, hd), hd), :]
    g.qp[...] = nn(g.xw[0:t, :], g.w_sp[:, :d]).astype(BF)
    tokens_all.step(0)
    tokens_all.cross_step(0)

    for copy in halo_copies:
        copy.wait()
    g.ps[...] = nn(g.xw[...], g.w_sp[:, d:]).astype(BF)
    loads["cm"].wait()
    g.pm[...] = nn(g.mw[...], g.w_cm[...]).astype(BF)
    for j in range(1, n // 4 - 1):
        tokens_all.step(j)
        tokens_all.cross_step(j)
    q_at = lax.broadcasted_iota(I32, (t, t), 0)
    k_at = lax.broadcasted_iota(I32, (t, t), 1)
    seg_q = g.segcol[...]

    def self_mask():
        seg_k, pad_k = g.codes[0:1, :], g.codes[1:2, :]
        own = (seg_q == seg_k) & (k_at <= q_at) & ((pad_k == 1) | (k_at == q_at))
        prev = (seg_q == g.cp[2:3, :]) & (g.cp[3:4, :] == 1)
        return own, prev[:, :z.halo]

    def cross_mask():
        at = lax.broadcasted_iota(I32, (1, 2 * mt), 1)
        seg_k = jnp.where(
            at < z.mhalo, g.cp[5:6, :],
            jnp.where(at < z.mhalo + mt, g.codes[4:5, :], g.cn[6:7, :]))
        return seg_q == seg_k

    def softmax_parts(scores):
        top = functools.reduce(jnp.maximum, [jnp.max(b, -1, keepdims=True) for b in scores])
        weights = [jnp.exp(b - top) for b in scores]
        total = functools.reduce(jnp.add, [jnp.sum(w, -1, keepdims=True) for w in weights])
        return weights, total, top + jnp.log(total)

    own_mask, prev_mask = self_mask()
    for p in range(pairs):
        q, k, v = g.qp[:, pair_cols(p)], g.ps[:, pair_cols(p)], g.ps[:, pair_cols(p, d)]
        outs = []
        for w in range(2):
            sc = nt(only(q, w), k) * softmax_scale
            blocks = [jnp.where(own_mask, sc[:, :t], NEGATIVE), jnp.where(prev_mask, sc[:, t:], NEGATIVE)]
            weights, total, lse = softmax_parts(blocks)
            keep_lse(SELF_PACKED + 2 * p + w, lse)
            o = nn(weights[0].astype(BF), v[:t]) + nn(weights[1].astype(BF), v[t:])
            outs.append(o / total)
        o = both(*outs)
        g.op[:, pair_cols(p)] = o
        g.att[t:, pair_cols(p)] = o.astype(BF)

    tokens_all.cross_step(n // 4 - 1)
    tokens_all.finish()
    memory_all.start()

    for b in range(n):
        made = nt(g.wt[...], g.xg[reverse_static(b, z.bits)]).astype(BF)
        g.qta[b] = made[0:hd]
        g.kts[:, b * t:(b + 1) * t] = made[hd:2 * hd]
        g.vts[:, b * t:(b + 1) * t] = made[2 * hd:]

    wide = split * t
    diag_q = lax.broadcasted_iota(I32, (t, wide), 0)
    diag_k = lax.broadcasted_iota(I32, (t, wide), 1)

    def turn_rest(i):
        return my_part if i % 2 == 0 else split - 1 - my_part

    def diag_mask(i):
        return diag_k <= diag_q + turn_rest(i) * t

    o_copies = []
    for i in range(HEADS):
        b = i * split + turn_rest(i)
        q = g.qta[b].T
        low = i * wide
        blocks = []
        if low:
            blocks.append(nn(q, g.kts[:, :low]) * softmax_scale)
        blocks.append(jnp.where(
            diag_mask(i), nn(q, g.kts[:, low:low + wide]) * softmax_scale, NEGATIVE))
        weights, total, lse = softmax_parts(blocks)
        keep_lse(SELF_DOC + i, lse)
        o = nt(weights[-1].astype(BF), g.vts[:, low:low + wide])
        if low:
            o = o + nt(weights[0].astype(BF), g.vts[:, :low])
        o = o / total
        g.of[i] = o
        g.ots[i] = o.T.astype(BF)
        copy = Spread(g.ots.at[i], g.otr.at[my_head], g.o_s.at[i], g.o_r, b)
        copy.start()
        o_copies.append(copy)
        if i in (3, 5) and i // 2 < n // 4:
            memory_all.step((i - 3) // 2)
            memory_all.cross_step((i - 3) // 2)

    for j in range(2, n // 4 - 1):
        memory_all.step(j)
        memory_all.cross_step(j)
    memory_all.cross_step(n // 4 - 1)
    memory_all.finish()

    for part in range(2):
        cols = slice(part * d, (part + 1) * d)
        g.mkv[:, :, cols] = nn(g.mg[...].reshape(n * mt, d), g.w_cm[:, cols]).astype(BF).reshape(n, mt, d)

    loads["so"].wait()
    wait_whole(g.otr, g.o_r)
    g.att[0:t, :] = g.otr[...].reshape(d, t).T
    g.tmp[...] = nn(g.att[...], g.w_so[...])

    def first_norm(rows):
        total = g.x[rows, :].astype(F32) * g.scale[0:1, :] + g.tmp[rows, :]
        normed, inverse = norm_forward(total)
        g.n1[rows, :] = normed
        g.i1[rows, :] = inverse
        g.h1b[rows, :] = (normed * g.gain[0:1, :] + g.bias[0:1, :]).astype(BF)

    over_rows(2 * t, 64, first_norm)
    loads["cq"].wait()
    g.cqv[...] = nn(g.h1b[...], g.w_cq[...]).astype(BF)

    seen = cross_mask()
    for p in range(pairs):
        q, k, v = g.cqv[t:, pair_cols(p)], g.pm[:, pair_cols(p)], g.pm[:, pair_cols(p, d)]
        outs = []
        for w in range(2):
            sc = jnp.where(seen, nt(only(q, w), k) * softmax_scale, NEGATIVE)
            (weights,), total, lse = softmax_parts([sc])
            keep_lse(CROSS_PACKED + 2 * p + w, lse)
            outs.append(nn(weights.astype(BF), v) / total)
        o = both(*outs)
        g.co32[t:, pair_cols(p)] = o
        g.catt[t:, pair_cols(p)] = o.astype(BF)
    for p in range(pairs):
        q = g.cqv[0:t, pair_cols(p)]
        k = g.mkv[:, :, pair_cols(p)].reshape(n * mt, half)
        v = g.mkv[:, :, pair_cols(p, d)].reshape(n * mt, half)
        outs = []
        for w in range(2):
            sc = nt(only(q, w), k) * softmax_scale
            (weights,), total, lse = softmax_parts([sc])
            keep_lse(CROSS_DOC + 2 * p + w, lse)
            outs.append(nn(weights.astype(BF), v) / total)
        o = both(*outs)
        g.co32[0:t, pair_cols(p)] = o
        g.catt[0:t, pair_cols(p)] = o.astype(BF)
    for copy in o_copies:
        copy.wait_send()
    tokens_all.drain()
    memory_all.drain()

    loads["co"].wait()
    g.tmp[...] = nn(g.catt[...], g.w_co[...])

    def second_norm(rows):
        hidden1 = g.n1[rows, :] * g.gain[0:1, :] + g.bias[0:1, :]
        normed, inverse = norm_forward(hidden1 * g.scale[1:2, :] + g.tmp[rows, :])
        g.n2[rows, :] = normed
        g.i2[rows, :] = inverse
        g.h2b[rows, :] = (normed * g.gain[1:2, :] + g.bias[1:2, :]).astype(BF)

    over_rows(2 * t, 64, second_norm)

    loads["fi"].wait()
    chunks = ff // d
    for c in range(chunks):
        cols = slice(c * d, (c + 1) * d)
        pre = nn(g.h2b[...], g.w_fi[:, cols]) + g.fi_b[0:1, cols]
        square = pre * pre
        bent = jnp.tanh(GELU_A * pre * (1.0 + GELU_B * square))
        g.act[:, cols] = (0.5 * pre * (1.0 + bent)).astype(BF)
        g.dg[:, cols] = 0.5 * (1.0 + bent) + 0.5 * pre * (1.0 - bent * bent) * (
            GELU_A * (1.0 + 3.0 * GELU_B * square))
    loads["fo"].wait()
    g.tmp[...] = nn(g.act[...], g.w_fo[...])

    def third_norm(rows):
        hidden2 = g.n2[rows, :] * g.gain[1:2, :] + g.bias[1:2, :]
        total = hidden2 * g.scale[2:3, :] + (g.tmp[rows, :] + g.fo_b[0:1, :])
        normed, inverse = norm_forward(total)
        g.out[rows, :] = (normed * g.gain[2:3, :] + g.bias[2:3, :]).astype(BF)
        grad = g.cot[rows, :].astype(F32)
        back = norm_backward(grad, normed, inverse, g.gain[2:3, :], 2)
        g.sm[8:9, :] += jnp.sum(back * hidden2, 0, keepdims=True)
        g.dx[rows, :] = back
        low = back.astype(BF)
        g.dtb[rows, :] = low
        g.sm[9:10, :] += jnp.sum(low.astype(F32), 0, keepdims=True)

    over_rows(2 * t, 64, third_norm)

    for c in range(chunks):
        cols = slice(c * d, (c + 1) * d)
        put_rows("fo", nn(g.act[:, cols].T, g.dtb[...]), 0, c * d // z.sums["fo"][0])
    advance("fo")
    for c in range(chunks):
        cols = slice(c * d, (c + 1) * d)
        back = (nt(g.dtb[...], g.w_fo[cols, :]) * g.dg[:, cols]).astype(BF)
        g.act[:, cols] = back
        g.sm[10 + c:11 + c, :] = jnp.sum(back.astype(F32), 0, keepdims=True)
    advance("fo")
    h2t = g.h2b[...].T
    for c in range(chunks):
        cols = slice(c * d, (c + 1) * d)
        put_rows("fi", nn(h2t, g.act[:, cols]), c * d)
    advance("fi")
    g.tmp[...] = nt(g.act[...], g.w_fi[...])

    def second_back(rows):
        grad = g.dx[rows, :] * g.scale[2:3, :] + g.tmp[rows, :]
        back = norm_backward(grad, g.n2[rows, :], g.i2[rows, :], g.gain[1:2, :], 1)
        hidden1 = g.n1[rows, :] * g.gain[0:1, :] + g.bias[0:1, :]
        g.sm[7:8, :] += jnp.sum(back * hidden1, 0, keepdims=True)
        g.dx[rows, :] = back
        g.dtb[rows, :] = back.astype(BF)

    over_rows(2 * t, 64, second_back)
    advance("fi")
    g.dc[...] = nt(g.dtb[...], g.w_co[...]).astype(BF)
    put_rows("co", nn(g.catt[...].T, g.dtb[...]))
    advance("co")

    for p in range(pairs):
        q, go, o = g.cqv[0:t, pair_cols(p)], g.dc[0:t, pair_cols(p)], g.co32[0:t, pair_cols(p)]
        qt, gt = q.T, go.T
        k = g.mkv[:, :, pair_cols(p)].reshape(n * mt, half)
        v = g.mkv[:, :, pair_cols(p, d)].reshape(n * mt, half)
        dqs, dks, dvs = [], [], []
        for w in range(2):
            qm, gm = only(q, w), only(go, w)
            weights = jnp.exp(nt(qm, k) * softmax_scale - kept_lse(CROSS_DOC + 2 * p + w))
            delta = jnp.sum(gm.astype(F32) * o, -1, keepdims=True)
            ds = (weights * (nt(gm, v) - delta)).astype(BF)
            dqs.append(nn(ds, k))
            dks.append(nn(qt[w * hd:(w + 1) * hd], ds))
            dvs.append(nn(gt[w * hd:(w + 1) * hd], weights.astype(BF)))
        g.dcq[0:t, pair_cols(p)] = (both(*dqs) * softmax_scale).astype(BF)
        dk = (jnp.concatenate(dks, 0) * softmax_scale).astype(BF).T
        dv = jnp.concatenate(dvs, 0).astype(BF).T
        g.mkv[:, :, pair_cols(p)] = dk.reshape(n, mt, half)
        g.mkv[:, :, pair_cols(p, d)] = dv.reshape(n, mt, half)

    advance("co")
    for p in range(pairs):
        q, k, v = g.cqv[t:, pair_cols(p)], g.pm[:, pair_cols(p)], g.pm[:, pair_cols(p, d)]
        go, o = g.dc[t:, pair_cols(p)], g.co32[t:, pair_cols(p)]
        dqs, dk, dv = [], 0.0, 0.0
        for w in range(2):
            qm, gm = only(q, w), only(go, w)
            weights = jnp.where(
                seen, jnp.exp(nt(qm, k) * softmax_scale - kept_lse(CROSS_PACKED + 2 * p + w)), 0.0)
            delta = jnp.sum(gm.astype(F32) * o, -1, keepdims=True)
            ds = (weights * (nt(gm, v) - delta)).astype(BF)
            dqs.append(nn(ds, k))
            dk = dk + tn(ds, qm)
            dv = dv + tn(weights.astype(BF), gm)
        g.dcq[t:, pair_cols(p)] = (both(*dqs) * softmax_scale).astype(BF)
        g.pm[:, pair_cols(p)] = (dk * softmax_scale).astype(BF)
        g.pm[:, pair_cols(p, d)] = dv.astype(BF)

    g.tmp[...] = nt(g.dcq[...], g.w_cq[...])

    def first_back(rows):
        grad = g.dx[rows, :] * g.scale[1:2, :] + g.tmp[rows, :]
        back = norm_backward(grad, g.n1[rows, :], g.i1[rows, :], g.gain[0:1, :], 0)
        g.sm[6:7, :] += jnp.sum(back * g.x[rows, :].astype(F32), 0, keepdims=True)
        g.dx[rows, :] = back
        g.dtb[rows, :] = back.astype(BF)

    over_rows(2 * t, 64, first_back)
    d_self = nt(g.dtb[...], g.w_so[...]).astype(BF)
    g.dself[...] = d_self[t:]
    g.dos[...] = d_self[:t].T.reshape(HEADS, hd, t)
    do_copies = [
        Spread(g.dos.at[h], g.dor.at[own_turn], g.do_s.at[h], g.do_r, h * split + own_part)
        for h in range(HEADS)
    ]
    for copy in do_copies:
        copy.start()

    class Small:
        def __init__(self):
            self.at = -1

        def advance(self):
            steps = z.bits + z.row_bits
            if self.at == steps:
                return
            if self.at >= 0:
                self.copy.wait()
                g.sm[...] = g.sm[...] + g.smr[self.at]
            self.at += 1
            k = self.at
            if k < steps:
                dev = (seq_partner(k), r) if k < z.bits else (s, row_partner(k - z.bits))
                self.copy = remote(g.sm, g.smr.at[k], g.sms.at[k], g.smrs.at[k], dev)
                self.copy.start()

    sums["small"] = Small()
    advance("small")

    doc_kv = g.mkv[...].reshape(n * mt, 2 * d)
    mem_t = g.mg[...].reshape(n * mt, d).T
    win_t = g.mw[...].T
    for part in range(2):
        cols = slice(part * d, (part + 1) * d)
        put_rows("cm", nn(mem_t, doc_kv[:, cols]) + nn(win_t, g.pm[:, cols]), part * d)
    advance("cm")
    g.mg[...] = nt(doc_kv, g.w_cm[...]).astype(BF).reshape(n, mt, d)
    advance("mk")
    g.dmp[...] = nt(g.pm[...], g.w_cm[...])
    g.hms[0:z.mhalo, :] = g.dmp[0:z.mhalo, :].astype(BF)
    g.hms[z.mhalo:, :] = g.dmp[z.mhalo + mt:, :].astype(BF)
    mem_halo = [
        remote(g.hms.at[pl.ds(0, z.mhalo)], g.hmr.at[pl.ds(z.mhalo, z.mhalo)],
               g.hs.at[5], g.hr.at[5], (prv, r)),
        remote(g.hms.at[pl.ds(z.mhalo, z.mhalo)], g.hmr.at[pl.ds(0, z.mhalo)],
               g.hs.at[6], g.hr.at[6], (nxt, r)),
    ]
    for copy in mem_halo:
        copy.start()

    put_rows("cq", nn(g.h1b[...].T, g.dcq[...]))
    advance("cq")
    put_rows("so", nn(g.att[...].T, g.dtb[...]))
    advance("so", "small")

    wait_whole(g.dor, g.do_r)
    g.dg[...] = jnp.zeros_like(g.dg)
    g.dwt[...] = jnp.zeros_like(g.dwt)
    dq_copies, kf_copies = [], []
    chunk = min(512, n * t)

    def kept(which, first, last):
        row, column = first // ff * 2 * hd + which * hd, first % ff
        return slice(row, row + hd), slice(column, column + last - first)

    def sibling(i, f):
        return remote(
            g.kvst.at[i, f], g.kvsib.at[i, my_part], g.sib_s.at[i, f], g.sib_r.at[i, my_part],
            (my_head * split + f, r))

    def share_kv(i):
        for f in range(split):
            @pl.when(my_part != f)
            def _():
                sibling(i, f).start()

    def close_kv(i):
        g.kvfin[i] = g.kvst[i, my_part]
        for f in range(split):
            @pl.when(my_part != f)
            def _():
                wait_whole(g.kvsib.at[i, f], g.sib_r.at[i, f])
                g.kvfin[i] = g.kvfin[i] + g.kvsib[i, f]
        copy = Spread(g.kvfin.at[i], g.dkvr.at[my_head], g.kf_s.at[i], g.kf_r, i * split + my_part)
        copy.start()
        kf_copies.append(copy)

    for i in reversed(range(HEADS)):
        b = i * split + turn_rest(i)
        qt, gt = g.qta[b], g.dor[i]
        q, go = qt.T, gt.T
        delta = jnp.sum(go.astype(F32) * g.of[i], -1, keepdims=True)
        lse = kept_lse(SELF_DOC + i)
        low = i * wide
        spans = [(a, min(a + chunk, low), False) for a in range(0, low, chunk)]
        spans.append((low, low + wide, True))
        dq = 0.0
        for first, last, masked in spans:
            k, v = g.kts[:, first:last], g.vts[:, first:last]
            weights = jnp.exp(nn(q, k) * softmax_scale - lse)
            if masked:
                weights = jnp.where(diag_mask(i), weights, 0.0)
            ds = (weights * (nn(go, v) - delta)).astype(BF)
            dq = dq + nt(ds, k)
            g.dg[kept(0, first, last)] += nn(qt, ds)
            g.dg[kept(1, first, last)] += nn(gt, weights.astype(BF))
        dqt = (dq * softmax_scale).T.astype(BF)
        g.ots[i] = dqt
        copy = Spread(g.ots.at[i], g.dqr.at[my_head], g.dq_s.at[i], g.dq_r, b)
        copy.start()
        dq_copies.append(copy)
        for f in range(split):
            first = (i * split + f) * t
            g.kvst[i, f, 0:hd] = (g.dg[kept(0, first, first + t)] * softmax_scale).astype(BF)
            g.kvst[i, f, hd:] = g.dg[kept(1, first, first + t)].astype(BF)
        share_kv(i)
        g.dwt[0:hd, :] += nn(dqt, g.xg[place_of(b)])
        for f in range(split):
            g.dwt[hd:, :] += nn(g.kvst[i, f], g.xg[reverse_static(i * split + f, z.bits)])
        if i < HEADS - 1:
            close_kv(i + 1)
        if i == 6:
            advance("mk", "cm", "small")
        if i == 4:
            advance("fo", "cq", "so", "small")
        if i == 2:
            advance("fi", "mk", "small")
    close_kv(0)

    whole = jnp.concatenate([g.dwt[...], jnp.zeros((hd, d), F32)], 0)
    g.dws[...] = whole.T.astype(BF).reshape(n, d // n, 4 * hd)
    dw_copies = [
        Spread(g.dws.at[o], g.dwr.at[s], g.dw_s.at[o], g.dw_r, o) for o in range(n)
    ]
    for copy in dw_copies:
        copy.start()

    for p in range(pairs):
        q, k, v = g.qp[:, pair_cols(p)], g.ps[:, pair_cols(p)], g.ps[:, pair_cols(p, d)]
        go, o = g.dself[:, pair_cols(p)], g.op[:, pair_cols(p)]
        dqs, dk, dv = [], 0.0, 0.0
        for w in range(2):
            qm, gm = only(q, w), only(go, w)
            sc = nt(qm, k) * softmax_scale - kept_lse(SELF_PACKED + 2 * p + w)
            weights = jnp.concatenate(
                [jnp.where(own_mask, jnp.exp(sc[:, :t]), 0.0),
                 jnp.where(prev_mask, jnp.exp(sc[:, t:]), 0.0)], 1)
            delta = jnp.sum(gm.astype(F32) * o, -1, keepdims=True)
            ds = (weights * (nt(gm, v) - delta)).astype(BF)
            dqs.append(nn(ds, k))
            dk = dk + tn(ds, qm)
            dv = dv + tn(weights.astype(BF), gm)
        g.qp[:, pair_cols(p)] = (both(*dqs) * softmax_scale).astype(BF)
        g.ps[:, pair_cols(p)] = (dk * softmax_scale).astype(BF)
        g.ps[:, pair_cols(p, d)] = dv.astype(BF)
    window_t = g.xw[...].T
    put_rows("sp", nn(window_t[:, :t], g.qp[...]), 0)
    put_rows("sp", nn(window_t, g.ps[:, :d]), d)
    put_rows("sp", nn(window_t, g.ps[:, d:]), 2 * d)
    advance("sp", "small")
    g.dxp[...] = nt(g.ps[...], g.w_sp[:, d:])
    g.hss[...] = g.dxp[t:, :].astype(BF)
    self_halo = remote(g.hss, g.hsr, g.hs.at[7], g.hr.at[7], (prv, r))
    self_halo.start()
    g.tmp[t:, :] = nt(g.qp[...], g.w_sp[:, :d]) + g.dxp[0:t, :]

    advance("sp", "fo", "fi", "co", "cq", "so", "cm", "mk", "small")
    wait_whole(g.dqr, g.dq_r)
    g.dproj[:, 0:d] = g.dqr[...].reshape(d, t).T
    wait_whole(g.dkvr, g.kf_r)
    for part in range(2):
        g.dproj[:, (part + 1) * d:(part + 2) * d] = (
            g.dkvr[:, part * hd:(part + 1) * hd, :].reshape(d, t).T)
    g.tmp[0:t, :] = nt(g.dproj[...], g.w_sp[...])
    self_halo.wait()
    g.tmp[2 * t - z.halo:, :] += g.hsr[...].astype(F32)

    def last(rows):
        g.dx[rows, :] = g.dx[rows, :] * g.scale[0:1, :] + g.tmp[rows, :]

    over_rows(2 * t, 64, last)

    wait_whole(g.dwr, g.dw_r)
    def parts_of(h):
        total = g.dwr[h * split].astype(F32)
        for f in range(1, split):
            total = total + g.dwr[h * split + f].astype(F32)
        return total
    for p in range(pairs):
        left, right = parts_of(2 * p), parts_of(2 * p + 1)
        for part in range(3):
            cols = slice(part * hd, (part + 1) * hd)
            g.dsh[:, pair_cols(p, part * d)] = jnp.concatenate([left[:, cols], right[:, cols]], 1).astype(BF)

    def shares(k):
        return remote(g.dsh, g.dshr.at[k], g.dy_s.at[k], g.dy_r.at[k], (s, row_partner(k)))

    shares(0).start()

    order = ("fo", "fi", "co", "cq", "so", "cm", "mk", "sp", "small")
    for k in range(z.row_bits - 1):
        shares(k).wait()
        g.dsh[...] = g.dsh[...] + g.dshr[k]
        shares(k + 1).start()
    while any(sums[name].at < (
            len(z.steps(name)) if name != "small" else z.bits + z.row_bits) for name in order):
        advance(*order)
    shares(z.row_bits - 1).wait()
    g.g_sp[...] = g.g_sp[...] + (g.dsh[...].astype(F32) + g.dshr[z.row_bits - 1].astype(F32))
    for copy in mem_halo:
        copy.wait()
    g.dm[0:mt, :] = sums["mk"].result().astype(F32)
    g.dm[mt:, :] = g.dmp[z.mhalo:z.mhalo + mt, :] + g.hmr[...].astype(F32)
    g.g_small[...] = g.sm[...]
    for copy in do_copies + dq_copies + kf_copies + dw_copies:
        copy.wait_send()
    for i in range(HEADS):
        for f in range(split):
            @pl.when(my_part != f)
            def _():
                sibling(i, f).wait_send()


def on_device(
    mesh_shape,
    tokens, memory, segments, padding, cotangent,
    self_project, self_output, cross_query, cross_memory, cross_output,
    feed_in, feed_in_bias, feed_out, feed_out_bias, norm_gain, norm_bias, residual_scale,
):
    t, _, d = tokens.shape
    mt = memory.shape[0]
    ff = feed_in.shape[1]
    n, rows = mesh_shape
    z = Sizes(n, rows, t, mt, d, ff)

    swap = segments[1, 0] == segments[1, t - 1]

    def ordered(array):
        first, second = array[:, 0], array[:, 1]
        return jnp.concatenate(
            [jnp.where(swap, second, first), jnp.where(swap, first, second)], 0)

    def restored(array):
        first, second = array[:array.shape[0] // 2], array[array.shape[0] // 2:]
        return jnp.stack([jnp.where(swap, second, first), jnp.where(swap, first, second)], 1)

    seg = jnp.where(swap, segments[0], segments[1])
    pad = jnp.where(swap, padding[0], padding[1])
    mem_seg = seg[::2]
    gap = jnp.full((t,), -1, I32)
    tail = jnp.full((t - z.halo,), -1, I32)
    codes = jnp.stack([
        seg, pad,
        jnp.concatenate([seg[t - z.halo:], tail]),
        jnp.concatenate([pad[t - z.halo:], tail]),
        jnp.concatenate([gap[:z.mhalo], mem_seg, gap[:t - z.mhalo - mt]]),
        jnp.concatenate([mem_seg[mt - z.mhalo:], gap[:t - z.mhalo]]),
        jnp.concatenate([gap[:t - z.mhalo], mem_seg[:z.mhalo]]),
        gap,
    ])

    scratch = z.scratch()
    names = INPUTS + OUTPUTS + tuple(scratch)
    vmem, anywhere = pl.BlockSpec(memory_space=pltpu.VMEM), pl.BlockSpec(memory_space=pl.ANY)
    outcome = pl.pallas_call(
        functools.partial(layer_kernel, z, names),
        out_shape=[
            jax.ShapeDtypeStruct((2 * t, d), BF),
            jax.ShapeDtypeStruct((2 * t, d), F32),
            jax.ShapeDtypeStruct((2 * mt, d), F32),
        ] + [
            jax.ShapeDtypeStruct(z.sums[name][:2], F32)
            for name in ("sp", "so", "cq", "cm", "co", "fi", "fo")
        ] + [jax.ShapeDtypeStruct((16, d), F32)],
        in_specs=[vmem] * 5 + [anywhere] * 7 + [vmem] * 5,
        out_specs=[vmem] * len(OUTPUTS),
        scratch_shapes=list(scratch.values()),
        compiler_params=pltpu.CompilerParams(
            collective_id=0, has_side_effects=True, vmem_limit_bytes=62 * 2 ** 20),
        name="layer",
    )(
        ordered(tokens), ordered(memory), ordered(cotangent), codes, seg.reshape(t, 1),
        self_project, self_output, cross_query, cross_memory, cross_output, feed_in, feed_out,
        feed_in_bias.reshape(1, ff), feed_out_bias.reshape(1, d), norm_gain, norm_bias, residual_scale,
    )
    out, dx, dm, g_sp, g_so, g_cq, g_cm, g_co, g_fi, g_fo, small = outcome
    at = lax.axis_index("seq")
    in_bias = lax.dynamic_slice(small[10:10 + ff // d].reshape(ff), (at * (ff // n),), (ff // n,))
    share = lax.dynamic_slice(small, (0, at * (d // n)), (16, d // n))
    return (
        restored(out), restored(dx), restored(dm),
        g_sp, g_so, g_cq, g_cm, g_co, g_fi, in_bias, g_fo, share[9],
        share[0:3], share[3:6], share[6:9],
    )


def solution(mesh):
    in_specs = (
        P("seq", "rows", None), P("seq", "rows", None), P("rows", "seq"), P("rows", "seq"),
        P("seq", "rows", None),
    ) + (P(),) * 12
    out_specs = (P("seq", "rows", None),) * 3 + (
        P("seq", None), P("seq", None), P("seq", None), P("seq", None), P("seq", None),
        P("seq", None), P("seq"), P("seq", None), P("seq"),
        P(None, "seq"), P(None, "seq"), P(None, "seq"),
    )
    shape = (mesh.shape["seq"], mesh.shape["rows"])
    return jax.shard_map(
        functools.partial(on_device, shape),
        mesh=mesh, in_specs=in_specs, out_specs=out_specs, check_vma=False,
    )
```

```python
import functools
import math

import jax
import jax.numpy as jnp
from jax import lax
from jax.experimental import pallas as pl
from jax.experimental.pallas import tpu as pltpu
from jax.sharding import PartitionSpec as P

HEADS = 8
EPSILON = 1e-05
NEGATIVE = -1e30
BF = jnp.bfloat16
F32 = jnp.float32
I32 = jnp.int32
MESH = pl.DeviceIdType.MESH
GELU_A = math.sqrt(2.0 / math.pi)
GELU_B = 0.044715


def nn(a, b):
    return jnp.dot(a, b, preferred_element_type=F32)


def nt(a, b):
    return lax.dot_general(a, b, (((1,), (1,)), ((), ())), preferred_element_type=F32)


def tn(a, b):
    return lax.dot_general(a, b, (((0,), (0,)), ((), ())), preferred_element_type=F32)


def log2(value):
    return int(value).bit_length() - 1


def reverse_static(index, bits):
    return sum(((index >> k) & 1) << (bits - 1 - k) for k in range(bits))


class Sizes:
    def __init__(self, n, rows, t, mt, d, ff):
        self.n, self.rows, self.t, self.mt, self.d, self.ff = n, rows, t, mt, d, ff
        self.bits, self.row_bits = log2(n), log2(rows)
        self.split = n // HEADS
        self.hd = d // HEADS
        self.halo = t // 2
        self.mhalo = mt // 2
        self.sums = {
            "fo": (ff // n, d, "rows first"),
            "fi": (d // n, ff, "rows last"),
            "co": (d // n, d, "rows first"),
            "cq": (d // n, d, "rows first"),
            "mk": (mt, d, "seq alone"),
            "cm": (d // n, 2 * d, "rows first"),
            "so": (d // n, d, "rows first"),
            "sp": (d // n, 3 * d, "rows first"),
        }

    def steps(self, name):
        order = self.sums[name][2]
        seq = [("seq", k) for k in range(self.bits)]
        rows = [("exchange", k) for k in range(self.row_bits)]
        if order == "seq alone":
            return seq
        if order == "rows last":
            return seq + rows
        return seq[:1] + [("halve", 0)] + seq[1:] + rows[1:] + [("gather", 0)]

    def parts(self, name):
        return 2 if self.sums[name][2] == "rows first" else 1

    def received(self, name):
        held, first, spans = self.n * self.parts(name), 0, []
        for kind, _ in self.steps(name):
            held = held // 2 if kind in ("seq", "halve") else held
            spans.append((first, held))
            first += held
        return spans, first

    def scratch(self):
        n, t, mt, d, ff, hd, split = self.n, self.t, self.mt, self.d, self.ff, self.hd, self.split
        v, dma = pltpu.VMEM, pltpu.SemaphoreType.DMA
        small_steps = self.bits + self.row_bits
        spec = dict(
            w_sp=v((d, 3 * d), BF), w_so=v((d, d), BF), w_cq=v((d, d), BF), w_cm=v((d, 2 * d), BF),
            w_co=v((d, d), BF), w_fi=v((d, ff), BF), w_fo=v((ff, d), BF),
            x=v((2 * t, d), BF), mem=v((2 * mt, d), BF), cot=v((2 * t, d), BF),
            dx=v((2 * t, d), F32), codes=v((8, t), I32),
            xg=v((n, t, d), BF), mg=v((n, mt, d), BF), mkv=v((n, mt, 2 * d), BF),
            qkvt=v((HEADS, 3 * hd, t), BF), kv=v((split, HEADS, 2 * hd, t), BF),
            qt=v((HEADS, hd, t), BF), kts=v((hd, n * t), BF), vts=v((hd, n * t), BF),
            ots=v((HEADS, hd, t), BF), otr=v((HEADS, hd, t), BF), of=v((HEADS, t, hd), F32),
            dos=v((HEADS, hd, t), BF), dor=v((HEADS, hd, t), BF), dqr=v((HEADS, hd, t), BF),
            dwt=v((3 * hd, d), F32),
            kvst=v((HEADS, split, 2 * hd, t), BF), kvsib=v((HEADS, split, 2 * hd, t), BF),
            kvfin=v((HEADS, 2 * hd, t), BF), dkvr=v((HEADS, 2 * hd, t), BF),
            dws=v((n, d // n, 4 * hd), BF), dwr=v((n, d // n, 4 * hd), BF),
            dsh=v((d // n, 3 * d), BF), dshr=v((self.row_bits, d // n, 3 * d), BF),
            xw=v((t + self.halo, d), BF), mw=v((2 * mt, d), BF),
            qp=v((t, d), BF), ps=v((t + self.halo, 2 * d), BF), pm=v((2 * mt, 2 * d), BF),
            cp=v((8, t), I32), cn=v((8, t), I32),
            lse=v((t, 4 * HEADS), F32),
            op=v((t, d), F32), co32=v((2 * t, d), F32),
            hss=v((self.halo, d), BF), hsr=v((self.halo, d), BF),
            hms=v((mt, d), BF), hmr=v((mt, d), BF),
            att=v((2 * t, d), BF), catt=v((2 * t, d), BF), cqv=v((2 * t, d), BF),
            tmp=v((2 * t, d), F32), n1=v((2 * t, d), F32), n2=v((2 * t, d), F32),
            i1=v((2 * t, 1), F32), i2=v((2 * t, 1), F32),
            h1b=v((2 * t, d), BF), h2b=v((2 * t, d), BF),
            act=v((2 * t, ff), BF), dg=v((2 * t, ff), F32),
            dtb=v((2 * t, d), BF), dc=v((2 * t, d), BF), dcq=v((2 * t, d), BF),
            dself=v((t, d), BF), dproj=v((t, 3 * d), BF),
            sm=v((16, d), F32), smr=v((small_steps, 16, d), F32),
        )
        for name, (r, c, order) in self.sums.items():
            parts = self.parts(name)
            if name != "mk":
                spec["a_" + name] = v((n * parts, r, c // parts), BF)
            spec["r_" + name] = v((self.received(name)[1], r, c // parts), BF)
            spec["ss_" + name] = dma((len(self.steps(name)),))
            spec["rs_" + name] = dma((len(self.steps(name)),))
        spec.update(
            sms=dma((small_steps,)), smrs=dma((small_steps,)),
            wsem=dma((7,)), xgs=dma((4, n)), xgr=dma((n,)), mgs=dma((4, n)), mgr=dma((n,)),
            hs=dma((8,)), hr=dma((8,)),
            kv_s=dma((HEADS,)), kv_r=dma, kw_s=dma((split,)), kw_r=dma((split,)),
            q_s=dma((HEADS,)), q_r=dma, o_s=dma((HEADS,)), o_r=dma, do_s=dma((HEADS,)), do_r=dma,
            dq_s=dma((HEADS,)), dq_r=dma, kf_s=dma((HEADS,)), kf_r=dma,
            sib_s=dma((HEADS, split)), sib_r=dma((HEADS, split)),
            dw_s=dma((n,)), dw_r=dma, dy_s=dma((self.row_bits,)), dy_r=dma((self.row_bits,)),
        )
        return spec


class Refs:
    def __init__(self, names, refs):
        for name, ref in zip(names, refs):
            setattr(self, name, ref)


INPUTS = (
    "x_in", "mem_in", "cot_in", "seg_in", "pad_in",
    "h_sp", "h_so", "h_cq", "h_cm", "h_co", "h_fi", "h_fo",
    "fi_b", "fo_b", "gain", "bias", "scale",
)
OUTPUTS = (
    "out", "dx_out", "dm_out", "g_sp", "g_so", "g_cq", "g_cm", "g_co", "g_fi", "g_fo",
    "b_fi", "b_fo", "b_gain", "b_bias", "b_scale",
)


def layer_kernel(z, names, *refs):
    g = Refs(names, refs)
    g.dxp, g.dmp = g.co32.at[pl.ds(0, z.t + z.halo)], g.n2.at[pl.ds(0, 2 * z.mt)]
    n, t, mt, d, ff, hd, split = z.n, z.t, z.mt, z.d, z.ff, z.hd, z.split
    half = 2 * hd
    pairs = d // half
    softmax_scale = 1.0 / math.sqrt(hd)
    s = lax.axis_index("seq")
    r = lax.axis_index("rows")

    def bit_of(index, k):
        return lax.rem(lax.div(index, 2 ** k), 2)

    def seq_partner(k):
        return s + (1 - 2 * bit_of(s, k)) * 2 ** k

    def row_partner(k):
        return r + (1 - 2 * bit_of(r, k)) * 2 ** k

    def place_of(index):
        return sum(bit_of(index, k) * 2 ** (z.bits - 1 - k) for k in range(z.bits))

    nxt = lax.rem(s + 1, n)
    prv = lax.rem(s + n - 1, n)
    my_head = lax.div(s, split)
    my_part = lax.rem(s, split)
    own_turn = lax.div(s, split)
    own_rest = lax.rem(s, split)
    own_part = own_rest + lax.rem(own_turn, 2) * (split - 1 - 2 * own_rest)

    barrier = pltpu.get_barrier_semaphore()
    for step in range(1, n):
        pl.semaphore_signal(barrier, inc=1, device_id=(lax.rem(s + step, n), r), device_id_type=MESH)
    for k in range(z.row_bits):
        pl.semaphore_signal(barrier, inc=1, device_id=(s, row_partner(k)), device_id_type=MESH)

    loads = {
        name: pltpu.make_async_copy(getattr(g, "h_" + name), getattr(g, "w_" + name), g.wsem.at[j])
        for j, name in enumerate(("sp", "cm", "so", "cq", "co", "fi", "fo"))
    }
    loads["sp"].start()

    def remote(src, dst, ssem, rsem, dev):
        return pltpu.make_async_remote_copy(
            src_ref=src, dst_ref=dst, send_sem=ssem, recv_sem=rsem,
            device_id=dev, device_id_type=MESH,
        )

    class Spread:
        def __init__(self, src, dst, ssem, rsem, dest):
            self.dest = dest
            self.far = remote(src, dst, ssem, rsem, (dest, r))
            self.near = pltpu.make_async_copy(src, dst, rsem)

        def start(self):
            @pl.when(self.dest != s)
            def _():
                self.far.start()

            @pl.when(self.dest == s)
            def _():
                self.near.start()

        def wait_send(self):
            @pl.when(self.dest != s)
            def _():
                self.far.wait_send()

    def wait_whole(ref, sem):
        pltpu.make_async_copy(ref, ref, sem).wait()

    class Chain:
        def __init__(self, buf, send, recv):
            self.buf, self.send, self.recv = buf, send, recv
            self.line = n // 4
            self.zz, self.xx, self.core = lax.div(s, 4), bit_of(s, 1), bit_of(s, 0)

        def copy(self, way, origin):
            dev = (s + 4, s - 4, s + 2 - 4 * self.xx, s + 1 - 2 * self.core)[way]
            at = place_of(origin)
            block = self.buf.at[at]
            return remote(block, block, self.send.at[way, at], self.recv.at[at], (dev, r))

        def arrive(self, origin):
            at = place_of(origin)
            wait_whole(self.buf.at[at], self.recv.at[at])

        def pass_on(self, action, zz, ahead, back):
            origin = s + 4 * (zz - self.zz)
            if ahead:
                @pl.when(self.zz < self.line - 1)
                def _():
                    action(self.copy(0, origin))
            if back:
                @pl.when(self.zz > 0)
                def _():
                    action(self.copy(1, origin))
            action(self.copy(2, origin))
            action(self.copy(3, origin))

        def start(self):
            self.pass_on(lambda c: c.start(), self.zz, True, True)

        def line_step(self, j, action, wait):
            low, high = self.zz - 1 - j, self.zz + 1 + j

            @pl.when(low >= 0)
            def _():
                if wait:
                    self.arrive(s + 4 * (low - self.zz))
                self.pass_on(action, low, True, False)

            @pl.when(high < self.line)
            def _():
                if wait:
                    self.arrive(s + 4 * (high - self.zz))
                self.pass_on(action, high, False, True)

        def step(self, j):
            self.line_step(j, lambda c: c.start(), True)

        def across(self, j, action, wait):
            other = s + 2 - 4 * self.xx
            for sign in ((1,) if j == 0 else (-1, 1)):
                zz = self.zz + sign * j

                @pl.when((zz >= 0) & (zz < self.line))
                def _():
                    origin = other + 4 * (zz - self.zz)
                    if wait:
                        self.arrive(origin)
                    action(self.copy(3, origin))

        def cross_step(self, j):
            self.across(j, lambda c: c.start(), True)

        def finish(self):
            other = s + 1 - 2 * self.core
            for k in range(2 * self.line):
                self.arrive(lax.rem(other, 2) + 2 * k)

        def drain(self):
            done = lambda c: c.wait_send()
            self.pass_on(done, self.zz, True, True)
            for j in range(self.line - 1):
                self.line_step(j, done, False)
            for j in range(self.line):
                self.across(j, done, False)

    class Sum:
        def __init__(self, name):
            self.name, self.out = name, getattr(g, "g_" + name, None)
            self.a = g.mg if name == "mk" else getattr(g, "a_" + name)
            self.r = getattr(g, "r_" + name)
            self.ss, self.rs = getattr(g, "ss_" + name), getattr(g, "rs_" + name)
            self.steps, self.parts = z.steps(name), z.parts(name)
            self.spans = z.received(name)[0]
            self.share, self.columns = z.sums[name][:2]
            self.copies = {}
            self.at = -1

        def held(self, i):
            if i == 0:
                return self.a, 0, n * self.parts
            return (self.r,) + self.spans[i - 1]

        def bit(self, i):
            kind, k = self.steps[i]
            return bit_of(s, k) if kind == "seq" else bit_of(r, k)

        def start(self, i):
            ref, first, blocks = self.held(i)
            into, into_first, count = self.held(i + 1)
            kind, k = self.steps[i]
            src = ref.at[pl.ds(first + (1 - self.bit(i)) * count, count)] if blocks > count else (
                ref.at[pl.ds(first, count)])
            dev = (seq_partner(k), r) if kind == "seq" else (s, row_partner(k))
            self.copies[i] = remote(src, into.at[pl.ds(into_first, count)], self.ss.at[i], self.rs.at[i], dev)
            self.copies[i].start()

        def finish(self, i):
            self.copies[i].wait()
            ref, first, blocks = self.held(i)
            into, into_first, count = self.held(i + 1)
            kind, k = self.steps[i]
            last = i + 1 == len(self.steps)
            if kind == "gather":
                width = self.columns // 2
                mine, theirs = bit_of(r, 0) * width, (1 - bit_of(r, 0)) * width
                self.out[:, pl.ds(pl.multiple_of(mine, width), width)] = ref[first].astype(F32)
                self.out[:, pl.ds(pl.multiple_of(theirs, width), width)] = into[into_first].astype(F32)
                return
            if last and self.out is not None:
                self.out[...] = into[into_first].astype(F32) + ref[first].astype(F32)
                return
            base = first + self.bit(i) * count if blocks > count else first
            if count <= 2:
                for j in range(count):
                    into[into_first + j] = into[into_first + j] + ref[base + j]
            else:
                def add(j, carry):
                    into[into_first + j] = into[into_first + j] + ref[base + j]
                    return carry
                lax.fori_loop(0, count, add, 0)

        def advance(self):
            if self.at == len(self.steps):
                return
            if self.at >= 0:
                self.finish(self.at)
            self.at += 1
            if self.at < len(self.steps):
                self.start(self.at)

        def result(self):
            ref, first, _ = self.held(len(self.steps))
            return ref[first]

        def put(self, owner, value, first_column):
            width = self.columns // self.parts
            core, rest = owner % 2, reverse_static(owner // 2, z.bits - 1)
            for part in range(self.parts):
                low = max(first_column, part * width)
                high = min(first_column + value.shape[1], (part + 1) * width)
                if low < high:
                    where = (core * self.parts + part) * (n // 2) + rest
                    self.a[where, :, low - part * width:high - part * width] = (
                        value[:, low - first_column:high - first_column])

    sums = {name: Sum(name) for name in z.sums}

    def advance(*which):
        for name in which:
            sums[name].advance()

    def put_rows(name, value, first_column=0, first_owner=0):
        share = z.sums[name][0]
        value = value.astype(BF)
        for j in range(value.shape[0] // share):
            sums[name].put(first_owner + j, value[j * share:(j + 1) * share], first_column)

    def over_rows(count, size, step):
        def one(j, carry):
            step(pl.ds(pl.multiple_of(j * size, size), size))
            return carry
        lax.fori_loop(0, count // size, one, 0)

    def mean(value):
        return jnp.sum(value, -1, keepdims=True) * (1.0 / d)

    def norm_forward(total):
        centred = total - mean(total)
        inverse = lax.rsqrt(mean(centred * centred) + EPSILON)
        return centred * inverse, inverse

    def norm_backward(grad, normed, inverse, gain_row, which):
        scaled = grad * gain_row
        result = inverse * (scaled - mean(scaled) - normed * mean(scaled * normed))
        g.sm[which:which + 1, :] += jnp.sum(grad * normed, 0, keepdims=True)
        g.sm[3 + which:4 + which, :] += jnp.sum(grad, 0, keepdims=True)
        return result

    lane = lax.broadcasted_iota(I32, (t, half), 1)

    def only(value, which):
        keep = (lane < hd) if which == 0 else (lane >= hd)
        return jnp.where(keep, value, jnp.zeros_like(value))

    def both(first, second):
        return jnp.where(lane < hd, first, second)

    def pair_cols(p, offset=0):
        return slice(offset + p * half, offset + (p + 1) * half)

    def keep_lse(index, value):
        g.lse[:, index:index + 1] = value

    def kept_lse(index):
        return g.lse[:, index:index + 1]

    SELF_PACKED, CROSS_PACKED, CROSS_DOC, SELF_DOC = (k * HEADS for k in range(4))

    tokens_all = Chain(g.xg, g.xgs, g.xgr)
    memory_all = Chain(g.mg, g.mgs, g.mgr)
    place = place_of(s)
    other_seg = g.seg_in[1:2, :]
    swap = jnp.min(other_seg, -1, keepdims=True) == jnp.max(other_seg, -1, keepdims=True)

    def ordered(ref, into):
        first, second, count = ref[:, 0, :], ref[:, 1, :], ref.shape[0]
        into[0:count, :] = jnp.where(swap, second, first)
        into[count:, :] = jnp.where(swap, first, second)

    def restored(first, second, ref):
        ref[:, 0, :] = jnp.where(swap, second, first)
        ref[:, 1, :] = jnp.where(swap, first, second)

    ordered(g.x_in, g.x)
    ordered(g.mem_in, g.mem)
    seg = jnp.where(swap, g.seg_in[0:1, :], other_seg)
    pad = jnp.where(swap, g.pad_in[0:1, :], g.pad_in[1:2, :])
    q_at = lax.broadcasted_iota(I32, (t, t), 0)
    k_at = lax.broadcasted_iota(I32, (t, t), 1)
    seg_q = jnp.sum(jnp.where(q_at == k_at, seg.astype(F32), 0.0), -1, keepdims=True).astype(I32)
    pick = (q_at == 2 * lax.rem(k_at + z.mhalo, mt)).astype(F32)
    mem_seg = jnp.dot(
        jnp.broadcast_to(seg.astype(F32), (8, t)), pick,
        precision=lax.Precision.HIGHEST, preferred_element_type=F32).astype(I32)
    g.codes[0:1, :] = seg
    g.codes[1:2, :] = pad
    g.codes[2:3, :] = pltpu.roll(seg, z.halo, 1)
    g.codes[3:4, :] = pltpu.roll(pad, z.halo, 1)
    g.codes[4:8, :] = mem_seg[0:4]
    loads["sp"].wait()
    for name in ("cm", "so", "cq", "co", "fi", "fo"):
        loads[name].start()

    for part in range(3):
        made = nn(g.x[0:t, :], g.w_sp[:, part * d:(part + 1) * d]).astype(BF)
        g.qkvt[:, part * hd:(part + 1) * hd, :] = made.T.reshape(HEADS, hd, t)
    g.xg[place] = g.x[0:t, :]
    g.mg[place] = g.mem[0:mt, :]
    g.xw[0:t, :] = g.x[t:, :]
    g.mw[z.mhalo:z.mhalo + mt, :] = g.mem[mt:, :]
    g.sm[...] = jnp.zeros_like(g.sm)
    pl.semaphore_wait(barrier, n - 1 + z.row_bits)
    kv_copies = [
        Spread(g.qkvt.at[h, pl.ds(hd, 2 * hd)], g.kv.at[my_part, own_turn], g.kv_s.at[h], g.kv_r,
               h * split + my_part)
        for h in range(HEADS)
    ]
    q_copies = [
        Spread(g.qkvt.at[h, pl.ds(0, hd)], g.qt.at[own_turn], g.q_s.at[h], g.q_r, h * split + own_part)
        for h in range(HEADS)
    ]
    for copy in kv_copies + q_copies:
        copy.start()
    halo_copies = [
        remote(g.codes, g.cn, g.hs.at[0], g.hr.at[0], (prv, r)),
        remote(g.codes, g.cp, g.hs.at[1], g.hr.at[1], (nxt, r)),
        remote(g.x.at[pl.ds(2 * t - z.halo, z.halo)], g.xw.at[pl.ds(t, z.halo)],
               g.hs.at[2], g.hr.at[2], (nxt, r)),
        remote(g.mem.at[pl.ds(mt, z.mhalo)], g.mw.at[pl.ds(z.mhalo + mt, z.mhalo)],
               g.hs.at[3], g.hr.at[3], (prv, r)),
        remote(g.mem.at[pl.ds(2 * mt - z.mhalo, z.mhalo)], g.mw.at[pl.ds(0, z.mhalo)],
               g.hs.at[4], g.hr.at[4], (nxt, r)),
    ]
    for copy in halo_copies:
        copy.start()

    memory_all.start()

    g.qp[...] = nn(g.xw[0:t, :], g.w_sp[:, :d]).astype(BF)
    ordered(g.cot_in, g.cot)

    def self_mask():
        seg_k, pad_k = g.codes[0:1, :], g.codes[1:2, :]
        own = (seg_q == seg_k) & (k_at <= q_at) & ((pad_k == 1) | (k_at == q_at))
        prev = (seg_q == g.cp[2:3, :]) & (g.cp[3:4, :] == 1)
        return own, prev[:, :z.halo]

    def cross_mask():
        at = lax.broadcasted_iota(I32, (1, 2 * mt), 1)
        seg_k = jnp.where(
            at < z.mhalo, g.cp[4:5, :],
            jnp.where(at < z.mhalo + mt, g.codes[4:5, :], g.cn[4:5, :]))
        return seg_q == seg_k

    def softmax_parts(scores):
        top = functools.reduce(jnp.maximum, [jnp.max(b, -1, keepdims=True) for b in scores])
        weights = [jnp.exp(b - top) for b in scores]
        total = functools.reduce(jnp.add, [jnp.sum(w, -1, keepdims=True) for w in weights])
        return weights, total, top + jnp.log(total)

    def hand_over(f):
        return remote(g.kv.at[my_part], g.kv.at[my_part], g.kw_s.at[f], g.kw_r.at[my_part],
                      (my_head * split + f, r))

    wait_whole(g.kv.at[my_part], g.kv_r)
    for f in range(split):
        @pl.when(my_part != f)
        def _():
            hand_over(f).start()
    wait_whole(g.qt, g.q_r)
    for f in range(split):
        @pl.when(my_part != f)
        def _():
            wait_whole(g.kv.at[f], g.kw_r.at[f])
    for b in range(n):
        g.kts[:, b * t:(b + 1) * t] = g.kv[b % split, b // split, 0:hd]
        g.vts[:, b * t:(b + 1) * t] = g.kv[b % split, b // split, hd:]

    wide = split * t
    diag_q = lax.broadcasted_iota(I32, (t, wide), 0)
    diag_k = lax.broadcasted_iota(I32, (t, wide), 1)

    def turn_rest(i):
        return my_part if i % 2 == 0 else split - 1 - my_part

    def diag_mask(i):
        return diag_k <= diag_q + turn_rest(i) * t

    o_copies = []
    for i in range(HEADS):
        b = i * split + turn_rest(i)
        q = g.qt[i].T
        low = i * wide
        blocks = []
        if low:
            blocks.append(nn(q, g.kts[:, :low]) * softmax_scale)
        blocks.append(jnp.where(
            diag_mask(i), nn(q, g.kts[:, low:low + wide]) * softmax_scale, NEGATIVE))
        weights, total, lse = softmax_parts(blocks)
        keep_lse(SELF_DOC + i, lse)
        o = nt(weights[-1].astype(BF), g.vts[:, low:low + wide])
        if low:
            o = o + nt(weights[0].astype(BF), g.vts[:, :low])
        o = o / total
        g.of[i] = o
        g.ots[i] = o.T.astype(BF)
        copy = Spread(g.ots.at[i], g.otr.at[my_head], g.o_s.at[i], g.o_r, b)
        copy.start()
        o_copies.append(copy)
        if i == 3:
            memory_all.step(0)
            memory_all.cross_step(0)
    for j in range(1, n // 4 - 2):
        memory_all.step(j)
        memory_all.cross_step(j)

    tokens_all.start()

    for copy in halo_copies:
        copy.wait()
    g.ps[...] = nn(g.xw[...], g.w_sp[:, d:]).astype(BF)
    loads["cm"].wait()
    g.pm[...] = nn(g.mw[...], g.w_cm[...]).astype(BF)
    own_mask, prev_mask = self_mask()
    for p in range(pairs):
        q, k, v = g.qp[:, pair_cols(p)], g.ps[:, pair_cols(p)], g.ps[:, pair_cols(p, d)]
        outs = []
        for w in range(2):
            sc = nt(only(q, w), k) * softmax_scale
            blocks = [jnp.where(own_mask, sc[:, :t], NEGATIVE), jnp.where(prev_mask, sc[:, t:], NEGATIVE)]
            weights, total, lse = softmax_parts(blocks)
            keep_lse(SELF_PACKED + 2 * p + w, lse)
            o = nn(weights[0].astype(BF), v[:t]) + nn(weights[1].astype(BF), v[t:])
            outs.append(o / total)
        o = both(*outs)
        g.op[:, pair_cols(p)] = o
        g.att[t:, pair_cols(p)] = o.astype(BF)

    memory_all.step(n // 4 - 2)
    memory_all.cross_step(n // 4 - 2)

    loads["so"].wait()
    wait_whole(g.otr, g.o_r)
    g.att[0:t, :] = g.otr[...].reshape(d, t).T
    g.tmp[...] = nn(g.att[...], g.w_so[...])

    def first_norm(rows):
        total = g.x[rows, :].astype(F32) * g.scale[0:1, :] + g.tmp[rows, :]
        normed, inverse = norm_forward(total)
        g.n1[rows, :] = normed
        g.i1[rows, :] = inverse
        g.h1b[rows, :] = (normed * g.gain[0:1, :] + g.bias[0:1, :]).astype(BF)

    over_rows(2 * t, 64, first_norm)
    loads["cq"].wait()
    g.cqv[...] = nn(g.h1b[...], g.w_cq[...]).astype(BF)

    seen = cross_mask()
    for p in range(pairs):
        q, k, v = g.cqv[t:, pair_cols(p)], g.pm[:, pair_cols(p)], g.pm[:, pair_cols(p, d)]
        outs = []
        for w in range(2):
            sc = jnp.where(seen, nt(only(q, w), k) * softmax_scale, NEGATIVE)
            (weights,), total, lse = softmax_parts([sc])
            keep_lse(CROSS_PACKED + 2 * p + w, lse)
            outs.append(nn(weights.astype(BF), v) / total)
        o = both(*outs)
        g.co32[t:, pair_cols(p)] = o
        g.catt[t:, pair_cols(p)] = o.astype(BF)
    tokens_all.step(0)
    tokens_all.cross_step(0)
    memory_all.cross_step(n // 4 - 1)
    memory_all.finish()

    for part in range(2):
        cols = slice(part * d, (part + 1) * d)
        g.mkv[:, :, cols] = nn(g.mg[...].reshape(n * mt, d), g.w_cm[:, cols]).astype(BF).reshape(n, mt, d)

    for p in range(pairs):
        q = g.cqv[0:t, pair_cols(p)]
        k = g.mkv[:, :, pair_cols(p)].reshape(n * mt, half)
        v = g.mkv[:, :, pair_cols(p, d)].reshape(n * mt, half)
        outs = []
        for w in range(2):
            sc = nt(only(q, w), k) * softmax_scale
            (weights,), total, lse = softmax_parts([sc])
            keep_lse(CROSS_DOC + 2 * p + w, lse)
            outs.append(nn(weights.astype(BF), v) / total)
        o = both(*outs)
        g.co32[0:t, pair_cols(p)] = o
        g.catt[0:t, pair_cols(p)] = o.astype(BF)
        if p == 3:
            tokens_all.step(1)
            tokens_all.cross_step(1)
    for copy in o_copies + kv_copies + q_copies:
        copy.wait_send()
    for f in range(split):
        @pl.when(my_part != f)
        def _():
            hand_over(f).wait_send()
    memory_all.drain()

    loads["co"].wait()
    g.tmp[...] = nn(g.catt[...], g.w_co[...])

    def second_norm(rows):
        hidden1 = g.n1[rows, :] * g.gain[0:1, :] + g.bias[0:1, :]
        normed, inverse = norm_forward(hidden1 * g.scale[1:2, :] + g.tmp[rows, :])
        g.n2[rows, :] = normed
        g.i2[rows, :] = inverse
        g.h2b[rows, :] = (normed * g.gain[1:2, :] + g.bias[1:2, :]).astype(BF)

    over_rows(2 * t, 64, second_norm)

    loads["fi"].wait()
    chunks = ff // d
    for c in range(chunks):
        cols = slice(c * d, (c + 1) * d)
        pre = nn(g.h2b[...], g.w_fi[:, cols]) + g.fi_b[0:1, cols]
        square = pre * pre
        bent = jnp.tanh(GELU_A * pre * (1.0 + GELU_B * square))
        g.act[:, cols] = (0.5 * pre * (1.0 + bent)).astype(BF)
        g.dg[:, cols] = 0.5 * (1.0 + bent) + 0.5 * pre * (1.0 - bent * bent) * (
            GELU_A * (1.0 + 3.0 * GELU_B * square))
    tokens_all.step(2)
    tokens_all.cross_step(2)
    loads["fo"].wait()
    g.tmp[...] = nn(g.act[...], g.w_fo[...])

    def third_norm(rows):
        hidden2 = g.n2[rows, :] * g.gain[1:2, :] + g.bias[1:2, :]
        total = hidden2 * g.scale[2:3, :] + (g.tmp[rows, :] + g.fo_b[0:1, :])
        normed, inverse = norm_forward(total)
        grad = g.cot[rows, :].astype(F32)
        g.cot[rows, :] = (normed * g.gain[2:3, :] + g.bias[2:3, :]).astype(BF)
        back = norm_backward(grad, normed, inverse, g.gain[2:3, :], 2)
        g.sm[8:9, :] += jnp.sum(back * hidden2, 0, keepdims=True)
        g.dx[rows, :] = back
        low = back.astype(BF)
        g.dtb[rows, :] = low
        g.sm[9:10, :] += jnp.sum(low.astype(F32), 0, keepdims=True)

    over_rows(2 * t, 64, third_norm)

    for j in range(3, n // 4 - 1):
        tokens_all.step(j)
        tokens_all.cross_step(j)

    for c in range(chunks):
        cols = slice(c * d, (c + 1) * d)
        put_rows("fo", nn(g.act[:, cols].T, g.dtb[...]), 0, c * d // z.sums["fo"][0])
    advance("fo")
    for c in range(chunks):
        cols = slice(c * d, (c + 1) * d)
        back = (nt(g.dtb[...], g.w_fo[cols, :]) * g.dg[:, cols]).astype(BF)
        g.act[:, cols] = back
        g.sm[10 + c:11 + c, :] = jnp.sum(back.astype(F32), 0, keepdims=True)
    advance("fo")
    tokens_all.cross_step(n // 4 - 1)
    h2t = g.h2b[...].T
    for c in range(chunks):
        cols = slice(c * d, (c + 1) * d)
        put_rows("fi", nn(h2t, g.act[:, cols]), c * d)
    advance("fi")
    g.tmp[...] = nt(g.act[...], g.w_fi[...])

    def second_back(rows):
        grad = g.dx[rows, :] * g.scale[2:3, :] + g.tmp[rows, :]
        back = norm_backward(grad, g.n2[rows, :], g.i2[rows, :], g.gain[1:2, :], 1)
        hidden1 = g.n1[rows, :] * g.gain[0:1, :] + g.bias[0:1, :]
        g.sm[7:8, :] += jnp.sum(back * hidden1, 0, keepdims=True)
        g.dx[rows, :] = back
        g.dtb[rows, :] = back.astype(BF)

    over_rows(2 * t, 64, second_back)
    advance("fi")
    restored(g.cot[0:t, :], g.cot[t:, :], g.out)
    g.dc[...] = nt(g.dtb[...], g.w_co[...]).astype(BF)
    put_rows("co", nn(g.catt[...].T, g.dtb[...]))
    advance("co")

    for p in range(pairs):
        q, go, o = g.cqv[0:t, pair_cols(p)], g.dc[0:t, pair_cols(p)], g.co32[0:t, pair_cols(p)]
        qt, gt = q.T, go.T
        k = g.mkv[:, :, pair_cols(p)].reshape(n * mt, half)
        v = g.mkv[:, :, pair_cols(p, d)].reshape(n * mt, half)
        dqs, dks, dvs = [], [], []
        for w in range(2):
            qm, gm = only(q, w), only(go, w)
            weights = jnp.exp(nt(qm, k) * softmax_scale - kept_lse(CROSS_DOC + 2 * p + w))
            delta = jnp.sum(gm.astype(F32) * o, -1, keepdims=True)
            ds = (weights * (nt(gm, v) - delta)).astype(BF)
            dqs.append(nn(ds, k))
            dks.append(nn(qt[w * hd:(w + 1) * hd], ds))
            dvs.append(nn(gt[w * hd:(w + 1) * hd], weights.astype(BF)))
        g.dcq[0:t, pair_cols(p)] = (both(*dqs) * softmax_scale).astype(BF)
        dk = (jnp.concatenate(dks, 0) * softmax_scale).astype(BF).T
        dv = jnp.concatenate(dvs, 0).astype(BF).T
        g.mkv[:, :, pair_cols(p)] = dk.reshape(n, mt, half)
        g.mkv[:, :, pair_cols(p, d)] = dv.reshape(n, mt, half)
        if p == 0:
            advance("co")

    for p in range(pairs):
        q, k, v = g.cqv[t:, pair_cols(p)], g.pm[:, pair_cols(p)], g.pm[:, pair_cols(p, d)]
        go, o = g.dc[t:, pair_cols(p)], g.co32[t:, pair_cols(p)]
        dqs, dk, dv = [], 0.0, 0.0
        for w in range(2):
            qm, gm = only(q, w), only(go, w)
            weights = jnp.where(
                seen, jnp.exp(nt(qm, k) * softmax_scale - kept_lse(CROSS_PACKED + 2 * p + w)), 0.0)
            delta = jnp.sum(gm.astype(F32) * o, -1, keepdims=True)
            ds = (weights * (nt(gm, v) - delta)).astype(BF)
            dqs.append(nn(ds, k))
            dk = dk + tn(ds, qm)
            dv = dv + tn(weights.astype(BF), gm)
        g.dcq[t:, pair_cols(p)] = (both(*dqs) * softmax_scale).astype(BF)
        g.pm[:, pair_cols(p)] = (dk * softmax_scale).astype(BF)
        g.pm[:, pair_cols(p, d)] = dv.astype(BF)

    g.tmp[...] = nt(g.dcq[...], g.w_cq[...])

    def first_back(rows):
        grad = g.dx[rows, :] * g.scale[1:2, :] + g.tmp[rows, :]
        back = norm_backward(grad, g.n1[rows, :], g.i1[rows, :], g.gain[0:1, :], 0)
        g.sm[6:7, :] += jnp.sum(back * g.x[rows, :].astype(F32), 0, keepdims=True)
        g.dx[rows, :] = back
        g.dtb[rows, :] = back.astype(BF)

    over_rows(2 * t, 64, first_back)
    d_self = nt(g.dtb[...], g.w_so[...]).astype(BF)
    g.dself[...] = d_self[t:]
    g.dos[...] = d_self[:t].T.reshape(HEADS, hd, t)
    do_copies = [
        Spread(g.dos.at[h], g.dor.at[own_turn], g.do_s.at[h], g.do_r, h * split + own_part)
        for h in range(HEADS)
    ]
    for copy in do_copies:
        copy.start()

    class Small:
        def __init__(self):
            self.at = -1

        def advance(self):
            steps = z.bits + z.row_bits
            if self.at == steps:
                return
            if self.at >= 0:
                self.copy.wait()
                g.sm[...] = g.sm[...] + g.smr[self.at]
            self.at += 1
            k = self.at
            if k < steps:
                dev = (seq_partner(k), r) if k < z.bits else (s, row_partner(k - z.bits))
                self.copy = remote(g.sm, g.smr.at[k], g.sms.at[k], g.smrs.at[k], dev)
                self.copy.start()

    sums["small"] = Small()
    advance("small")

    doc_kv = g.mkv[...].reshape(n * mt, 2 * d)
    mem_t = g.mg[...].reshape(n * mt, d).T
    win_t = g.mw[...].T
    for part in range(2):
        cols = slice(part * d, (part + 1) * d)
        put_rows("cm", nn(mem_t, doc_kv[:, cols]) + nn(win_t, g.pm[:, cols]), part * d)
    advance("cm", "fo")
    g.mg[...] = nt(doc_kv, g.w_cm[...]).astype(BF).reshape(n, mt, d)
    advance("mk", "cm")
    g.dmp[...] = nt(g.pm[...], g.w_cm[...])
    g.hms[0:z.mhalo, :] = g.dmp[0:z.mhalo, :].astype(BF)
    g.hms[z.mhalo:, :] = g.dmp[z.mhalo + mt:, :].astype(BF)
    mem_halo = [
        remote(g.hms.at[pl.ds(0, z.mhalo)], g.hmr.at[pl.ds(z.mhalo, z.mhalo)],
               g.hs.at[5], g.hr.at[5], (prv, r)),
        remote(g.hms.at[pl.ds(z.mhalo, z.mhalo)], g.hmr.at[pl.ds(0, z.mhalo)],
               g.hs.at[6], g.hr.at[6], (nxt, r)),
    ]
    for copy in mem_halo:
        copy.start()

    put_rows("cq", nn(g.h1b[...].T, g.dcq[...]))
    advance("cq", "mk")
    put_rows("so", nn(g.att[...].T, g.dtb[...]))
    advance("so", "small", "fi", "cq")

    for p in range(pairs):
        q, k, v = g.qp[:, pair_cols(p)], g.ps[:, pair_cols(p)], g.ps[:, pair_cols(p, d)]
        go, o = g.dself[:, pair_cols(p)], g.op[:, pair_cols(p)]
        dqs, dk, dv = [], 0.0, 0.0
        for w in range(2):
            qm, gm = only(q, w), only(go, w)
            sc = nt(qm, k) * softmax_scale - kept_lse(SELF_PACKED + 2 * p + w)
            weights = jnp.concatenate(
                [jnp.where(own_mask, jnp.exp(sc[:, :t]), 0.0),
                 jnp.where(prev_mask, jnp.exp(sc[:, t:]), 0.0)], 1)
            delta = jnp.sum(gm.astype(F32) * o, -1, keepdims=True)
            ds = (weights * (nt(gm, v) - delta)).astype(BF)
            dqs.append(nn(ds, k))
            dk = dk + tn(ds, qm)
            dv = dv + tn(weights.astype(BF), gm)
        g.qp[:, pair_cols(p)] = (both(*dqs) * softmax_scale).astype(BF)
        g.ps[:, pair_cols(p)] = (dk * softmax_scale).astype(BF)
        g.ps[:, pair_cols(p, d)] = dv.astype(BF)
    window_t = g.xw[...].T
    put_rows("sp", nn(window_t[:, :t], g.qp[...]), 0)
    put_rows("sp", nn(window_t, g.ps[:, :d]), d)
    put_rows("sp", nn(window_t, g.ps[:, d:]), 2 * d)
    advance("sp", "so", "co")
    g.dxp[...] = nt(g.ps[...], g.w_sp[:, d:])
    g.hss[...] = g.dxp[t:, :].astype(BF)
    self_halo = remote(g.hss, g.hsr, g.hs.at[7], g.hr.at[7], (prv, r))
    self_halo.start()
    g.tmp[t:, :] = nt(g.qp[...], g.w_sp[:, :d]) + g.dxp[0:t, :]


    tokens_all.finish()
    tokens_all.drain()
    wait_whole(g.dor, g.do_r)
    g.dg[...] = jnp.zeros_like(g.dg)
    g.dwt[...] = jnp.zeros_like(g.dwt)
    dq_copies, kf_copies = [], []
    chunk = min(512, n * t)

    def kept(which, first, last):
        row, column = first // ff * 2 * hd + which * hd, first % ff
        return slice(row, row + hd), slice(column, column + last - first)

    def sibling(i, f):
        return remote(
            g.kvst.at[i, f], g.kvsib.at[i, my_part], g.sib_s.at[i, f], g.sib_r.at[i, my_part],
            (my_head * split + f, r))

    def share_kv(i):
        for f in range(split):
            @pl.when(my_part != f)
            def _():
                sibling(i, f).start()

    def close_kv(i):
        g.kvfin[i] = g.kvst[i, my_part]
        for f in range(split):
            @pl.when(my_part != f)
            def _():
                wait_whole(g.kvsib.at[i, f], g.sib_r.at[i, f])
                g.kvfin[i] = g.kvfin[i] + g.kvsib[i, f]
        copy = Spread(g.kvfin.at[i], g.dkvr.at[my_head], g.kf_s.at[i], g.kf_r, i * split + my_part)
        copy.start()
        kf_copies.append(copy)

    turns = {
        7: ("sp", "fi", "small"), 6: ("fo",), 5: ("cm", "co"), 4: ("fo", "fi", "small"),
        3: ("mk", "cq", "so"), 2: ("fi", "fo", "co"), 1: ("cm", "small"), 0: ("mk", "cq", "so", "fo", "co"),
    }
    for i in reversed(range(HEADS)):
        b = i * split + turn_rest(i)
        qt, gt = g.qt[i], g.dor[i]
        q, go = qt.T, gt.T
        delta = jnp.sum(go.astype(F32) * g.of[i], -1, keepdims=True)
        lse = kept_lse(SELF_DOC + i)
        low = i * wide
        spans = [(a, min(a + chunk, low), False) for a in range(0, low, chunk)]
        spans.append((low, low + wide, True))
        dq = 0.0
        for first, last, masked in spans:
            k, v = g.kts[:, first:last], g.vts[:, first:last]
            weights = jnp.exp(nn(q, k) * softmax_scale - lse)
            if masked:
                weights = jnp.where(diag_mask(i), weights, 0.0)
            ds = (weights * (nn(go, v) - delta)).astype(BF)
            dq = dq + nt(ds, k)
            g.dg[kept(0, first, last)] += nn(qt, ds)
            g.dg[kept(1, first, last)] += nn(gt, weights.astype(BF))
        dqt = (dq * softmax_scale).T.astype(BF)
        g.ots[i] = dqt
        copy = Spread(g.ots.at[i], g.dqr.at[my_head], g.dq_s.at[i], g.dq_r, b)
        copy.start()
        dq_copies.append(copy)
        for f in range(split):
            first = (i * split + f) * t
            g.kvst[i, f, 0:hd] = (g.dg[kept(0, first, first + t)] * softmax_scale).astype(BF)
            g.kvst[i, f, hd:] = g.dg[kept(1, first, first + t)].astype(BF)
        share_kv(i)
        g.dwt[0:hd, :] += nn(dqt, g.xg[place_of(b)])
        for f in range(split):
            g.dwt[hd:, :] += nn(g.kvst[i, f], g.xg[reverse_static(i * split + f, z.bits)])
        if i < HEADS - 1:
            close_kv(i + 1)
        advance(*turns[i])
    close_kv(0)

    whole = jnp.concatenate([g.dwt[...], jnp.zeros((hd, d), F32)], 0)
    g.dws[...] = whole.T.astype(BF).reshape(n, d // n, 4 * hd)
    dw_copies = [
        Spread(g.dws.at[o], g.dwr.at[s], g.dw_s.at[o], g.dw_r, o) for o in range(n)
    ]
    for copy in dw_copies:
        copy.start()

    advance("sp", "small")
    wait_whole(g.dqr, g.dq_r)
    g.dproj[:, 0:d] = g.dqr[...].reshape(d, t).T
    wait_whole(g.dkvr, g.kf_r)
    for part in range(2):
        g.dproj[:, (part + 1) * d:(part + 2) * d] = (
            g.dkvr[:, part * hd:(part + 1) * hd, :].reshape(d, t).T)
    g.tmp[0:t, :] = nt(g.dproj[...], g.w_sp[...])
    self_halo.wait()
    g.tmp[2 * t - z.halo:, :] += g.hsr[...].astype(F32)

    def last(rows):
        g.dx[rows, :] = g.dx[rows, :] * g.scale[0:1, :] + g.tmp[rows, :]

    over_rows(2 * t, 64, last)

    wait_whole(g.dwr, g.dw_r)
    def parts_of(h):
        total = g.dwr[h * split].astype(F32)
        for f in range(1, split):
            total = total + g.dwr[h * split + f].astype(F32)
        return total
    for p in range(pairs):
        left, right = parts_of(2 * p), parts_of(2 * p + 1)
        for part in range(3):
            cols = slice(part * hd, (part + 1) * hd)
            g.dsh[:, pair_cols(p, part * d)] = jnp.concatenate([left[:, cols], right[:, cols]], 1).astype(BF)

    def shares(k):
        return remote(g.dsh, g.dshr.at[k], g.dy_s.at[k], g.dy_r.at[k], (s, row_partner(k)))

    shares(0).start()
    advance("cm", "mk", "cq", "so", "sp")

    restored(g.dx[0:t, :], g.dx[t:, :], g.dx_out)

    order = ("fo", "fi", "co", "cm", "mk", "cq", "so", "sp", "small")
    for k in range(z.row_bits - 1):
        shares(k).wait()
        g.dsh[...] = g.dsh[...] + g.dshr[k]
        shares(k + 1).start()
    while any(sums[name].at < (
            len(z.steps(name)) if name != "small" else z.bits + z.row_bits) for name in order):
        advance(*order)
    shares(z.row_bits - 1).wait()
    g.g_sp[...] = g.g_sp[...] + (g.dsh[...].astype(F32) + g.dshr[z.row_bits - 1].astype(F32))
    for copy in mem_halo:
        copy.wait()
    restored(sums["mk"].result().astype(F32),
             g.dmp[z.mhalo:z.mhalo + mt, :] + g.hmr[...].astype(F32), g.dm_out)
    turned = pltpu.roll(g.sm[...], lax.rem(d - s * (d // n), d), 1)
    g.b_gain[...] = turned[0:3, :d // n]
    g.b_bias[...] = turned[3:6, :d // n]
    g.b_scale[...] = turned[6:9, :d // n]
    g.b_fo[...] = turned[9:10, :d // n]
    at = s * (ff // n)
    row = g.sm[pl.ds(10 + lax.div(at, d), 1), :]
    g.b_fi[...] = pltpu.roll(row, lax.rem(d - lax.rem(at, d), d), 1)[:, :ff // n]
    for copy in do_copies + dq_copies + kf_copies + dw_copies:
        copy.wait_send()
    for i in range(HEADS):
        for f in range(split):
            @pl.when(my_part != f)
            def _():
                sibling(i, f).wait_send()


def on_device(
    mesh_shape,
    tokens, memory, segments, padding, cotangent,
    self_project, self_output, cross_query, cross_memory, cross_output,
    feed_in, feed_in_bias, feed_out, feed_out_bias, norm_gain, norm_bias, residual_scale,
):
    t, _, d = tokens.shape
    mt = memory.shape[0]
    ff = feed_in.shape[1]
    n, rows = mesh_shape
    z = Sizes(n, rows, t, mt, d, ff)

    scratch = z.scratch()
    names = INPUTS + OUTPUTS + tuple(scratch)
    vmem, anywhere = pl.BlockSpec(memory_space=pltpu.VMEM), pl.BlockSpec(memory_space=pl.ANY)
    shapes = [
        jax.ShapeDtypeStruct((t, 2, d), BF),
        jax.ShapeDtypeStruct((t, 2, d), F32),
        jax.ShapeDtypeStruct((mt, 2, d), F32),
    ] + [
        jax.ShapeDtypeStruct(z.sums[name][:2], F32)
        for name in ("sp", "so", "cq", "cm", "co", "fi", "fo")
    ] + [
        jax.ShapeDtypeStruct((1, ff // n), F32), jax.ShapeDtypeStruct((1, d // n), F32),
    ] + [jax.ShapeDtypeStruct((3, d // n), F32)] * 3
    outcome = pl.pallas_call(
        functools.partial(layer_kernel, z, names),
        out_shape=shapes,
        in_specs=[vmem] * 5 + [anywhere] * 7 + [vmem] * 5,
        out_specs=[vmem] * len(OUTPUTS),
        scratch_shapes=list(scratch.values()),
        compiler_params=pltpu.CompilerParams(
            collective_id=0, has_side_effects=True, vmem_limit_bytes=63 * 2 ** 20),
        name="layer",
    )(
        tokens, memory, cotangent, segments, padding,
        self_project, self_output, cross_query, cross_memory, cross_output, feed_in, feed_out,
        feed_in_bias.reshape(1, ff), feed_out_bias.reshape(1, d), norm_gain, norm_bias, residual_scale,
    )

    def hand_on(*refs):
        sources, results, sems = refs[:len(shapes)], refs[len(shapes):-1], refs[-1]
        copies = [
            pltpu.make_async_copy(source, result, sems.at[j])
            for j, (source, result) in enumerate(zip(sources, results))
        ]
        for copy in copies:
            copy.start()
        for copy in copies:
            copy.wait()

    outcome = pl.pallas_call(
        hand_on,
        out_shape=shapes,
        in_specs=[vmem] * len(shapes),
        out_specs=[anywhere] * len(shapes),
        scratch_shapes=[pltpu.SemaphoreType.DMA((len(shapes),))],
        name="results",
    )(*outcome)
    (out, dx, dm, g_sp, g_so, g_cq, g_cm, g_co, g_fi, g_fo,
     in_bias, out_bias, gain, bias, scale) = outcome
    return (
        out, dx, dm, g_sp, g_so, g_cq, g_cm, g_co, g_fi, in_bias.reshape(ff // n),
        g_fo, out_bias.reshape(d // n), gain, bias, scale,
    )


def solution(mesh):
    in_specs = (
        P("seq", "rows", None), P("seq", "rows", None), P("rows", "seq"), P("rows", "seq"),
        P("seq", "rows", None),
    ) + (P(),) * 12
    out_specs = (P("seq", "rows", None),) * 3 + (
        P("seq", None), P("seq", None), P("seq", None), P("seq", None), P("seq", None),
        P("seq", None), P("seq"), P("seq", None), P("seq"),
        P(None, "seq"), P(None, "seq"), P(None, "seq"),
    )
    shape = (mesh.shape["seq"], mesh.shape["rows"])
    return jax.shard_map(
        functools.partial(on_device, shape),
        mesh=mesh, in_specs=in_specs, out_specs=out_specs, check_vma=False,
    )
```

```python
import functools
import math

import jax
import jax.numpy as jnp
from jax import lax
from jax.experimental import pallas as pl
from jax.experimental.pallas import tpu as pltpu
from jax.sharding import PartitionSpec as P

HEADS = 8
EPSILON = 1e-05
NEGATIVE = -1e30
BF = jnp.bfloat16
F32 = jnp.float32
I32 = jnp.int32
MESH = pl.DeviceIdType.MESH
GELU_A = math.sqrt(2.0 / math.pi)
GELU_B = 0.044715


def nn(a, b):
    return jnp.dot(a, b, preferred_element_type=F32)


def nt(a, b):
    return lax.dot_general(a, b, (((1,), (1,)), ((), ())), preferred_element_type=F32)


def tn(a, b):
    return lax.dot_general(a, b, (((0,), (0,)), ((), ())), preferred_element_type=F32)


def log2(value):
    return int(value).bit_length() - 1


def reverse_static(index, bits):
    return sum(((index >> k) & 1) << (bits - 1 - k) for k in range(bits))


class Sizes:
    def __init__(self, n, rows, t, mt, d, ff):
        self.n, self.rows, self.t, self.mt, self.d, self.ff = n, rows, t, mt, d, ff
        self.bits, self.row_bits = log2(n), log2(rows)
        self.split = n // HEADS
        self.hd = d // HEADS
        self.halo = t // 2
        self.mhalo = mt // 2
        self.sums = {
            "fo0": (ff // n, d // 2, "rows second", "fo", 0),
            "fo1": (ff // n, d // 2, "rows third", "fo", d // 2),
            "fi0": (d // n, ff // 2, "far first", "fi", 0),
            "fi1": (d // n, ff // 2, "rows second", "fi", ff // 2),
            "co": (d // n, d, "rows second", "co", 0),
            "cq": (d // n, d, "rows third", "cq", 0),
            "mk": (mt, d, "seq alone", "mk", 0),
            "cm": (d // n, 2 * d, "rows third", "cm", 0),
            "so": (d // n, d, "rows second", "so", 0),
            "sp": (d // n, 3 * d, "rows third", "sp", 0),
        }

    def seq_bits(self, name):
        if self.sums[name][2] == "far first":
            return [0, 2, 1] + list(range(3, self.bits))
        return list(range(self.bits))

    def steps(self, name):
        order = self.sums[name][2]
        seq = [("seq", k) for k in self.seq_bits(name)]
        rows = [("exchange", k) for k in range(self.row_bits)]
        if order == "seq alone":
            return seq
        at = self.halving(name)
        if at is not None:
            return seq[:at] + [("halve", 0)] + seq[at:] + rows[1:] + [("gather", 0)]
        return seq + rows

    def halving(self, name):
        return {"rows second": 1, "rows third": 2}.get(self.sums[name][2])

    def parts(self, name):
        return 1 if self.halving(name) is None else 2

    def received(self, name):
        held, first, spans = self.n * self.parts(name), 0, []
        for kind, _ in self.steps(name):
            held = held // 2 if kind in ("seq", "halve") else held
            spans.append((first, held))
            first += held
        return spans, first

    def scratch(self):
        n, t, mt, d, ff, hd, split = self.n, self.t, self.mt, self.d, self.ff, self.hd, self.split
        v, dma = pltpu.VMEM, pltpu.SemaphoreType.DMA
        small_steps = self.bits + self.row_bits
        spec = dict(
            w_sp=v((d, 3 * d), BF), w_so=v((d, d), BF), w_cq=v((d, d), BF), w_cm=v((d, 2 * d), BF),
            w_co=v((d, d), BF), w_fi=v((d, ff), BF), w_fo=v((ff, d), BF),
            x=v((2 * t, d), BF), mem=v((2 * mt, d), BF), cot=v((2 * t, d), BF),
            dx=v((2 * t, d), F32), codes=v((8, t), I32),
            xg=v((n, t, d), BF), mg=v((n, mt, d), BF), mkv=v((n, mt, 2 * d), BF),
            qkvt=v((HEADS, 3 * hd, t), BF), kv=v((split, HEADS, 2 * hd, t), BF),
            qt=v((HEADS, hd, t), BF), kts=v((hd, n * t), BF), vts=v((hd, n * t), BF),
            ots=v((HEADS, hd, t), BF), otr=v((HEADS, hd, t), BF), of=v((HEADS, t, hd), F32),
            dos=v((HEADS, hd, t), BF), dor=v((HEADS, hd, t), BF), dqr=v((HEADS, hd, t), BF),
            dwt=v((3 * hd, d), F32),
            kvst=v((HEADS, split, 2 * hd, t), BF), kvsib=v((HEADS, split, 2 * hd, t), BF),
            kvfin=v((HEADS, 2 * hd, t), BF), dkvr=v((HEADS, 2 * hd, t), BF),
            dws=v((split, n // split, d // n, 4 * hd), BF), dwsib=v((split, n // split, d // n, 4 * hd), BF),
            dwr=v((HEADS, d // n, 4 * hd), BF),
            dsh=v((d // n, 3 * d), BF), dshr=v((self.row_bits, d // n, 3 * d), BF),
            xw=v((t + self.halo, d), BF), mw=v((2 * mt, d), BF),
            qp=v((t, d), BF), ps=v((t + self.halo, 2 * d), BF), pm=v((2 * mt, 2 * d), BF),
            cp=v((8, t), I32), cn=v((8, t), I32),
            lse=v((t, 4 * HEADS), F32),
            op=v((t, d), F32), co32=v((2 * t, d), F32),
            hss=v((self.halo, d), BF), hsr=v((self.halo, d), BF),
            hms=v((mt, d), BF), hmr=v((mt, d), BF),
            att=v((2 * t, d), BF), catt=v((2 * t, d), BF), cqv=v((2 * t, d), BF),
            tmp=v((2 * t, d), F32), n1=v((2 * t, d), F32), n2=v((2 * t, d), F32),
            i1=v((2 * t, 1), F32), i2=v((2 * t, 1), F32),
            h1b=v((2 * t, d), BF), h2b=v((2 * t, d), BF),
            act=v((2 * t, ff), BF), dg=v((2 * t, ff), F32),
            dtb=v((2 * t, d), BF), dc=v((2 * t, d), BF), dcq=v((2 * t, d), BF),
            dself=v((t, d), BF), dproj=v((t, 3 * d), BF),
            o_out=v((t, 2, d), BF), o_dx=v((t, 2, d), F32), o_dm=v((mt, 2, d), F32),
            o_sp=v((d // n, 3 * d), F32), o_so=v((d // n, d), F32), o_cq=v((d // n, d), F32),
            o_cm=v((d // n, 2 * d), F32), o_co=v((d // n, d), F32),
            o_fi=v((d // n, ff), F32), o_fo=v((ff // n, d), F32),
            sm=v((16, d), F32), smr=v((small_steps, 16, d), F32),
        )
        for name, (r, c, _, _, _) in self.sums.items():
            parts = self.parts(name)
            if name != "mk":
                spec["a_" + name] = v((n * parts, r, c // parts), BF)
            spec["r_" + name] = v((self.received(name)[1], r, c // parts), BF)
            spec["ss_" + name] = dma
            spec["rs_" + name] = dma((len(self.steps(name)),))
        spec.update(
            sms=dma, smrs=dma((small_steps,)),
            wsem=dma((7,)), xgs=dma((4,)), xgr=dma((n,)), mgs=dma((4,)), mgr=dma((n,)),
            hs=dma((8,)), hr=dma((8,)),
            kv_s=dma, kv_r=dma, kw_s=dma((split,)), kw_r=dma((split,)),
            q_s=dma, q_r=dma, o_s=dma, o_r=dma, do_s=dma, do_r=dma,
            dq_s=dma, dq_r=dma, kf_s=dma, kf_r=dma,
            sib_s=dma, sib_r=dma((HEADS, split - 1)),
            ds_s=dma((split,)), ds_r=dma((split,)), dw_s=dma, dw_r=dma,
            outs=dma((len(self.sums) + 3,)), dy_s=dma((self.row_bits,)), dy_r=dma((self.row_bits,)),
        )
        return spec


ORDER = (
    "fo_mm", "fo0", "dpre", "fo1", "sb", "fo0", "fi_mm", "fi1", "fo1", "dc", "xd0", "fi0", "xd1", "xd2",
    "fi0", "fi1", "co_mm", "xp", "xd3", "fo0", "cqm", "fb", "fo1", "cq", "psb", "fi0", "som", "so", "fo0",
    "cmm", "fi1", "small", "fo1", "cq", "spm", "dmp", "fo0", "sp", "out", "xg3", "cm", "fi0", "small",
    "sd7", "fi1", "fo1", "co", "mkm", "cm", "so", "sd6", "fi1", "cq", "small", "fo0", "sd5", "sp", "cq",
    "sd4", "fi0", "small", "co", "sd3", "so", "sd2", "cm", "sd1", "fi1", "small", "sd0", "cq", "mk", "fo1",
    "co", "mk", "dwm", "dwo", "cm", "sp", "so", "co", "sp", "so", "cm", "co", "dxp", "mk", "fi0", "cm",
    "small", "co", "cq", "sp", "so", "cq", "fo1", "mk", "fin2", "fin1", "cm", "sp", "fo0", "co", "fi1",
    "mk", "so", "sp",
)


class Refs:
    def __init__(self, names, refs):
        for name, ref in zip(names, refs):
            setattr(self, name, ref)


INPUTS = (
    "x_in", "mem_in", "cot_in", "seg_in", "pad_in",
    "h_sp", "h_so", "h_cq", "h_cm", "h_co", "h_fi", "h_fo",
    "fi_b", "fo_b", "gain", "bias", "scale",
)
OUTPUTS = (
    "out", "dx_out", "dm_out", "g_sp", "g_so", "g_cq", "g_cm", "g_co", "g_fi", "g_fo",
    "b_fi", "b_fo", "b_gain", "b_bias", "b_scale",
)


def layer_kernel(z, names, *refs):
    g = Refs(names, refs)
    g.dxp, g.dmp = g.co32.at[pl.ds(0, z.t + z.halo)], g.n2.at[pl.ds(0, 2 * z.mt)]
    n, t, mt, d, ff, hd, split = z.n, z.t, z.mt, z.d, z.ff, z.hd, z.split
    half = 2 * hd
    pairs = d // half
    softmax_scale = 1.0 / math.sqrt(hd)
    s = lax.axis_index("seq")
    r = lax.axis_index("rows")

    def bit_of(index, k):
        return lax.rem(lax.div(index, 2 ** k), 2)

    def seq_partner(k):
        return s + (1 - 2 * bit_of(s, k)) * 2 ** k

    def row_partner(k):
        return r + (1 - 2 * bit_of(r, k)) * 2 ** k

    def place_of(index):
        return sum(bit_of(index, k) * 2 ** (z.bits - 1 - k) for k in range(z.bits))

    nxt = lax.rem(s + 1, n)
    prv = lax.rem(s + n - 1, n)
    my_head = lax.div(s, split)
    my_part = lax.rem(s, split)
    own_turn = lax.div(s, split)
    own_rest = lax.rem(s, split)
    own_part = own_rest + lax.rem(own_turn, 2) * (split - 1 - 2 * own_rest)

    barrier = pltpu.get_barrier_semaphore()
    for step in range(1, n):
        pl.semaphore_signal(barrier, inc=1, device_id=(lax.rem(s + step, n), r), device_id_type=MESH)
    for k in range(z.row_bits):
        pl.semaphore_signal(barrier, inc=1, device_id=(s, row_partner(k)), device_id_type=MESH)

    loads = {
        name: pltpu.make_async_copy(getattr(g, "h_" + name), getattr(g, "w_" + name), g.wsem.at[j])
        for j, name in enumerate(("sp", "cm", "so", "cq", "co", "fi", "fo"))
    }
    loads["sp"].start()

    def remote(src, dst, ssem, rsem, dev):
        return pltpu.make_async_remote_copy(
            src_ref=src, dst_ref=dst, send_sem=ssem, recv_sem=rsem,
            device_id=dev, device_id_type=MESH,
        )

    class Spread:
        def __init__(self, src, dst, ssem, rsem, dest):
            self.dest = dest
            self.far = remote(src, dst, ssem, rsem, (dest, r))
            self.near = pltpu.make_async_copy(src, dst, rsem)

        def start(self):
            @pl.when(self.dest != s)
            def _():
                self.far.start()

            @pl.when(self.dest == s)
            def _():
                self.near.start()

    def wait_whole(ref, sem):
        pltpu.make_async_copy(ref, ref, sem).wait()

    def wait_sent(ref, sem, own):
        count = ref.shape[0]

        @pl.when(own)
        def _():
            wait_whole(ref.at[pl.ds(0, count - 1)], sem)

        @pl.when(jnp.logical_not(own))
        def _():
            wait_whole(ref, sem)

    class Chain:
        def __init__(self, buf, send, recv):
            self.buf, self.send, self.recv = buf, send, recv
            self.line = n // 4
            self.zz, self.xx, self.core = lax.div(s, 4), bit_of(s, 1), bit_of(s, 0)

        def copy(self, way, origin):
            dev = (s + 4, s - 4, s + 2 - 4 * self.xx, s + 1 - 2 * self.core)[way]
            at = place_of(origin)
            block = self.buf.at[at]
            return remote(block, block, self.send.at[way], self.recv.at[at], (dev, r))

        def arrive(self, origin):
            at = place_of(origin)
            wait_whole(self.buf.at[at], self.recv.at[at])

        def pass_on(self, zz, ahead, back):
            origin = s + 4 * (zz - self.zz)
            if ahead:
                @pl.when(self.zz < self.line - 1)
                def _():
                    self.copy(0, origin).start()
            if back:
                @pl.when(self.zz > 0)
                def _():
                    self.copy(1, origin).start()
            self.copy(2, origin).start()
            self.copy(3, origin).start()

        def start(self):
            self.pass_on(self.zz, True, True)

        def step(self, j):
            low, high = self.zz - 1 - j, self.zz + 1 + j

            @pl.when(low >= 0)
            def _():
                self.arrive(s + 4 * (low - self.zz))
                self.pass_on(low, True, False)

            @pl.when(high < self.line)
            def _():
                self.arrive(s + 4 * (high - self.zz))
                self.pass_on(high, False, True)

        def cross_step(self, j):
            other = s + 2 - 4 * self.xx
            for sign in ((1,) if j == 0 else (-1, 1)):
                zz = self.zz + sign * j

                @pl.when((zz >= 0) & (zz < self.line))
                def _():
                    origin = other + 4 * (zz - self.zz)
                    self.arrive(origin)
                    self.copy(3, origin).start()

        def finish(self):
            other = s + 1 - 2 * self.core
            for k in range(2 * self.line):
                self.arrive(lax.rem(other, 2) + 2 * k)

        def drain(self):
            for zz in range(self.line):
                for way, count in ((0, zz + 1 if zz < self.line - 1 else 0), (1, self.line - zz if zz else 0)):
                    if count:
                        @pl.when(self.zz == zz)
                        def _():
                            wait_whole(self.buf.at[pl.ds(0, count)], self.send.at[way])
            wait_whole(self.buf.at[pl.ds(0, self.line)], self.send.at[2])
            wait_whole(self.buf.at[pl.ds(0, 2 * self.line)], self.send.at[3])

    class Sum:
        def __init__(self, name, number):
            self.name, self.number = name, number
            self.share, self.columns, _, target, self.offset = z.sums[name]
            self.out, self.result_at = getattr(g, "o_" + target, None), getattr(g, "g_" + target, None)
            self.a = g.mg if name == "mk" else getattr(g, "a_" + name)
            self.r = getattr(g, "r_" + name)
            self.ss, self.rs = getattr(g, "ss_" + name), getattr(g, "rs_" + name)
            self.steps, self.parts = z.steps(name), z.parts(name)
            self.spans = z.received(name)[0]
            self.copies = {}
            self.at = -1

        def held(self, i):
            if i == 0:
                return self.a, 0, n * self.parts
            return (self.r,) + self.spans[i - 1]

        def bit(self, i):
            kind, k = self.steps[i]
            return bit_of(s, k) if kind == "seq" else bit_of(r, k)

        def start(self, i):
            ref, first, blocks = self.held(i)
            into, into_first, count = self.held(i + 1)
            kind, k = self.steps[i]
            src = ref.at[pl.ds(first + (1 - self.bit(i)) * count, count)] if blocks > count else (
                ref.at[pl.ds(first, count)])
            dev = (seq_partner(k), r) if kind == "seq" else (s, row_partner(k))
            self.copies[i] = remote(src, into.at[pl.ds(into_first, count)], self.ss, self.rs.at[i], dev)
            self.copies[i].start()

        def finish(self, i):
            self.copies[i].wait()
            ref, first, blocks = self.held(i)
            into, into_first, count = self.held(i + 1)
            kind, k = self.steps[i]
            last = i + 1 == len(self.steps)
            if kind == "gather":
                width = self.columns // 2
                mine, theirs = bit_of(r, 0) * width, (1 - bit_of(r, 0)) * width
                self.out[:, pl.ds(pl.multiple_of(self.offset + mine, 128), width)] = ref[first].astype(F32)
                self.out[:, pl.ds(pl.multiple_of(self.offset + theirs, 128), width)] = (
                    into[into_first].astype(F32))
                return
            if last and self.out is not None:
                self.out[:, self.offset:self.offset + self.columns] = (
                    into[into_first].astype(F32) + ref[first].astype(F32))
                return
            base = first + self.bit(i) * count if blocks > count else first
            if count <= 2:
                for j in range(count):
                    into[into_first + j] = into[into_first + j] + ref[base + j]
            else:
                def add(j, carry):
                    into[into_first + j] = into[into_first + j] + ref[base + j]
                    return carry
                lax.fori_loop(0, count, add, 0)

        def output(self):
            cols = pl.ds(self.offset, self.columns)
            return pltpu.make_async_copy(
                self.out.at[:, cols], self.result_at.at[:, cols], g.outs.at[self.number])

        def over(self):
            return self.at == len(self.steps)

        def advance(self):
            if self.over():
                return
            if self.at >= 0:
                self.finish(self.at)
            self.at += 1
            if not self.over():
                self.start(self.at)
            elif self.out is not None and self.name != "sp":
                self.output().start()

        def result(self):
            ref, first, _ = self.held(len(self.steps))
            return ref[first]

        def put(self, owner, value, first_column):
            width = self.columns // self.parts
            position = sum(
                ((owner >> k) & 1) << (z.bits - 1 - j) for j, k in enumerate(z.seq_bits(self.name)))
            below = n >> (z.halving(self.name) or 0)
            above, rest = position // below, position % below
            for part in range(self.parts):
                start = self.offset + part * width
                low, high = max(first_column, start), min(first_column + value.shape[1], start + width)
                if low < high:
                    where = (above * self.parts + part) * below + rest
                    self.a[where, :, low - start:high - start] = (
                        value[:, low - first_column:high - first_column])

    class Small:
        def __init__(self):
            self.at = -1

        def over(self):
            return self.at == z.bits + z.row_bits

        def advance(self):
            if self.over():
                return
            if self.at >= 0:
                self.copy.wait()
                g.sm[...] = g.sm[...] + g.smr[self.at]
            self.at += 1
            k = self.at
            if not self.over():
                dev = (seq_partner(k), r) if k < z.bits else (s, row_partner(k - z.bits))
                self.copy = remote(g.sm, g.smr.at[k], g.sms, g.smrs.at[k], dev)
                self.copy.start()

    sums = {name: Sum(name, j) for j, name in enumerate(z.sums)}
    sums["small"] = Small()

    def put_rows(target, value, first_column=0, first_owner=0):
        value = value.astype(BF)
        for name, (share, _, _, output, _) in z.sums.items():
            if output == target:
                for j in range(value.shape[0] // share):
                    sums[name].put(first_owner + j, value[j * share:(j + 1) * share], first_column)

    def over_rows(count, size, step):
        def one(j, carry):
            step(pl.ds(pl.multiple_of(j * size, size), size))
            return carry
        lax.fori_loop(0, count // size, one, 0)

    def mean(value):
        return jnp.sum(value, -1, keepdims=True) * (1.0 / d)

    def norm_forward(total):
        centred = total - mean(total)
        inverse = lax.rsqrt(mean(centred * centred) + EPSILON)
        return centred * inverse, inverse

    def norm_backward(grad, normed, inverse, gain_row, which):
        scaled = grad * gain_row
        result = inverse * (scaled - mean(scaled) - normed * mean(scaled * normed))
        g.sm[which:which + 1, :] += jnp.sum(grad * normed, 0, keepdims=True)
        g.sm[3 + which:4 + which, :] += jnp.sum(grad, 0, keepdims=True)
        return result

    lane = lax.broadcasted_iota(I32, (t, half), 1)

    def only(value, which):
        keep = (lane < hd) if which == 0 else (lane >= hd)
        return jnp.where(keep, value, jnp.zeros_like(value))

    def both(first, second):
        return jnp.where(lane < hd, first, second)

    def pair_cols(p, offset=0):
        return slice(offset + p * half, offset + (p + 1) * half)

    def keep_lse(index, value):
        g.lse[:, index:index + 1] = value

    def kept_lse(index):
        return g.lse[:, index:index + 1]

    SELF_PACKED, CROSS_PACKED, CROSS_DOC, SELF_DOC = (k * HEADS for k in range(4))

    tokens_all = Chain(g.xg, g.xgs, g.xgr)
    memory_all = Chain(g.mg, g.mgs, g.mgr)
    place = place_of(s)
    other_seg = g.seg_in[1:2, :]
    swap = jnp.min(other_seg, -1, keepdims=True) == jnp.max(other_seg, -1, keepdims=True)

    def ordered(ref, into):
        first, second, count = ref[:, 0, :], ref[:, 1, :], ref.shape[0]
        into[0:count, :] = jnp.where(swap, second, first)
        into[count:, :] = jnp.where(swap, first, second)

    def restored(first, second, ref):
        ref[:, 0, :] = jnp.where(swap, second, first)
        ref[:, 1, :] = jnp.where(swap, first, second)

    ordered(g.x_in, g.x)
    ordered(g.mem_in, g.mem)
    seg = jnp.where(swap, g.seg_in[0:1, :], other_seg)
    pad = jnp.where(swap, g.pad_in[0:1, :], g.pad_in[1:2, :])
    q_at = lax.broadcasted_iota(I32, (t, t), 0)
    k_at = lax.broadcasted_iota(I32, (t, t), 1)
    seg_q = jnp.sum(jnp.where(q_at == k_at, seg.astype(F32), 0.0), -1, keepdims=True).astype(I32)
    pick = (q_at == 2 * lax.rem(k_at + z.mhalo, mt)).astype(F32)
    mem_seg = jnp.dot(
        jnp.broadcast_to(seg.astype(F32), (8, t)), pick,
        precision=lax.Precision.HIGHEST, preferred_element_type=F32).astype(I32)
    g.codes[0:1, :] = seg
    g.codes[1:2, :] = pad
    g.codes[2:3, :] = pltpu.roll(seg, z.halo, 1)
    g.codes[3:4, :] = pltpu.roll(pad, z.halo, 1)
    g.codes[4:8, :] = mem_seg[0:4]
    loads["sp"].wait()
    for name in ("cm", "so", "cq", "co", "fi", "fo"):
        loads[name].start()

    for part in range(3):
        made = nn(g.x[0:t, :], g.w_sp[:, part * d:(part + 1) * d]).astype(BF)
        g.qkvt[:, part * hd:(part + 1) * hd, :] = made.T.reshape(HEADS, hd, t)
    g.xg[place] = g.x[0:t, :]
    g.mg[place] = g.mem[0:mt, :]
    g.xw[0:t, :] = g.x[t:, :]
    g.mw[z.mhalo:z.mhalo + mt, :] = g.mem[mt:, :]
    g.sm[...] = jnp.zeros_like(g.sm)
    pl.semaphore_wait(barrier, n - 1 + z.row_bits)
    for h in range(HEADS):
        Spread(g.qkvt.at[h, pl.ds(hd, 2 * hd)], g.kv.at[my_part, own_turn], g.kv_s, g.kv_r,
               h * split + my_part).start()
    for h in range(HEADS):
        Spread(g.qkvt.at[h, pl.ds(0, hd)], g.qt.at[own_turn], g.q_s, g.q_r, h * split + own_part).start()
    halo_copies = [
        remote(g.codes, g.cn, g.hs.at[0], g.hr.at[0], (prv, r)),
        remote(g.codes, g.cp, g.hs.at[1], g.hr.at[1], (nxt, r)),
        remote(g.x.at[pl.ds(2 * t - z.halo, z.halo)], g.xw.at[pl.ds(t, z.halo)],
               g.hs.at[2], g.hr.at[2], (nxt, r)),
        remote(g.mem.at[pl.ds(mt, z.mhalo)], g.mw.at[pl.ds(z.mhalo + mt, z.mhalo)],
               g.hs.at[3], g.hr.at[3], (prv, r)),
        remote(g.mem.at[pl.ds(2 * mt - z.mhalo, z.mhalo)], g.mw.at[pl.ds(0, z.mhalo)],
               g.hs.at[4], g.hr.at[4], (nxt, r)),
    ]
    for copy in halo_copies:
        copy.start()

    memory_all.start()

    g.qp[...] = nn(g.xw[0:t, :], g.w_sp[:, :d]).astype(BF)
    ordered(g.cot_in, g.cot)

    def self_mask():
        seg_k, pad_k = g.codes[0:1, :], g.codes[1:2, :]
        own = (seg_q == seg_k) & (k_at <= q_at) & ((pad_k == 1) | (k_at == q_at))
        prev = (seg_q == g.cp[2:3, :]) & (g.cp[3:4, :] == 1)
        return own, prev[:, :z.halo]

    def cross_mask():
        at = lax.broadcasted_iota(I32, (1, 2 * mt), 1)
        seg_k = jnp.where(
            at < z.mhalo, g.cp[4:5, :],
            jnp.where(at < z.mhalo + mt, g.codes[4:5, :], g.cn[4:5, :]))
        return seg_q == seg_k

    def softmax_parts(scores):
        top = functools.reduce(jnp.maximum, [jnp.max(b, -1, keepdims=True) for b in scores])
        weights = [jnp.exp(b - top) for b in scores]
        total = functools.reduce(jnp.add, [jnp.sum(w, -1, keepdims=True) for w in weights])
        return weights, total, top + jnp.log(total)

    def hand_over(f):
        return remote(g.kv.at[my_part], g.kv.at[my_part], g.kw_s.at[f], g.kw_r.at[my_part],
                      (my_head * split + f, r))

    wait_whole(g.kv.at[my_part], g.kv_r)
    for f in range(split):
        @pl.when(my_part != f)
        def _():
            hand_over(f).start()
    wait_whole(g.qt, g.q_r)
    for f in range(split):
        @pl.when(my_part != f)
        def _():
            wait_whole(g.kv.at[f], g.kw_r.at[f])
    for b in range(n):
        g.kts[:, b * t:(b + 1) * t] = g.kv[b % split, b // split, 0:hd]
        g.vts[:, b * t:(b + 1) * t] = g.kv[b % split, b // split, hd:]

    wide = split * t
    diag_q = lax.broadcasted_iota(I32, (t, wide), 0)
    diag_k = lax.broadcasted_iota(I32, (t, wide), 1)

    def turn_rest(i):
        return my_part if i % 2 == 0 else split - 1 - my_part

    def diag_mask(i):
        return diag_k <= diag_q + turn_rest(i) * t

    for i in range(HEADS):
        b = i * split + turn_rest(i)
        q = g.qt[i].T
        low = i * wide
        blocks = []
        if low:
            blocks.append(nn(q, g.kts[:, :low]) * softmax_scale)
        blocks.append(jnp.where(
            diag_mask(i), nn(q, g.kts[:, low:low + wide]) * softmax_scale, NEGATIVE))
        weights, total, lse = softmax_parts(blocks)
        keep_lse(SELF_DOC + i, lse)
        o = nt(weights[-1].astype(BF), g.vts[:, low:low + wide])
        if low:
            o = o + nt(weights[0].astype(BF), g.vts[:, :low])
        o = o / total
        g.of[i] = o
        g.ots[i] = o.T.astype(BF)
        Spread(g.ots.at[i], g.otr.at[my_head], g.o_s, g.o_r, b).start()
        if i == 3:
            memory_all.step(0)
            memory_all.cross_step(0)
    for j in range(1, n // 4 - 2):
        memory_all.step(j)
        memory_all.cross_step(j)

    tokens_all.start()

    for copy in halo_copies:
        copy.wait()
    g.ps[...] = nn(g.xw[...], g.w_sp[:, d:]).astype(BF)
    loads["cm"].wait()
    g.pm[...] = nn(g.mw[...], g.w_cm[...]).astype(BF)
    own_mask, prev_mask = self_mask()
    for p in range(pairs):
        q, k, v = g.qp[:, pair_cols(p)], g.ps[:, pair_cols(p)], g.ps[:, pair_cols(p, d)]
        outs = []
        for w in range(2):
            sc = nt(only(q, w), k) * softmax_scale
            blocks = [jnp.where(own_mask, sc[:, :t], NEGATIVE), jnp.where(prev_mask, sc[:, t:], NEGATIVE)]
            weights, total, lse = softmax_parts(blocks)
            keep_lse(SELF_PACKED + 2 * p + w, lse)
            o = nn(weights[0].astype(BF), v[:t]) + nn(weights[1].astype(BF), v[t:])
            outs.append(o / total)
        o = both(*outs)
        g.op[:, pair_cols(p)] = o
        g.att[t:, pair_cols(p)] = o.astype(BF)

    memory_all.step(n // 4 - 2)
    memory_all.cross_step(n // 4 - 2)

    loads["so"].wait()
    wait_whole(g.otr, g.o_r)
    g.att[0:t, :] = g.otr[...].reshape(d, t).T
    g.tmp[...] = nn(g.att[...], g.w_so[...])

    def first_norm(rows):
        total = g.x[rows, :].astype(F32) * g.scale[0:1, :] + g.tmp[rows, :]
        normed, inverse = norm_forward(total)
        g.n1[rows, :] = normed
        g.i1[rows, :] = inverse
        g.h1b[rows, :] = (normed * g.gain[0:1, :] + g.bias[0:1, :]).astype(BF)

    over_rows(2 * t, 64, first_norm)
    loads["cq"].wait()
    g.cqv[...] = nn(g.h1b[...], g.w_cq[...]).astype(BF)

    seen = cross_mask()
    for p in range(pairs):
        q, k, v = g.cqv[t:, pair_cols(p)], g.pm[:, pair_cols(p)], g.pm[:, pair_cols(p, d)]
        outs = []
        for w in range(2):
            sc = jnp.where(seen, nt(only(q, w), k) * softmax_scale, NEGATIVE)
            (weights,), total, lse = softmax_parts([sc])
            keep_lse(CROSS_PACKED + 2 * p + w, lse)
            outs.append(nn(weights.astype(BF), v) / total)
        o = both(*outs)
        g.co32[t:, pair_cols(p)] = o
        g.catt[t:, pair_cols(p)] = o.astype(BF)
    tokens_all.step(0)
    tokens_all.cross_step(0)
    memory_all.cross_step(n // 4 - 1)
    memory_all.finish()

    for part in range(2):
        cols = slice(part * d, (part + 1) * d)
        g.mkv[:, :, cols] = nn(g.mg[...].reshape(n * mt, d), g.w_cm[:, cols]).astype(BF).reshape(n, mt, d)

    for p in range(pairs):
        q = g.cqv[0:t, pair_cols(p)]
        k = g.mkv[:, :, pair_cols(p)].reshape(n * mt, half)
        v = g.mkv[:, :, pair_cols(p, d)].reshape(n * mt, half)
        outs = []
        for w in range(2):
            sc = nt(only(q, w), k) * softmax_scale
            (weights,), total, lse = softmax_parts([sc])
            keep_lse(CROSS_DOC + 2 * p + w, lse)
            outs.append(nn(weights.astype(BF), v) / total)
        o = both(*outs)
        g.co32[0:t, pair_cols(p)] = o
        g.catt[0:t, pair_cols(p)] = o.astype(BF)
        if p == 3:
            tokens_all.step(1)
            tokens_all.cross_step(1)
    stays = own_part == my_part
    wait_whole(g.kvfin.at[pl.ds(0, HEADS - 1)], g.kv_s)
    wait_sent(g.qt, g.q_s, stays)
    wait_sent(g.ots, g.o_s, stays)
    for f in range(split):
        @pl.when(my_part != f)
        def _():
            hand_over(f).wait_send()
    memory_all.drain()

    loads["co"].wait()
    g.tmp[...] = nn(g.catt[...], g.w_co[...])

    def second_norm(rows):
        hidden1 = g.n1[rows, :] * g.gain[0:1, :] + g.bias[0:1, :]
        normed, inverse = norm_forward(hidden1 * g.scale[1:2, :] + g.tmp[rows, :])
        g.n2[rows, :] = normed
        g.i2[rows, :] = inverse
        g.h2b[rows, :] = (normed * g.gain[1:2, :] + g.bias[1:2, :]).astype(BF)

    over_rows(2 * t, 64, second_norm)

    loads["fi"].wait()
    chunks = ff // d
    for c in range(chunks):
        cols = slice(c * d, (c + 1) * d)
        pre = nn(g.h2b[...], g.w_fi[:, cols]) + g.fi_b[0:1, cols]
        square = pre * pre
        bent = jnp.tanh(GELU_A * pre * (1.0 + GELU_B * square))
        g.act[:, cols] = (0.5 * pre * (1.0 + bent)).astype(BF)
        g.dg[:, cols] = 0.5 * (1.0 + bent) + 0.5 * pre * (1.0 - bent * bent) * (
            GELU_A * (1.0 + 3.0 * GELU_B * square))
    tokens_all.step(2)
    tokens_all.cross_step(2)
    loads["fo"].wait()
    g.tmp[...] = nn(g.act[...], g.w_fo[...])

    def third_norm(rows):
        hidden2 = g.n2[rows, :] * g.gain[1:2, :] + g.bias[1:2, :]
        total = hidden2 * g.scale[2:3, :] + (g.tmp[rows, :] + g.fo_b[0:1, :])
        normed, inverse = norm_forward(total)
        grad = g.cot[rows, :].astype(F32)
        g.cot[rows, :] = (normed * g.gain[2:3, :] + g.bias[2:3, :]).astype(BF)
        back = norm_backward(grad, normed, inverse, g.gain[2:3, :], 2)
        g.sm[8:9, :] += jnp.sum(back * hidden2, 0, keepdims=True)
        g.dx[rows, :] = back
        low = back.astype(BF)
        g.dtb[rows, :] = low
        g.sm[9:10, :] += jnp.sum(low.astype(F32), 0, keepdims=True)

    over_rows(2 * t, 64, third_norm)

    for j in range(3, n // 4 - 1):
        tokens_all.step(j)
        tokens_all.cross_step(j)

    def feed_out_grads():
        for c in range(chunks):
            cols = slice(c * d, (c + 1) * d)
            put_rows("fo", nn(g.act[:, cols].T, g.dtb[...]), 0, c * d // z.sums["fo0"][0])

    def before_gelu():
        for c in range(chunks):
            cols = slice(c * d, (c + 1) * d)
            back = (nt(g.dtb[...], g.w_fo[cols, :]) * g.dg[:, cols]).astype(BF)
            g.act[:, cols] = back
            g.sm[10 + c:11 + c, :] = jnp.sum(back.astype(F32), 0, keepdims=True)

    def feed_in_grads():
        h2t = g.h2b[...].T
        for c in range(chunks):
            cols = slice(c * d, (c + 1) * d)
            put_rows("fi", nn(h2t, g.act[:, cols]), c * d)

    def second_norm_back():
        g.tmp[...] = nt(g.act[...], g.w_fi[...])

        def second_back(rows):
            grad = g.dx[rows, :] * g.scale[2:3, :] + g.tmp[rows, :]
            back = norm_backward(grad, g.n2[rows, :], g.i2[rows, :], g.gain[1:2, :], 1)
            hidden1 = g.n1[rows, :] * g.gain[0:1, :] + g.bias[0:1, :]
            g.sm[7:8, :] += jnp.sum(back * hidden1, 0, keepdims=True)
            g.dx[rows, :] = back
            g.dtb[rows, :] = back.astype(BF)

        over_rows(2 * t, 64, second_back)

    def cross_output_back():
        g.dc[...] = nt(g.dtb[...], g.w_co[...]).astype(BF)

    def cross_output_grads():
        put_rows("co", nn(g.catt[...].T, g.dtb[...]))

    def result_out():
        restored(g.cot[0:t, :], g.cot[t:, :], g.o_out)
        pltpu.make_async_copy(g.o_out, g.out, g.outs.at[len(z.sums)]).start()

    def cross_document(p):
        q, go, o = g.cqv[0:t, pair_cols(p)], g.dc[0:t, pair_cols(p)], g.co32[0:t, pair_cols(p)]
        qt, gt = q.T, go.T
        k = g.mkv[:, :, pair_cols(p)].reshape(n * mt, half)
        v = g.mkv[:, :, pair_cols(p, d)].reshape(n * mt, half)
        dqs, dks, dvs = [], [], []
        for w in range(2):
            qm, gm = only(q, w), only(go, w)
            weights = jnp.exp(nt(qm, k) * softmax_scale - kept_lse(CROSS_DOC + 2 * p + w))
            delta = jnp.sum(gm.astype(F32) * o, -1, keepdims=True)
            ds = (weights * (nt(gm, v) - delta)).astype(BF)
            dqs.append(nn(ds, k))
            dks.append(nn(qt[w * hd:(w + 1) * hd], ds))
            dvs.append(nn(gt[w * hd:(w + 1) * hd], weights.astype(BF)))
        g.dcq[0:t, pair_cols(p)] = (both(*dqs) * softmax_scale).astype(BF)
        dk = (jnp.concatenate(dks, 0) * softmax_scale).astype(BF).T
        dv = jnp.concatenate(dvs, 0).astype(BF).T
        g.mkv[:, :, pair_cols(p)] = dk.reshape(n, mt, half)
        g.mkv[:, :, pair_cols(p, d)] = dv.reshape(n, mt, half)

    def cross_packed():
        for p in range(pairs):
            q, k, v = g.cqv[t:, pair_cols(p)], g.pm[:, pair_cols(p)], g.pm[:, pair_cols(p, d)]
            go, o = g.dc[t:, pair_cols(p)], g.co32[t:, pair_cols(p)]
            dqs, dk, dv = [], 0.0, 0.0
            for w in range(2):
                qm, gm = only(q, w), only(go, w)
                weights = jnp.where(
                    seen, jnp.exp(nt(qm, k) * softmax_scale - kept_lse(CROSS_PACKED + 2 * p + w)), 0.0)
                delta = jnp.sum(gm.astype(F32) * o, -1, keepdims=True)
                ds = (weights * (nt(gm, v) - delta)).astype(BF)
                dqs.append(nn(ds, k))
                dk = dk + tn(ds, qm)
                dv = dv + tn(weights.astype(BF), gm)
            g.dcq[t:, pair_cols(p)] = (both(*dqs) * softmax_scale).astype(BF)
            g.pm[:, pair_cols(p)] = (dk * softmax_scale).astype(BF)
            g.pm[:, pair_cols(p, d)] = dv.astype(BF)

    late = {}

    def first_norm_back():
        g.tmp[...] = nt(g.dcq[...], g.w_cq[...])

        def first_back(rows):
            grad = g.dx[rows, :] * g.scale[1:2, :] + g.tmp[rows, :]
            back = norm_backward(grad, g.n1[rows, :], g.i1[rows, :], g.gain[0:1, :], 0)
            g.sm[6:7, :] += jnp.sum(back * g.x[rows, :].astype(F32), 0, keepdims=True)
            g.dx[rows, :] = back
            g.dtb[rows, :] = back.astype(BF)

        over_rows(2 * t, 64, first_back)
        d_self = nt(g.dtb[...], g.w_so[...]).astype(BF)
        g.dself[...] = d_self[t:]
        g.dos[...] = d_self[:t].T.reshape(HEADS, hd, t)
        for h in range(HEADS):
            Spread(g.dos.at[h], g.dor.at[own_turn], g.do_s, g.do_r, h * split + own_part).start()

    def cross_memory_grads():
        mem_t = g.mg[...].reshape(n * mt, d).T
        win_t = g.mw[...].T
        for part in range(2):
            cols = slice(part * d, (part + 1) * d)
            doc_kv = g.mkv[:, :, cols].reshape(n * mt, d)
            put_rows("cm", nn(mem_t, doc_kv) + nn(win_t, g.pm[:, cols]), part * d)

    def memory_back():
        g.mg[...] = nt(g.mkv[...].reshape(n * mt, 2 * d), g.w_cm[...]).astype(BF).reshape(n, mt, d)

    def memory_halo():
        g.dmp[...] = nt(g.pm[...], g.w_cm[...])
        g.hms[0:z.mhalo, :] = g.dmp[0:z.mhalo, :].astype(BF)
        g.hms[z.mhalo:, :] = g.dmp[z.mhalo + mt:, :].astype(BF)
        late["memory"] = [
            remote(g.hms.at[pl.ds(0, z.mhalo)], g.hmr.at[pl.ds(z.mhalo, z.mhalo)],
                   g.hs.at[5], g.hr.at[5], (prv, r)),
            remote(g.hms.at[pl.ds(z.mhalo, z.mhalo)], g.hmr.at[pl.ds(0, z.mhalo)],
                   g.hs.at[6], g.hr.at[6], (nxt, r)),
        ]
        for copy in late["memory"]:
            copy.start()

    def cross_query_grads():
        put_rows("cq", nn(g.h1b[...].T, g.dcq[...]))

    def self_output_grads():
        put_rows("so", nn(g.att[...].T, g.dtb[...]))

    def self_packed():
        for p in range(pairs):
            q, k, v = g.qp[:, pair_cols(p)], g.ps[:, pair_cols(p)], g.ps[:, pair_cols(p, d)]
            go, o = g.dself[:, pair_cols(p)], g.op[:, pair_cols(p)]
            dqs, dk, dv = [], 0.0, 0.0
            for w in range(2):
                qm, gm = only(q, w), only(go, w)
                sc = nt(qm, k) * softmax_scale - kept_lse(SELF_PACKED + 2 * p + w)
                weights = jnp.concatenate(
                    [jnp.where(own_mask, jnp.exp(sc[:, :t]), 0.0),
                     jnp.where(prev_mask, jnp.exp(sc[:, t:]), 0.0)], 1)
                delta = jnp.sum(gm.astype(F32) * o, -1, keepdims=True)
                ds = (weights * (nt(gm, v) - delta)).astype(BF)
                dqs.append(nn(ds, k))
                dk = dk + tn(ds, qm)
                dv = dv + tn(weights.astype(BF), gm)
            g.qp[:, pair_cols(p)] = (both(*dqs) * softmax_scale).astype(BF)
            g.ps[:, pair_cols(p)] = (dk * softmax_scale).astype(BF)
            g.ps[:, pair_cols(p, d)] = dv.astype(BF)

    def self_project_grads():
        window_t = g.xw[...].T
        put_rows("sp", nn(window_t[:, :t], g.qp[...]), 0)
        put_rows("sp", nn(window_t, g.ps[:, :d]), d)
        put_rows("sp", nn(window_t, g.ps[:, d:]), 2 * d)

    def tokens_halo():
        g.dxp[...] = nt(g.ps[...], g.w_sp[:, d:])
        g.hss[...] = g.dxp[t:, :].astype(BF)
        late["tokens"] = remote(g.hss, g.hsr, g.hs.at[7], g.hr.at[7], (prv, r))
        late["tokens"].start()
        g.tmp[t:, :] = nt(g.qp[...], g.w_sp[:, :d]) + g.dxp[0:t, :]

    chunk = min(512, n * t)

    def kept(which, first, last):
        row, column = first // ff * 2 * hd + which * hd, first % ff
        return slice(row, row + hd), slice(column, column + last - first)

    def sibling(i, f):
        return remote(
            g.kvst.at[i, f], g.kvsib.at[i, my_part], g.sib_s,
            g.sib_r.at[i, lax.rem(my_part - f + split, split) - 1], (my_head * split + f, r))

    def to_siblings(action):
        for f in range(split):
            @pl.when(my_part != f)
            def _():
                action(f)

    def close_kv(i):
        g.kvfin[i] = g.kvst[i, my_part]

        def add(f):
            wait_whole(g.kvsib.at[i, f], g.sib_r.at[i, lax.rem(f - my_part + split, split) - 1])
            g.kvfin[i] = g.kvfin[i] + g.kvsib[i, f]

        to_siblings(add)
        Spread(g.kvfin.at[i], g.dkvr.at[my_head], g.kf_s, g.kf_r, i * split + my_part).start()

    def self_document(i):
        if i == HEADS - 1:
            tokens_all.finish()
            tokens_all.drain()
            wait_whole(g.dor, g.do_r)
            g.dg[...] = jnp.zeros_like(g.dg)
            g.dwt[...] = jnp.zeros_like(g.dwt)
        b = i * split + turn_rest(i)
        qt, gt = g.qt[i], g.dor[i]
        q, go = qt.T, gt.T
        delta = jnp.sum(go.astype(F32) * g.of[i], -1, keepdims=True)
        lse = kept_lse(SELF_DOC + i)
        low = i * wide
        spans = [(a, min(a + chunk, low), False) for a in range(0, low, chunk)]
        spans.append((low, low + wide, True))
        dq = 0.0
        for first, last, masked in spans:
            k, v = g.kts[:, first:last], g.vts[:, first:last]
            weights = jnp.exp(nn(q, k) * softmax_scale - lse)
            if masked:
                weights = jnp.where(diag_mask(i), weights, 0.0)
            ds = (weights * (nn(go, v) - delta)).astype(BF)
            dq = dq + nt(ds, k)
            g.dg[kept(0, first, last)] += nn(qt, ds)
            g.dg[kept(1, first, last)] += nn(gt, weights.astype(BF))
        dqt = (dq * softmax_scale).T.astype(BF)
        g.ots[i] = dqt
        Spread(g.ots.at[i], g.dqr.at[my_head], g.dq_s, g.dq_r, b).start()
        for f in range(split):
            first = (i * split + f) * t
            g.kvst[i, f, 0:hd] = (g.dg[kept(0, first, first + t)] * softmax_scale).astype(BF)
            g.kvst[i, f, hd:] = g.dg[kept(1, first, first + t)].astype(BF)
        to_siblings(lambda f: sibling(i, f).start())
        g.dwt[0:hd, :] += nn(dqt, g.xg[place_of(b)])
        for f in range(split):
            g.dwt[hd:, :] += nn(g.kvst[i, f], g.xg[reverse_static(i * split + f, z.bits)])
        if i < HEADS - 1:
            close_kv(i + 1)

    def head_parts(f):
        return remote(g.dws.at[f], g.dwsib.at[my_part], g.ds_s.at[f], g.ds_r.at[my_part],
                      (my_head * split + f, r))

    def head_grads():
        whole = jnp.concatenate([g.dwt[...], jnp.zeros((hd, d), F32)], 0).T.astype(BF)
        share = d // n
        for o in range(n):
            g.dws[o % split, o // split] = whole[o * share:(o + 1) * share]
        to_siblings(lambda f: head_parts(f).start())

    def head_owners():
        close_kv(0)

        def add(f):
            wait_whole(g.dwsib.at[f], g.ds_r.at[f])
            g.dws[my_part] = g.dws[my_part] + g.dwsib[f]

        to_siblings(add)
        for j in range(n // split):
            Spread(g.dws.at[my_part, j], g.dwr.at[my_head], g.dw_s, g.dw_r, j * split + my_part).start()

    def tokens_back():
        wait_whole(g.dqr, g.dq_r)
        g.dproj[:, 0:d] = g.dqr[...].reshape(d, t).T
        wait_whole(g.dkvr, g.kf_r)
        for part in range(2):
            g.dproj[:, (part + 1) * d:(part + 2) * d] = (
                g.dkvr[:, part * hd:(part + 1) * hd, :].reshape(d, t).T)
        g.tmp[0:t, :] = nt(g.dproj[...], g.w_sp[...])
        late["tokens"].wait()
        g.tmp[2 * t - z.halo:, :] += g.hsr[...].astype(F32)

        def last(rows):
            g.dx[rows, :] = g.dx[rows, :] * g.scale[0:1, :] + g.tmp[rows, :]

        over_rows(2 * t, 64, last)
        restored(g.dx[0:t, :], g.dx[t:, :], g.o_dx)
        pltpu.make_async_copy(g.o_dx, g.dx_out, g.outs.at[len(z.sums) + 1]).start()

    def shares(k):
        return remote(g.dsh, g.dshr.at[k], g.dy_s.at[k], g.dy_r.at[k], (s, row_partner(k)))

    def head_shares():
        wait_whole(g.dwr, g.dw_r)
        for p in range(pairs):
            left, right = g.dwr[2 * p], g.dwr[2 * p + 1]
            for part in range(3):
                cols = slice(part * hd, (part + 1) * hd)
                g.dsh[:, pair_cols(p, part * d)] = jnp.concatenate([left[:, cols], right[:, cols]], 1)
        shares(0).start()

    pieces = dict(
        fo_mm=feed_out_grads, dpre=before_gelu, fi_mm=feed_in_grads, sb=second_norm_back,
        dc=cross_output_back, co_mm=cross_output_grads, out=result_out, xp=cross_packed,
        fb=first_norm_back, cmm=cross_memory_grads, mkm=memory_back, dmp=memory_halo,
        cqm=cross_query_grads, som=self_output_grads, psb=self_packed, spm=self_project_grads,
        dxp=tokens_halo, dwm=head_grads, dwo=head_owners, fin1=tokens_back, fin2=head_shares,
        xg3=lambda: tokens_all.cross_step(n // 4 - 1),
    )
    for p in range(pairs):
        pieces["xd%d" % p] = functools.partial(cross_document, p)
    for i in range(HEADS):
        pieces["sd%d" % i] = functools.partial(self_document, i)
    for name in ORDER:
        if name in pieces:
            pieces[name]()
        else:
            sums[name].advance()

    for k in range(z.row_bits - 1):
        shares(k).wait()
        g.dsh[...] = g.dsh[...] + g.dshr[k]
        shares(k + 1).start()
    while not all(one.over() for one in sums.values()):
        for one in sums.values():
            one.advance()
    for copy in late["memory"]:
        copy.wait()
    restored(sums["mk"].result().astype(F32),
             g.dmp[z.mhalo:z.mhalo + mt, :] + g.hmr[...].astype(F32), g.o_dm)
    pltpu.make_async_copy(g.o_dm, g.dm_out, g.outs.at[len(z.sums) + 2]).start()
    turned = pltpu.roll(g.sm[...], lax.rem(d - s * (d // n), d), 1)
    g.b_gain[...] = turned[0:3, :d // n]
    g.b_bias[...] = turned[3:6, :d // n]
    g.b_scale[...] = turned[6:9, :d // n]
    g.b_fo[...] = turned[9:10, :d // n]
    at = s * (ff // n)
    row = g.sm[pl.ds(10 + lax.div(at, d), 1), :]
    g.b_fi[...] = pltpu.roll(row, lax.rem(d - lax.rem(at, d), d), 1)[:, :ff // n]
    shares(z.row_bits - 1).wait()
    g.o_sp[...] = g.o_sp[...] + (g.dsh[...].astype(F32) + g.dshr[z.row_bits - 1].astype(F32))
    sums["sp"].output().start()
    wait_sent(g.dos, g.do_s, stays)
    wait_sent(g.ots, g.dq_s, stays)
    wait_whole(g.kvfin.at[pl.ds(0, HEADS - 1)], g.kf_s)
    wait_whole(g.dws.at[0, pl.ds(0, HEADS - 1)], g.dw_s)
    wait_whole(g.kvst.at[:, pl.ds(0, split - 1)], g.sib_s)
    to_siblings(lambda f: head_parts(f).wait_send())

    for one in sums.values():
        if isinstance(one, Sum) and one.out is not None:
            one.output().wait()
    for j, (src, dst) in enumerate(((g.o_out, g.out), (g.o_dx, g.dx_out), (g.o_dm, g.dm_out))):
        pltpu.make_async_copy(src, dst, g.outs.at[len(z.sums) + j]).wait()


def on_device(
    mesh_shape,
    tokens, memory, segments, padding, cotangent,
    self_project, self_output, cross_query, cross_memory, cross_output,
    feed_in, feed_in_bias, feed_out, feed_out_bias, norm_gain, norm_bias, residual_scale,
):
    t, _, d = tokens.shape
    mt = memory.shape[0]
    ff = feed_in.shape[1]
    n, rows = mesh_shape
    z = Sizes(n, rows, t, mt, d, ff)

    scratch = z.scratch()
    names = INPUTS + OUTPUTS + tuple(scratch)
    vmem, anywhere = pl.BlockSpec(memory_space=pltpu.VMEM), pl.BlockSpec(memory_space=pl.ANY)
    shapes = [
        jax.ShapeDtypeStruct((t, 2, d), BF),
        jax.ShapeDtypeStruct((t, 2, d), F32),
        jax.ShapeDtypeStruct((mt, 2, d), F32),
    ] + [
        jax.ShapeDtypeStruct(shape, F32)
        for shape in (
            (d // n, 3 * d), (d // n, d), (d // n, d), (d // n, 2 * d), (d // n, d), (d // n, ff), (ff // n, d))
    ] + [
        jax.ShapeDtypeStruct((1, ff // n), F32), jax.ShapeDtypeStruct((1, d // n), F32),
    ] + [jax.ShapeDtypeStruct((3, d // n), F32)] * 3
    outcome = pl.pallas_call(
        functools.partial(layer_kernel, z, names),
        out_shape=shapes,
        in_specs=[vmem] * 5 + [anywhere] * 7 + [vmem] * 5,
        out_specs=[anywhere] * 10 + [vmem] * 5,
        scratch_shapes=list(scratch.values()),
        compiler_params=pltpu.CompilerParams(
            collective_id=0, has_side_effects=True, vmem_limit_bytes=63 * 2 ** 20),
        name="layer",
    )(
        tokens, memory, cotangent, segments, padding,
        self_project, self_output, cross_query, cross_memory, cross_output, feed_in, feed_out,
        feed_in_bias.reshape(1, ff), feed_out_bias.reshape(1, d), norm_gain, norm_bias, residual_scale,
    )

    def hand_on(*refs):
        count = len(shapes)
        sources, results, held, sems = refs[:count], refs[count:2 * count], refs[2 * count:-1], refs[-1]
        into = [pltpu.make_async_copy(a, b, sems.at[0, j]) for j, (a, b) in enumerate(zip(sources, held))]
        out = [pltpu.make_async_copy(a, b, sems.at[1, j]) for j, (a, b) in enumerate(zip(held, results))]
        for copy in into:
            copy.start()
        for one, two in zip(into, out):
            one.wait()
            two.start()
        for copy in out:
            copy.wait()

    outcome = pl.pallas_call(
        hand_on,
        out_shape=shapes,
        in_specs=[anywhere] * len(shapes),
        out_specs=[anywhere] * len(shapes),
        scratch_shapes=[pltpu.VMEM(one.shape, one.dtype) for one in shapes] + [
            pltpu.SemaphoreType.DMA((2, len(shapes)))],
        name="results",
    )(*outcome)
    (out, dx, dm, g_sp, g_so, g_cq, g_cm, g_co, g_fi, g_fo,
     in_bias, out_bias, gain, bias, scale) = outcome
    return (
        out, dx, dm, g_sp, g_so, g_cq, g_cm, g_co, g_fi, in_bias.reshape(ff // n),
        g_fo, out_bias.reshape(d // n), gain, bias, scale,
    )


def solution(mesh):
    in_specs = (
        P("seq", "rows", None), P("seq", "rows", None), P("rows", "seq"), P("rows", "seq"),
        P("seq", "rows", None),
    ) + (P(),) * 12
    out_specs = (P("seq", "rows", None),) * 3 + (
        P("seq", None), P("seq", None), P("seq", None), P("seq", None), P("seq", None),
        P("seq", None), P("seq"), P("seq", None), P("seq"),
        P(None, "seq"), P(None, "seq"), P(None, "seq"),
    )
    shape = (mesh.shape["seq"], mesh.shape["rows"])
    return jax.shard_map(
        functools.partial(on_device, shape),
        mesh=mesh, in_specs=in_specs, out_specs=out_specs, check_vma=False,
    )
```

```python
import functools
import math

import jax
import jax.numpy as jnp
from jax import lax
from jax.experimental import pallas as pl
from jax.experimental.pallas import tpu as pltpu
from jax.sharding import PartitionSpec as P

HEADS = 8
EPSILON = 1e-05
NEGATIVE = -1e30
BF = jnp.bfloat16
F32 = jnp.float32
I32 = jnp.int32
MESH = pl.DeviceIdType.MESH
GELU_A = math.sqrt(2.0 / math.pi)
GELU_B = 0.044715


def nn(a, b):
    return jnp.dot(a, b, preferred_element_type=F32)


def nt(a, b):
    return lax.dot_general(a, b, (((1,), (1,)), ((), ())), preferred_element_type=F32)


def tn(a, b):
    return lax.dot_general(a, b, (((0,), (0,)), ((), ())), preferred_element_type=F32)


def log2(value):
    return int(value).bit_length() - 1


def reverse_static(index, bits):
    return sum(((index >> k) & 1) << (bits - 1 - k) for k in range(bits))


class Sizes:
    def __init__(self, n, rows, t, mt, d, ff):
        self.n, self.rows, self.t, self.mt, self.d, self.ff = n, rows, t, mt, d, ff
        self.bits, self.row_bits = log2(n), log2(rows)
        self.split = n // HEADS
        self.hd = d // HEADS
        self.halo = t // 2
        self.mhalo = mt // 2
        self.sums = {
            "fo0": (ff // n, d // 2, "far first", "fo", 0),
            "fo1": (ff // n, d // 2, "rows second", "fo", d // 2),
            "fi0": (d // n, ff // 2, "rows third", "fi", 0),
            "fi1": (d // n, ff // 2, "far first", "fi", ff // 2),
            "co": (d // n, d, "rows second", "co", 0),
            "cq": (d // n, d, "rows third", "cq", 0),
            "mk": (mt, d, "seq alone", "mk", 0),
            "cm": (d // n, 2 * d, "rows second", "cm", 0),
            "so": (d // n, d, "rows second", "so", 0),
            "sp": (d // n, 3 * d, "rows second", "sp", 0),
            "sm": (16, 128, "rows last", "sm", 0),
        }
        self.types = {"sm": F32}

    def seq_bits(self, name):
        if self.sums[name][2] == "far first":
            return [0, 2, 1] + list(range(3, self.bits))
        return list(range(self.bits))

    def steps(self, name):
        order = self.sums[name][2]
        seq = [("seq", k) for k in self.seq_bits(name)]
        rows = [("exchange", k) for k in range(self.row_bits)]
        if order == "seq alone":
            return seq
        at = self.halving(name)
        if at is not None:
            return seq[:at] + [("halve", 0)] + seq[at:] + rows[1:] + [("gather", 0)]
        return seq + rows

    def halving(self, name):
        return {"rows second": 1, "rows third": 2}.get(self.sums[name][2])

    def parts(self, name):
        return 1 if self.halving(name) is None else 2

    def received(self, name):
        held, first, spans = self.n * self.parts(name), 0, []
        for kind, _ in self.steps(name):
            held = held // 2 if kind in ("seq", "halve") else held
            spans.append((first, held))
            first += held
        return spans, first

    def scratch(self):
        n, t, mt, d, ff, hd, split = self.n, self.t, self.mt, self.d, self.ff, self.hd, self.split
        v, dma = pltpu.VMEM, pltpu.SemaphoreType.DMA
        spec = dict(
            w_sp=v((d, 3 * d), BF), w_so=v((d, d), BF), w_cq=v((d, d), BF), w_cm=v((d, 2 * d), BF),
            w_co=v((d, d), BF), w_fi=v((d, ff), BF), w_fo=v((ff, d), BF),
            x=v((2 * t, d), BF), mem=v((2 * mt, d), BF), cot=v((2 * t, d), BF),
            dx=v((2 * t, d), F32), codes=v((8, t), I32),
            xg=v((n, t, d), BF), mg=v((n, mt, d), BF), mkv=v((n, mt, 2 * d), BF),
            qkvt=v((HEADS, 3 * hd, t), BF), kv=v((split, HEADS, 2 * hd, t), BF),
            qt=v((HEADS, hd, t), BF), kts=v((hd, n * t), BF), vts=v((hd, n * t), BF),
            ots=v((HEADS, hd, t), BF), otr=v((HEADS, hd, t), BF), of=v((HEADS, t, hd), F32),
            dos=v((HEADS, hd, t), BF), dor=v((HEADS, hd, t), BF), dqr=v((HEADS, hd, t), BF),
            dwt=v((3 * hd, d), F32),
            kvst=v((HEADS, split, 2 * hd, t), BF), kvsib=v((HEADS, split, 2 * hd, t), BF),
            kvfin=v((HEADS, 2 * hd, t), BF), dkvr=v((HEADS, 2 * hd, t), BF),
            dws=v((split, n // split, d // n, 4 * hd), BF), dwsib=v((split, n // split, d // n, 4 * hd), BF),
            dwr=v((HEADS, d // n, 4 * hd), BF),
            dsh=v((d // n, 3 * d), BF), dshr=v((self.row_bits, d // n, 3 * d), BF),
            xw=v((t + self.halo, d), BF), mw=v((2 * mt, d), BF),
            qp=v((t, d), BF), ps=v((t + self.halo, 2 * d), BF), pm=v((2 * mt, 2 * d), BF),
            cp=v((8, t), I32), cn=v((8, t), I32),
            lse=v((t, 4 * HEADS), F32),
            op=v((t, d), F32), co32=v((2 * t, d), F32),
            hss=v((self.halo, d), BF), hsr=v((self.halo, d), BF),
            hms=v((mt, d), BF), hmr=v((mt, d), BF),
            att=v((2 * t, d), BF), catt=v((2 * t, d), BF), cqv=v((2 * t, d), BF),
            tmp=v((2 * t, d), F32), n1=v((2 * t, d), F32), n2=v((2 * t, d), F32),
            i1=v((2 * t, 1), F32), i2=v((2 * t, 1), F32),
            h1b=v((2 * t, d), BF), h2b=v((2 * t, d), BF),
            act=v((2 * t, ff), BF), dg=v((2 * t, ff), F32),
            dtb=v((2 * t, d), BF), dc=v((2 * t, d), BF), dcq=v((2 * t, d), BF),
            dself=v((t, d), BF), dproj=v((t, 3 * d), BF),
            o_out=v((t, 2, d), BF), o_dx=v((t, 2, d), F32), o_dm=v((mt, 2, d), F32),
            o_sp=v((d // n, 3 * d), F32), o_so=v((d // n, d), F32), o_cq=v((d // n, d), F32),
            o_cm=v((d // n, 2 * d), F32), o_co=v((d // n, d), F32),
            o_fi=v((d // n, ff), F32), o_fo=v((ff // n, d), F32),
            sm=v((16, d), F32), o_sm=v((16, 128), F32),
            o_bfi=v((1, ff // n), F32), o_bfo=v((1, d // n), F32),
            o_bgain=v((3, d // n), F32), o_bbias=v((3, d // n), F32), o_bscale=v((3, d // n), F32),
        )
        for name, (r, c, _, _, _) in self.sums.items():
            parts = self.parts(name)
            if name != "mk":
                spec["a_" + name] = v((n * parts, r, c // parts), self.types.get(name, BF))
            spec["r_" + name] = v((self.received(name)[1], r, c // parts), self.types.get(name, BF))
            spec["ss_" + name] = dma
            spec["rs_" + name] = dma((len(self.steps(name)),))
        spec.update(
            wsem=dma((7,)), xgs=dma((4,)), xgr=dma((n,)), mgs=dma((4,)), mgr=dma((n,)),
            hs=dma((8,)), hr=dma((8,)),
            kv_s=dma, kv_r=dma, kw_s=dma((split,)), kw_r=dma((split,)),
            q_s=dma, q_r=dma, o_s=dma, o_r=dma, do_s=dma, do_r=dma,
            dq_s=dma, dq_r=dma, kf_s=dma, kf_r=dma,
            sib_s=dma, sib_r=dma((HEADS, split - 1)),
            ds_s=dma((split,)), ds_r=dma((split,)), dw_s=dma, dw_r=dma,
            outs=dma((len(self.sums) + 8,)), dy_s=dma((self.row_bits,)), dy_r=dma((self.row_bits,)),
        )
        return spec


ORDER = (
    "fo_mm", "fo0", "dpre", "fi_mm", "fi0", "fi1", "fo0", "sb", "fi0", "co_mm", "dc", "co", "xd0", "out",
    "fi1", "xd1", "xp", "co", "fo0", "xd2", "xd3", "fo1", "fi0", "fb", "som", "fo1", "xg3", "smm", "sm",
    "cqm", "cq", "fi1", "so", "psb", "fi0", "spm", "sp", "fo0", "so", "cq", "cmm", "cm", "co", "sm", "fi1",
    "dmp", "sp", "sd7", "co", "fi0", "so", "sm", "sd5", "fo1", "co", "cq", "sd3", "sd1", "sp", "cm", "mkm",
    "so", "dwm", "mk", "dwo", "cm", "co", "fo1", "sm", "sp", "fi0", "mk", "dxp", "fo1", "cq", "sp", "cm",
    "fo0", "sm", "cq", "mk", "sp", "fi0", "cm", "co", "fo1", "so", "fi1", "fin2", "sm", "cq", "mk", "fin1",
    "fo0", "fo1", "cm", "so", "cm", "sp", "cq", "so", "fi1", "mk",
)


class Refs:
    def __init__(self, names, refs):
        for name, ref in zip(names, refs):
            setattr(self, name, ref)


INPUTS = (
    "x_in", "mem_in", "cot_in", "seg_in", "pad_in",
    "h_sp", "h_so", "h_cq", "h_cm", "h_co", "h_fi", "h_fo",
    "fi_b", "fo_b", "gain", "bias", "scale",
)
OUTPUTS = (
    "out", "dx_out", "dm_out", "g_sp", "g_so", "g_cq", "g_cm", "g_co", "g_fi", "g_fo",
    "b_fi", "b_fo", "b_gain", "b_bias", "b_scale",
)


def layer_kernel(z, names, *refs):
    g = Refs(names, refs)
    g.dxp, g.dmp = g.co32.at[pl.ds(0, z.t + z.halo)], g.n2.at[pl.ds(0, 2 * z.mt)]
    n, t, mt, d, ff, hd, split = z.n, z.t, z.mt, z.d, z.ff, z.hd, z.split
    half = 2 * hd
    pairs = d // half
    softmax_scale = 1.0 / math.sqrt(hd)
    s = lax.axis_index("seq")
    r = lax.axis_index("rows")

    def bit_of(index, k):
        return lax.rem(lax.div(index, 2 ** k), 2)

    def seq_partner(k):
        return s + (1 - 2 * bit_of(s, k)) * 2 ** k

    def row_partner(k):
        return r + (1 - 2 * bit_of(r, k)) * 2 ** k

    def place_of(index):
        return sum(bit_of(index, k) * 2 ** (z.bits - 1 - k) for k in range(z.bits))

    nxt = lax.rem(s + 1, n)
    prv = lax.rem(s + n - 1, n)
    my_head = lax.div(s, split)
    my_part = lax.rem(s, split)
    own_turn = lax.div(s, split)
    own_rest = lax.rem(s, split)
    own_part = own_rest + lax.rem(own_turn, 2) * (split - 1 - 2 * own_rest)

    barrier = pltpu.get_barrier_semaphore()
    for step in range(1, n):
        pl.semaphore_signal(barrier, inc=1, device_id=(lax.rem(s + step, n), r), device_id_type=MESH)
    for k in range(z.row_bits):
        pl.semaphore_signal(barrier, inc=1, device_id=(s, row_partner(k)), device_id_type=MESH)

    loads = {
        name: pltpu.make_async_copy(getattr(g, "h_" + name), getattr(g, "w_" + name), g.wsem.at[j])
        for j, name in enumerate(("sp", "cm", "so", "cq", "co", "fi", "fo"))
    }
    loads["sp"].start()

    def remote(src, dst, ssem, rsem, dev):
        return pltpu.make_async_remote_copy(
            src_ref=src, dst_ref=dst, send_sem=ssem, recv_sem=rsem,
            device_id=dev, device_id_type=MESH,
        )

    class Spread:
        def __init__(self, src, dst, ssem, rsem, dest):
            self.dest = dest
            self.far = remote(src, dst, ssem, rsem, (dest, r))
            self.near = pltpu.make_async_copy(src, dst, rsem)

        def start(self):
            @pl.when(self.dest != s)
            def _():
                self.far.start()

            @pl.when(self.dest == s)
            def _():
                self.near.start()

    def wait_whole(ref, sem):
        pltpu.make_async_copy(ref, ref, sem).wait()

    def wait_sent(ref, sem, own):
        count = ref.shape[0]

        @pl.when(own)
        def _():
            wait_whole(ref.at[pl.ds(0, count - 1)], sem)

        @pl.when(jnp.logical_not(own))
        def _():
            wait_whole(ref, sem)

    class Chain:
        def __init__(self, buf, send, recv):
            self.buf, self.send, self.recv = buf, send, recv
            self.line = n // 4
            self.zz, self.xx, self.core = lax.div(s, 4), bit_of(s, 1), bit_of(s, 0)

        def copy(self, way, origin):
            dev = (s + 4, s - 4, s + 2 - 4 * self.xx, s + 1 - 2 * self.core)[way]
            at = place_of(origin)
            block = self.buf.at[at]
            return remote(block, block, self.send.at[way], self.recv.at[at], (dev, r))

        def arrive(self, origin):
            at = place_of(origin)
            wait_whole(self.buf.at[at], self.recv.at[at])

        def pass_on(self, zz, ahead, back):
            origin = s + 4 * (zz - self.zz)
            if ahead:
                @pl.when(self.zz < self.line - 1)
                def _():
                    self.copy(0, origin).start()
            if back:
                @pl.when(self.zz > 0)
                def _():
                    self.copy(1, origin).start()
            self.copy(2, origin).start()
            self.copy(3, origin).start()

        def start(self):
            self.pass_on(self.zz, True, True)

        def step(self, j):
            low, high = self.zz - 1 - j, self.zz + 1 + j

            @pl.when(low >= 0)
            def _():
                self.arrive(s + 4 * (low - self.zz))
                self.pass_on(low, True, False)

            @pl.when(high < self.line)
            def _():
                self.arrive(s + 4 * (high - self.zz))
                self.pass_on(high, False, True)

        def cross_step(self, j):
            other = s + 2 - 4 * self.xx
            for sign in ((1,) if j == 0 else (-1, 1)):
                zz = self.zz + sign * j

                @pl.when((zz >= 0) & (zz < self.line))
                def _():
                    origin = other + 4 * (zz - self.zz)
                    self.arrive(origin)
                    self.copy(3, origin).start()

        def finish(self):
            other = s + 1 - 2 * self.core
            for k in range(2 * self.line):
                self.arrive(lax.rem(other, 2) + 2 * k)

        def drain(self):
            for zz in range(self.line):
                for way, count in ((0, zz + 1 if zz < self.line - 1 else 0), (1, self.line - zz if zz else 0)):
                    if count:
                        @pl.when(self.zz == zz)
                        def _():
                            wait_whole(self.buf.at[pl.ds(0, count)], self.send.at[way])
            wait_whole(self.buf.at[pl.ds(0, self.line)], self.send.at[2])
            wait_whole(self.buf.at[pl.ds(0, 2 * self.line)], self.send.at[3])

    class Sum:
        def __init__(self, name, number):
            self.name, self.number = name, number
            self.share, self.columns, _, target, self.offset = z.sums[name]
            self.out, self.result_at = getattr(g, "o_" + target, None), getattr(g, "g_" + target, None)
            self.a = g.mg if name == "mk" else getattr(g, "a_" + name)
            self.r = getattr(g, "r_" + name)
            self.ss, self.rs = getattr(g, "ss_" + name), getattr(g, "rs_" + name)
            self.steps, self.parts = z.steps(name), z.parts(name)
            self.spans = z.received(name)[0]
            self.copies = {}
            self.at = -1

        def held(self, i):
            if i == 0:
                return self.a, 0, n * self.parts
            return (self.r,) + self.spans[i - 1]

        def bit(self, i):
            kind, k = self.steps[i]
            return bit_of(s, k) if kind == "seq" else bit_of(r, k)

        def start(self, i):
            ref, first, blocks = self.held(i)
            into, into_first, count = self.held(i + 1)
            kind, k = self.steps[i]
            src = ref.at[pl.ds(first + (1 - self.bit(i)) * count, count)] if blocks > count else (
                ref.at[pl.ds(first, count)])
            dev = (seq_partner(k), r) if kind == "seq" else (s, row_partner(k))
            self.copies[i] = remote(src, into.at[pl.ds(into_first, count)], self.ss, self.rs.at[i], dev)
            self.copies[i].start()

        def finish(self, i):
            self.copies[i].wait()
            ref, first, blocks = self.held(i)
            into, into_first, count = self.held(i + 1)
            kind, k = self.steps[i]
            last = i + 1 == len(self.steps)
            if kind == "gather":
                width = self.columns // 2
                mine, theirs = bit_of(r, 0) * width, (1 - bit_of(r, 0)) * width
                self.out[:, pl.ds(pl.multiple_of(self.offset + mine, 128), width)] = ref[first].astype(F32)
                self.out[:, pl.ds(pl.multiple_of(self.offset + theirs, 128), width)] = (
                    into[into_first].astype(F32))
                return
            if last and self.out is not None:
                self.out[:, self.offset:self.offset + self.columns] = (
                    into[into_first].astype(F32) + ref[first].astype(F32))
                return
            base = first + self.bit(i) * count if blocks > count else first
            if count <= 2:
                for j in range(count):
                    into[into_first + j] = into[into_first + j] + ref[base + j]
            else:
                def add(j, carry):
                    into[into_first + j] = into[into_first + j] + ref[base + j]
                    return carry
                lax.fori_loop(0, count, add, 0)

        def output(self):
            cols = pl.ds(self.offset, self.columns)
            return pltpu.make_async_copy(
                self.out.at[:, cols], self.result_at.at[:, cols], g.outs.at[self.number])

        def over(self):
            return self.at == len(self.steps)

        def advance(self):
            if self.over():
                return
            if self.at >= 0:
                self.finish(self.at)
            self.at += 1
            if not self.over():
                self.start(self.at)
            elif self.out is not None and self.name not in ("sp", "sm"):
                self.output().start()

        def result(self):
            ref, first, _ = self.held(len(self.steps))
            return ref[first]

        def put(self, owner, value, first_column):
            width = self.columns // self.parts
            position = sum(
                ((owner >> k) & 1) << (z.bits - 1 - j) for j, k in enumerate(z.seq_bits(self.name)))
            below = n >> (z.halving(self.name) or 0)
            above, rest = position // below, position % below
            for part in range(self.parts):
                start = self.offset + part * width
                low, high = max(first_column, start), min(first_column + value.shape[1], start + width)
                if low < high:
                    where = (above * self.parts + part) * below + rest
                    self.a[where, :, low - start:high - start] = (
                        value[:, low - first_column:high - first_column])

    sums = {name: Sum(name, j) for j, name in enumerate(z.sums)}

    def put_rows(target, value, first_column=0, first_owner=0):
        value = value.astype(BF)
        for name, (share, _, _, output, _) in z.sums.items():
            if output == target:
                for j in range(value.shape[0] // share):
                    sums[name].put(first_owner + j, value[j * share:(j + 1) * share], first_column)

    def over_rows(count, size, step):
        def one(j, carry):
            step(pl.ds(pl.multiple_of(j * size, size), size))
            return carry
        lax.fori_loop(0, count // size, one, 0)

    def mean(value):
        return jnp.sum(value, -1, keepdims=True) * (1.0 / d)

    def norm_forward(total):
        centred = total - mean(total)
        inverse = lax.rsqrt(mean(centred * centred) + EPSILON)
        return centred * inverse, inverse

    def norm_backward(grad, normed, inverse, gain_row, which):
        scaled = grad * gain_row
        result = inverse * (scaled - mean(scaled) - normed * mean(scaled * normed))
        g.sm[which:which + 1, :] += jnp.sum(grad * normed, 0, keepdims=True)
        g.sm[3 + which:4 + which, :] += jnp.sum(grad, 0, keepdims=True)
        return result

    lane = lax.broadcasted_iota(I32, (t, half), 1)

    def only(value, which):
        keep = (lane < hd) if which == 0 else (lane >= hd)
        return jnp.where(keep, value, jnp.zeros_like(value))

    def both(first, second):
        return jnp.where(lane < hd, first, second)

    def pair_cols(p, offset=0):
        return slice(offset + p * half, offset + (p + 1) * half)

    def keep_lse(index, value):
        g.lse[:, index:index + 1] = value

    def kept_lse(index):
        return g.lse[:, index:index + 1]

    SELF_PACKED, CROSS_PACKED, CROSS_DOC, SELF_DOC = (k * HEADS for k in range(4))

    tokens_all = Chain(g.xg, g.xgs, g.xgr)
    memory_all = Chain(g.mg, g.mgs, g.mgr)
    place = place_of(s)
    other_seg = g.seg_in[1:2, :]
    swap = jnp.min(other_seg, -1, keepdims=True) == jnp.max(other_seg, -1, keepdims=True)

    def ordered(ref, into):
        first, second, count = ref[:, 0, :], ref[:, 1, :], ref.shape[0]
        into[0:count, :] = jnp.where(swap, second, first)
        into[count:, :] = jnp.where(swap, first, second)

    def restored(first, second, ref):
        ref[:, 0, :] = jnp.where(swap, second, first)
        ref[:, 1, :] = jnp.where(swap, first, second)

    ordered(g.x_in, g.x)
    loads["sp"].wait()
    for name in ("cm", "so", "cq", "co", "fi", "fo"):
        loads[name].start()

    for part in range(3):
        made = nn(g.x[0:t, :], g.w_sp[:, part * d:(part + 1) * d]).astype(BF)
        g.qkvt[:, part * hd:(part + 1) * hd, :] = made.T.reshape(HEADS, hd, t)
    pl.semaphore_wait(barrier, n - 1 + z.row_bits)
    for h in range(HEADS):
        Spread(g.qkvt.at[h, pl.ds(hd, 2 * hd)], g.kv.at[my_part, own_turn], g.kv_s, g.kv_r,
               h * split + my_part).start()
    for h in range(HEADS):
        Spread(g.qkvt.at[h, pl.ds(0, hd)], g.qt.at[own_turn], g.q_s, g.q_r, h * split + own_part).start()
    ordered(g.mem_in, g.mem)
    seg = jnp.where(swap, g.seg_in[0:1, :], other_seg)
    pad = jnp.where(swap, g.pad_in[0:1, :], g.pad_in[1:2, :])
    q_at = lax.broadcasted_iota(I32, (t, t), 0)
    k_at = lax.broadcasted_iota(I32, (t, t), 1)
    seg_q = jnp.sum(jnp.where(q_at == k_at, seg.astype(F32), 0.0), -1, keepdims=True).astype(I32)
    pick = (q_at == 2 * lax.rem(k_at + z.mhalo, mt)).astype(F32)
    mem_seg = jnp.dot(
        jnp.broadcast_to(seg.astype(F32), (8, t)), pick,
        precision=lax.Precision.HIGHEST, preferred_element_type=F32).astype(I32)
    g.codes[0:1, :] = seg
    g.codes[1:2, :] = pad
    g.codes[2:3, :] = pltpu.roll(seg, z.halo, 1)
    g.codes[3:4, :] = pltpu.roll(pad, z.halo, 1)
    g.codes[4:8, :] = mem_seg[0:4]
    g.xg[place] = g.x[0:t, :]
    g.mg[place] = g.mem[0:mt, :]
    g.xw[0:t, :] = g.x[t:, :]
    g.mw[z.mhalo:z.mhalo + mt, :] = g.mem[mt:, :]
    halo_copies = [
        remote(g.codes, g.cn, g.hs.at[0], g.hr.at[0], (prv, r)),
        remote(g.codes, g.cp, g.hs.at[1], g.hr.at[1], (nxt, r)),
        remote(g.x.at[pl.ds(2 * t - z.halo, z.halo)], g.xw.at[pl.ds(t, z.halo)],
               g.hs.at[2], g.hr.at[2], (nxt, r)),
        remote(g.mem.at[pl.ds(mt, z.mhalo)], g.mw.at[pl.ds(z.mhalo + mt, z.mhalo)],
               g.hs.at[3], g.hr.at[3], (prv, r)),
        remote(g.mem.at[pl.ds(2 * mt - z.mhalo, z.mhalo)], g.mw.at[pl.ds(0, z.mhalo)],
               g.hs.at[4], g.hr.at[4], (nxt, r)),
    ]
    for copy in halo_copies:
        copy.start()

    memory_all.start()

    g.qp[...] = nn(g.xw[0:t, :], g.w_sp[:, :d]).astype(BF)
    ordered(g.cot_in, g.cot)
    g.sm[...] = jnp.zeros_like(g.sm)

    def self_mask():
        seg_k, pad_k = g.codes[0:1, :], g.codes[1:2, :]
        own = (seg_q == seg_k) & (k_at <= q_at) & ((pad_k == 1) | (k_at == q_at))
        prev = (seg_q == g.cp[2:3, :]) & (g.cp[3:4, :] == 1)
        return own, prev[:, :z.halo]

    def cross_mask():
        at = lax.broadcasted_iota(I32, (1, 2 * mt), 1)
        seg_k = jnp.where(
            at < z.mhalo, g.cp[4:5, :],
            jnp.where(at < z.mhalo + mt, g.codes[4:5, :], g.cn[4:5, :]))
        return seg_q == seg_k

    def softmax_parts(scores):
        top = functools.reduce(jnp.maximum, [jnp.max(b, -1, keepdims=True) for b in scores])
        weights = [jnp.exp(b - top) for b in scores]
        total = functools.reduce(jnp.add, [jnp.sum(w, -1, keepdims=True) for w in weights])
        return weights, total, top + jnp.log(total)

    def hand_over(f):
        return remote(g.kv.at[my_part], g.kv.at[my_part], g.kw_s.at[f], g.kw_r.at[my_part],
                      (my_head * split + f, r))

    wait_whole(g.kv.at[my_part], g.kv_r)
    for f in range(split):
        @pl.when(my_part != f)
        def _():
            hand_over(f).start()
    wait_whole(g.qt, g.q_r)
    for f in range(split):
        @pl.when(my_part != f)
        def _():
            wait_whole(g.kv.at[f], g.kw_r.at[f])
    for b in range(n):
        g.kts[:, b * t:(b + 1) * t] = g.kv[b % split, b // split, 0:hd]
        g.vts[:, b * t:(b + 1) * t] = g.kv[b % split, b // split, hd:]

    wide = split * t
    diag_q = lax.broadcasted_iota(I32, (t, wide), 0)
    diag_k = lax.broadcasted_iota(I32, (t, wide), 1)

    def turn_rest(i):
        return my_part if i % 2 == 0 else split - 1 - my_part

    def diag_mask(i):
        return diag_k <= diag_q + turn_rest(i) * t

    def attend_document(i):
        q = g.qt[i].T
        low = i * wide
        blocks = []
        if low:
            blocks.append(nn(q, g.kts[:, :low]) * softmax_scale)
        blocks.append(jnp.where(
            diag_mask(i), nn(q, g.kts[:, low:low + wide]) * softmax_scale, NEGATIVE))
        weights, total, lse = softmax_parts(blocks)
        keep_lse(SELF_DOC + i, lse)
        o = nt(weights[-1].astype(BF), g.vts[:, low:low + wide])
        if low:
            o = o + nt(weights[0].astype(BF), g.vts[:, :low])
        o = o / total
        g.of[i] = o
        g.ots[i] = o.T.astype(BF)

    for turns in ((0, 1, 2, 3, 4), (5, 6, 7)):
        for i in turns:
            attend_document(i)
        for i in turns:
            Spread(g.ots.at[i], g.otr.at[my_head], g.o_s, g.o_r, i * split + turn_rest(i)).start()
        if turns[0] == 0:
            memory_all.step(0)
    memory_all.cross_step(0)

    for copy in halo_copies:
        copy.wait()
    g.ps[...] = nn(g.xw[...], g.w_sp[:, d:]).astype(BF)
    loads["cm"].wait()
    g.pm[...] = nn(g.mw[...], g.w_cm[...]).astype(BF)
    for j in range(1, n // 4 - 2):
        memory_all.step(j)

    own_mask, prev_mask = self_mask()
    for p in range(pairs):
        q, k, v = g.qp[:, pair_cols(p)], g.ps[:, pair_cols(p)], g.ps[:, pair_cols(p, d)]
        outs = []
        for w in range(2):
            sc = nt(only(q, w), k) * softmax_scale
            blocks = [jnp.where(own_mask, sc[:, :t], NEGATIVE), jnp.where(prev_mask, sc[:, t:], NEGATIVE)]
            weights, total, lse = softmax_parts(blocks)
            keep_lse(SELF_PACKED + 2 * p + w, lse)
            o = nn(weights[0].astype(BF), v[:t]) + nn(weights[1].astype(BF), v[t:])
            outs.append(o / total)
        o = both(*outs)
        g.op[:, pair_cols(p)] = o
        g.att[t:, pair_cols(p)] = o.astype(BF)

    for j in range(1, n // 4 - 2):
        memory_all.cross_step(j)
    memory_all.step(n // 4 - 2)

    loads["so"].wait()
    wait_whole(g.otr, g.o_r)
    g.att[0:t, :] = g.otr[...].reshape(d, t).T
    g.tmp[...] = nn(g.att[...], g.w_so[...])

    def first_norm(rows):
        total = g.x[rows, :].astype(F32) * g.scale[0:1, :] + g.tmp[rows, :]
        normed, inverse = norm_forward(total)
        g.n1[rows, :] = normed
        g.i1[rows, :] = inverse
        g.h1b[rows, :] = (normed * g.gain[0:1, :] + g.bias[0:1, :]).astype(BF)

    over_rows(2 * t, 128, first_norm)
    memory_all.cross_step(n // 4 - 2)
    tokens_all.start()
    loads["cq"].wait()
    g.cqv[...] = nn(g.h1b[...], g.w_cq[...]).astype(BF)

    seen = cross_mask()
    for p in range(pairs):
        q, k, v = g.cqv[t:, pair_cols(p)], g.pm[:, pair_cols(p)], g.pm[:, pair_cols(p, d)]
        outs = []
        for w in range(2):
            sc = jnp.where(seen, nt(only(q, w), k) * softmax_scale, NEGATIVE)
            (weights,), total, lse = softmax_parts([sc])
            keep_lse(CROSS_PACKED + 2 * p + w, lse)
            outs.append(nn(weights.astype(BF), v) / total)
        o = both(*outs)
        g.co32[t:, pair_cols(p)] = o
        g.catt[t:, pair_cols(p)] = o.astype(BF)
    memory_all.cross_step(n // 4 - 1)
    memory_all.finish()

    for part in range(2):
        cols = slice(part * d, (part + 1) * d)
        g.mkv[:, :, cols] = nn(g.mg[...].reshape(n * mt, d), g.w_cm[:, cols]).astype(BF).reshape(n, mt, d)

    tokens_all.step(0)
    tokens_all.cross_step(0)

    for p in range(pairs):
        q = g.cqv[0:t, pair_cols(p)]
        k = g.mkv[:, :, pair_cols(p)].reshape(n * mt, half)
        v = g.mkv[:, :, pair_cols(p, d)].reshape(n * mt, half)
        outs = []
        for w in range(2):
            sc = nt(only(q, w), k) * softmax_scale
            (weights,), total, lse = softmax_parts([sc])
            keep_lse(CROSS_DOC + 2 * p + w, lse)
            outs.append(nn(weights.astype(BF), v) / total)
        o = both(*outs)
        g.co32[0:t, pair_cols(p)] = o
        g.catt[0:t, pair_cols(p)] = o.astype(BF)
    stays = own_part == my_part
    wait_whole(g.kvfin.at[pl.ds(0, HEADS - 1)], g.kv_s)
    wait_sent(g.qt, g.q_s, stays)
    wait_sent(g.ots, g.o_s, stays)
    for f in range(split):
        @pl.when(my_part != f)
        def _():
            hand_over(f).wait_send()
    memory_all.drain()

    tokens_all.step(1)

    loads["co"].wait()
    g.tmp[...] = nn(g.catt[...], g.w_co[...])

    def second_norm(rows):
        hidden1 = g.n1[rows, :] * g.gain[0:1, :] + g.bias[0:1, :]
        normed, inverse = norm_forward(hidden1 * g.scale[1:2, :] + g.tmp[rows, :])
        g.n2[rows, :] = normed
        g.i2[rows, :] = inverse
        g.h2b[rows, :] = (normed * g.gain[1:2, :] + g.bias[1:2, :]).astype(BF)

    over_rows(2 * t, 128, second_norm)

    tokens_all.cross_step(1)
    loads["fi"].wait()
    chunks = ff // d
    for c in range(chunks):
        cols = slice(c * d, (c + 1) * d)
        pre = nn(g.h2b[...], g.w_fi[:, cols]) + g.fi_b[0:1, cols]
        square = pre * pre
        bent = jnp.tanh(GELU_A * pre * (1.0 + GELU_B * square))
        g.act[:, cols] = (0.5 * pre * (1.0 + bent)).astype(BF)
        g.dg[:, cols] = 0.5 * (1.0 + bent) + 0.5 * pre * (1.0 - bent * bent) * (
            GELU_A * (1.0 + 3.0 * GELU_B * square))
    tokens_all.step(2)
    loads["fo"].wait()
    g.tmp[...] = nn(g.act[...], g.w_fo[...])

    def third_norm(rows):
        hidden2 = g.n2[rows, :] * g.gain[1:2, :] + g.bias[1:2, :]
        total = hidden2 * g.scale[2:3, :] + (g.tmp[rows, :] + g.fo_b[0:1, :])
        normed, inverse = norm_forward(total)
        grad = g.cot[rows, :].astype(F32)
        g.cot[rows, :] = (normed * g.gain[2:3, :] + g.bias[2:3, :]).astype(BF)
        back = norm_backward(grad, normed, inverse, g.gain[2:3, :], 2)
        g.sm[8:9, :] += jnp.sum(back * hidden2, 0, keepdims=True)
        g.dx[rows, :] = back
        low = back.astype(BF)
        g.dtb[rows, :] = low
        g.sm[9:10, :] += jnp.sum(low.astype(F32), 0, keepdims=True)

    over_rows(2 * t, 128, third_norm)
    tokens_all.cross_step(2)

    for j in range(3, n // 4 - 1):
        tokens_all.step(j)
        tokens_all.cross_step(j)

    def feed_out_grads():
        for c in range(chunks):
            cols = slice(c * d, (c + 1) * d)
            put_rows("fo", nn(g.act[:, cols].T, g.dtb[...]), 0, c * d // z.sums["fo0"][0])

    def before_gelu():
        for c in range(chunks):
            cols = slice(c * d, (c + 1) * d)
            back = (nt(g.dtb[...], g.w_fo[cols, :]) * g.dg[:, cols]).astype(BF)
            g.act[:, cols] = back
            g.sm[10 + c:11 + c, :] = jnp.sum(back.astype(F32), 0, keepdims=True)

    def feed_in_grads():
        h2t = g.h2b[...].T
        for c in range(chunks):
            cols = slice(c * d, (c + 1) * d)
            put_rows("fi", nn(h2t, g.act[:, cols]), c * d)

    def second_norm_back():
        g.tmp[...] = nt(g.act[...], g.w_fi[...])

        def second_back(rows):
            grad = g.dx[rows, :] * g.scale[2:3, :] + g.tmp[rows, :]
            back = norm_backward(grad, g.n2[rows, :], g.i2[rows, :], g.gain[1:2, :], 1)
            hidden1 = g.n1[rows, :] * g.gain[0:1, :] + g.bias[0:1, :]
            g.sm[7:8, :] += jnp.sum(back * hidden1, 0, keepdims=True)
            g.dx[rows, :] = back
            g.dtb[rows, :] = back.astype(BF)

        over_rows(2 * t, 128, second_back)

    def cross_output_back():
        g.dc[...] = nt(g.dtb[...], g.w_co[...]).astype(BF)

    def cross_output_grads():
        put_rows("co", nn(g.catt[...].T, g.dtb[...]))

    def result_out():
        restored(g.cot[0:t, :], g.cot[t:, :], g.o_out)
        pltpu.make_async_copy(g.o_out, g.out, g.outs.at[len(z.sums)]).start()

    def cross_document(p):
        q, go, o = g.cqv[0:t, pair_cols(p)], g.dc[0:t, pair_cols(p)], g.co32[0:t, pair_cols(p)]
        qt, gt = q.T, go.T
        k = g.mkv[:, :, pair_cols(p)].reshape(n * mt, half)
        v = g.mkv[:, :, pair_cols(p, d)].reshape(n * mt, half)
        dqs, dks, dvs = [], [], []
        for w in range(2):
            qm, gm = only(q, w), only(go, w)
            weights = jnp.exp(nt(qm, k) * softmax_scale - kept_lse(CROSS_DOC + 2 * p + w))
            delta = jnp.sum(gm.astype(F32) * o, -1, keepdims=True)
            ds = (weights * (nt(gm, v) - delta)).astype(BF)
            dqs.append(nn(ds, k))
            dks.append(nn(qt[w * hd:(w + 1) * hd], ds))
            dvs.append(nn(gt[w * hd:(w + 1) * hd], weights.astype(BF)))
        g.dcq[0:t, pair_cols(p)] = (both(*dqs) * softmax_scale).astype(BF)
        dk = (jnp.concatenate(dks, 0) * softmax_scale).astype(BF).T
        dv = jnp.concatenate(dvs, 0).astype(BF).T
        g.mkv[:, :, pair_cols(p)] = dk.reshape(n, mt, half)
        g.mkv[:, :, pair_cols(p, d)] = dv.reshape(n, mt, half)

    def cross_packed():
        for p in range(pairs):
            q, k, v = g.cqv[t:, pair_cols(p)], g.pm[:, pair_cols(p)], g.pm[:, pair_cols(p, d)]
            go, o = g.dc[t:, pair_cols(p)], g.co32[t:, pair_cols(p)]
            dqs, dk, dv = [], 0.0, 0.0
            for w in range(2):
                qm, gm = only(q, w), only(go, w)
                weights = jnp.where(
                    seen, jnp.exp(nt(qm, k) * softmax_scale - kept_lse(CROSS_PACKED + 2 * p + w)), 0.0)
                delta = jnp.sum(gm.astype(F32) * o, -1, keepdims=True)
                ds = (weights * (nt(gm, v) - delta)).astype(BF)
                dqs.append(nn(ds, k))
                dk = dk + tn(ds, qm)
                dv = dv + tn(weights.astype(BF), gm)
            g.dcq[t:, pair_cols(p)] = (both(*dqs) * softmax_scale).astype(BF)
            g.pm[:, pair_cols(p)] = (dk * softmax_scale).astype(BF)
            g.pm[:, pair_cols(p, d)] = dv.astype(BF)

    late = {}

    def first_norm_back():
        g.tmp[...] = nt(g.dcq[...], g.w_cq[...])

        def first_back(rows):
            grad = g.dx[rows, :] * g.scale[1:2, :] + g.tmp[rows, :]
            back = norm_backward(grad, g.n1[rows, :], g.i1[rows, :], g.gain[0:1, :], 0)
            g.sm[6:7, :] += jnp.sum(back * g.x[rows, :].astype(F32), 0, keepdims=True)
            g.dx[rows, :] = back
            g.dtb[rows, :] = back.astype(BF)

        over_rows(2 * t, 128, first_back)
        d_self = nt(g.dtb[...], g.w_so[...]).astype(BF)
        g.dself[...] = d_self[t:]
        g.dos[...] = d_self[:t].T.reshape(HEADS, hd, t)
        for h in range(HEADS):
            Spread(g.dos.at[h], g.dor.at[own_turn], g.do_s, g.do_r, h * split + own_part).start()

    def small_sums():
        share, bias_share = d // n, ff // n
        for o in range(n):
            first, bias_first = o * share, o * bias_share
            row = 10 + bias_first // d
            tile = g.sm[:, first // 128 * 128:first // 128 * 128 + 128]
            if first % 128:
                tile = pltpu.roll(tile, 128 - first % 128, 1)
            bias = g.sm[row:row + 1, bias_first % d // 128 * 128:bias_first % d // 128 * 128 + 128]
            if bias_first % 128:
                bias = pltpu.roll(bias, 128 - bias_first % 128, 1)
            sums["sm"].put(o, jnp.concatenate([tile[0:10], bias, tile[11:16]], 0), 0)

    def cross_memory_grads():
        mem_t = g.mg[...].reshape(n * mt, d).T
        win_t = g.mw[...].T
        for part in range(2):
            cols = slice(part * d, (part + 1) * d)
            doc_kv = g.mkv[:, :, cols].reshape(n * mt, d)
            put_rows("cm", nn(mem_t, doc_kv) + nn(win_t, g.pm[:, cols]), part * d)

    def memory_back():
        g.mg[...] = nt(g.mkv[...].reshape(n * mt, 2 * d), g.w_cm[...]).astype(BF).reshape(n, mt, d)

    def memory_halo():
        g.dmp[...] = nt(g.pm[...], g.w_cm[...])
        g.hms[0:z.mhalo, :] = g.dmp[0:z.mhalo, :].astype(BF)
        g.hms[z.mhalo:, :] = g.dmp[z.mhalo + mt:, :].astype(BF)
        late["memory"] = [
            remote(g.hms.at[pl.ds(0, z.mhalo)], g.hmr.at[pl.ds(z.mhalo, z.mhalo)],
                   g.hs.at[5], g.hr.at[5], (prv, r)),
            remote(g.hms.at[pl.ds(z.mhalo, z.mhalo)], g.hmr.at[pl.ds(0, z.mhalo)],
                   g.hs.at[6], g.hr.at[6], (nxt, r)),
        ]
        for copy in late["memory"]:
            copy.start()

    def cross_query_grads():
        put_rows("cq", nn(g.h1b[...].T, g.dcq[...]))

    def self_output_grads():
        put_rows("so", nn(g.att[...].T, g.dtb[...]))

    def self_packed():
        for p in range(pairs):
            q, k, v = g.qp[:, pair_cols(p)], g.ps[:, pair_cols(p)], g.ps[:, pair_cols(p, d)]
            go, o = g.dself[:, pair_cols(p)], g.op[:, pair_cols(p)]
            dqs, dk, dv = [], 0.0, 0.0
            for w in range(2):
                qm, gm = only(q, w), only(go, w)
                sc = nt(qm, k) * softmax_scale - kept_lse(SELF_PACKED + 2 * p + w)
                weights = jnp.concatenate(
                    [jnp.where(own_mask, jnp.exp(sc[:, :t]), 0.0),
                     jnp.where(prev_mask, jnp.exp(sc[:, t:]), 0.0)], 1)
                delta = jnp.sum(gm.astype(F32) * o, -1, keepdims=True)
                ds = (weights * (nt(gm, v) - delta)).astype(BF)
                dqs.append(nn(ds, k))
                dk = dk + tn(ds, qm)
                dv = dv + tn(weights.astype(BF), gm)
            g.qp[:, pair_cols(p)] = (both(*dqs) * softmax_scale).astype(BF)
            g.ps[:, pair_cols(p)] = (dk * softmax_scale).astype(BF)
            g.ps[:, pair_cols(p, d)] = dv.astype(BF)

    def self_project_grads():
        window_t = g.xw[...].T
        put_rows("sp", nn(window_t[:, :t], g.qp[...]), 0)
        put_rows("sp", nn(window_t, g.ps[:, :d]), d)
        put_rows("sp", nn(window_t, g.ps[:, d:]), 2 * d)

    def tokens_halo():
        g.dxp[...] = nt(g.ps[...], g.w_sp[:, d:])
        g.hss[...] = g.dxp[t:, :].astype(BF)
        late["tokens"] = remote(g.hss, g.hsr, g.hs.at[7], g.hr.at[7], (prv, r))
        late["tokens"].start()
        g.tmp[t:, :] = nt(g.qp[...], g.w_sp[:, :d]) + g.dxp[0:t, :]

    chunk = min(512, n * t)

    def kept(which, first, last):
        row, column = first // ff * 2 * hd + which * hd, first % ff
        return slice(row, row + hd), slice(column, column + last - first)

    def sibling(i, f):
        return remote(
            g.kvst.at[i, f], g.kvsib.at[i, my_part], g.sib_s,
            g.sib_r.at[i, lax.rem(my_part - f + split, split) - 1], (my_head * split + f, r))

    def to_siblings(action):
        for f in range(split):
            @pl.when(my_part != f)
            def _():
                action(f)

    def close_kv(i):
        g.kvfin[i] = g.kvst[i, my_part]

        def add(f):
            wait_whole(g.kvsib.at[i, f], g.sib_r.at[i, lax.rem(f - my_part + split, split) - 1])
            g.kvfin[i] = g.kvfin[i] + g.kvsib[i, f]

        to_siblings(add)
        Spread(g.kvfin.at[i], g.dkvr.at[my_head], g.kf_s, g.kf_r, i * split + my_part).start()

    def attend_document_back(i):
        b = i * split + turn_rest(i)
        qt, gt = g.qt[i], g.dor[i]
        q, go = qt.T, gt.T
        delta = jnp.sum(go.astype(F32) * g.of[i], -1, keepdims=True)
        lse = kept_lse(SELF_DOC + i)
        low = i * wide
        spans = [(a, min(a + chunk, low), False) for a in range(0, low, chunk)]
        spans.append((low, low + wide, True))
        dq = 0.0
        for first, last, masked in spans:
            k, v = g.kts[:, first:last], g.vts[:, first:last]
            weights = jnp.exp(nn(q, k) * softmax_scale - lse)
            if masked:
                weights = jnp.where(diag_mask(i), weights, 0.0)
            ds = (weights * (nn(go, v) - delta)).astype(BF)
            dq = dq + nt(ds, k)
            g.dg[kept(0, first, last)] += nn(qt, ds)
            g.dg[kept(1, first, last)] += nn(gt, weights.astype(BF))
        dqt = (dq * softmax_scale).T.astype(BF)
        g.ots[i] = dqt
        for f in range(split):
            first = (i * split + f) * t
            g.kvst[i, f, 0:hd] = (g.dg[kept(0, first, first + t)] * softmax_scale).astype(BF)
            g.kvst[i, f, hd:] = g.dg[kept(1, first, first + t)].astype(BF)
        g.dwt[0:hd, :] += nn(dqt, g.xg[place_of(b)])
        for f in range(split):
            g.dwt[hd:, :] += nn(g.kvst[i, f], g.xg[reverse_static(i * split + f, z.bits)])

    def self_document(turns):
        if turns[0] == HEADS - 1:
            tokens_all.finish()
            tokens_all.drain()
            wait_whole(g.dor, g.do_r)
            g.dg[...] = jnp.zeros_like(g.dg)
            g.dwt[...] = jnp.zeros_like(g.dwt)
        for i in turns:
            attend_document_back(i)
        for i in turns:
            Spread(g.ots.at[i], g.dqr.at[my_head], g.dq_s, g.dq_r, i * split + turn_rest(i)).start()
            to_siblings(lambda f: sibling(i, f).start())
        for i in late.get("turns", ()):
            close_kv(i)
        late["turns"] = turns

    def head_parts(f):
        return remote(g.dws.at[f], g.dwsib.at[my_part], g.ds_s.at[f], g.ds_r.at[my_part],
                      (my_head * split + f, r))

    def head_grads():
        whole = jnp.concatenate([g.dwt[...], jnp.zeros((hd, d), F32)], 0).T.astype(BF)
        share = d // n
        for o in range(n):
            g.dws[o % split, o // split] = whole[o * share:(o + 1) * share]
        to_siblings(lambda f: head_parts(f).start())

    def head_owners():
        for i in late["turns"]:
            close_kv(i)

        def add(f):
            wait_whole(g.dwsib.at[f], g.ds_r.at[f])
            g.dws[my_part] = g.dws[my_part] + g.dwsib[f]

        to_siblings(add)
        for j in range(HEADS):
            Spread(g.dws.at[my_part, j], g.dwr.at[my_head], g.dw_s, g.dw_r, j * split + my_part).start()

    def tokens_back():
        wait_whole(g.dqr, g.dq_r)
        g.dproj[:, 0:d] = g.dqr[...].reshape(d, t).T
        wait_whole(g.dkvr, g.kf_r)
        for part in range(2):
            g.dproj[:, (part + 1) * d:(part + 2) * d] = (
                g.dkvr[:, part * hd:(part + 1) * hd, :].reshape(d, t).T)
        g.tmp[0:t, :] = nt(g.dproj[...], g.w_sp[...])
        late["tokens"].wait()
        g.tmp[2 * t - z.halo:, :] += g.hsr[...].astype(F32)

        def last(rows):
            g.dx[rows, :] = g.dx[rows, :] * g.scale[0:1, :] + g.tmp[rows, :]

        over_rows(2 * t, 128, last)
        restored(g.dx[0:t, :], g.dx[t:, :], g.o_dx)
        pltpu.make_async_copy(g.o_dx, g.dx_out, g.outs.at[len(z.sums) + 1]).start()

    def shares(k):
        return remote(g.dsh, g.dshr.at[k], g.dy_s.at[k], g.dy_r.at[k], (s, row_partner(k)))

    def head_shares():
        wait_whole(g.dwr, g.dw_r)
        for p in range(pairs):
            left, right = g.dwr[2 * p], g.dwr[2 * p + 1]
            for part in range(3):
                cols = slice(part * hd, (part + 1) * hd)
                g.dsh[:, pair_cols(p, part * d)] = jnp.concatenate([left[:, cols], right[:, cols]], 1)
        shares(0).start()

    pieces = dict(
        fo_mm=feed_out_grads, dpre=before_gelu, fi_mm=feed_in_grads, sb=second_norm_back,
        dc=cross_output_back, co_mm=cross_output_grads, out=result_out, xp=cross_packed,
        fb=first_norm_back, cmm=cross_memory_grads, mkm=memory_back, dmp=memory_halo,
        cqm=cross_query_grads, smm=small_sums, som=self_output_grads, psb=self_packed, spm=self_project_grads,
        dxp=tokens_halo, dwm=head_grads, dwo=head_owners, fin1=tokens_back, fin2=head_shares,
        xg3=lambda: tokens_all.cross_step(n // 4 - 1),
    )
    for p in range(pairs):
        pieces["xd%d" % p] = functools.partial(cross_document, p)
    for i in range(1, HEADS, 2):
        pieces["sd%d" % i] = functools.partial(self_document, (i, i - 1))
    for name in ORDER:
        if name in pieces:
            pieces[name]()
        else:
            sums[name].advance()

    for k in range(z.row_bits - 1):
        shares(k).wait()
        g.dsh[...] = g.dsh[...] + g.dshr[k]
        shares(k + 1).start()
    while not all(one.over() for one in sums.values()):
        for one in sums.values():
            one.advance()
    for copy in late["memory"]:
        copy.wait()
    restored(sums["mk"].result().astype(F32),
             g.dmp[z.mhalo:z.mhalo + mt, :] + g.hmr[...].astype(F32), g.o_dm)
    pltpu.make_async_copy(g.o_dm, g.dm_out, g.outs.at[len(z.sums) + 2]).start()
    small = g.o_sm[...]
    g.o_bgain[...] = small[0:3, :d // n]
    g.o_bbias[...] = small[3:6, :d // n]
    g.o_bscale[...] = small[6:9, :d // n]
    g.o_bfo[...] = small[9:10, :d // n]
    g.o_bfi[...] = small[10:11, :ff // n]
    small_copies = [
        pltpu.make_async_copy(src, dst, g.outs.at[len(z.sums) + 3 + j])
        for j, (src, dst) in enumerate((
            (g.o_bgain, g.b_gain), (g.o_bbias, g.b_bias), (g.o_bscale, g.b_scale),
            (g.o_bfo, g.b_fo), (g.o_bfi, g.b_fi)))
    ]
    for copy in small_copies:
        copy.start()
    shares(z.row_bits - 1).wait()
    g.o_sp[...] = g.o_sp[...] + (g.dsh[...].astype(F32) + g.dshr[z.row_bits - 1].astype(F32))
    sums["sp"].output().start()
    wait_sent(g.dos, g.do_s, stays)
    wait_sent(g.ots, g.dq_s, stays)
    wait_whole(g.kvfin.at[pl.ds(0, HEADS - 1)], g.kf_s)
    wait_whole(g.dws.at[0, pl.ds(0, HEADS - 1)], g.dw_s)
    wait_whole(g.kvst.at[:, pl.ds(0, split - 1)], g.sib_s)
    to_siblings(lambda f: head_parts(f).wait_send())

    for copy in small_copies:
        copy.wait()
    for one in sums.values():
        if one.out is not None and one.name != "sm":
            one.output().wait()
    for j, (src, dst) in enumerate(((g.o_out, g.out), (g.o_dx, g.dx_out), (g.o_dm, g.dm_out))):
        pltpu.make_async_copy(src, dst, g.outs.at[len(z.sums) + j]).wait()


def on_device(
    mesh_shape,
    tokens, memory, segments, padding, cotangent,
    self_project, self_output, cross_query, cross_memory, cross_output,
    feed_in, feed_in_bias, feed_out, feed_out_bias, norm_gain, norm_bias, residual_scale,
):
    t, _, d = tokens.shape
    mt = memory.shape[0]
    ff = feed_in.shape[1]
    n, rows = mesh_shape
    z = Sizes(n, rows, t, mt, d, ff)

    scratch = z.scratch()
    names = INPUTS + OUTPUTS + tuple(scratch)
    vmem, anywhere = pl.BlockSpec(memory_space=pltpu.VMEM), pl.BlockSpec(memory_space=pl.ANY)
    shapes = [
        jax.ShapeDtypeStruct((t, 2, d), BF),
        jax.ShapeDtypeStruct((t, 2, d), F32),
        jax.ShapeDtypeStruct((mt, 2, d), F32),
    ] + [
        jax.ShapeDtypeStruct(shape, F32)
        for shape in (
            (d // n, 3 * d), (d // n, d), (d // n, d), (d // n, 2 * d), (d // n, d), (d // n, ff), (ff // n, d))
    ] + [
        jax.ShapeDtypeStruct((1, ff // n), F32), jax.ShapeDtypeStruct((1, d // n), F32),
    ] + [jax.ShapeDtypeStruct((3, d // n), F32)] * 3
    outcome = pl.pallas_call(
        functools.partial(layer_kernel, z, names),
        out_shape=shapes,
        in_specs=[vmem] * 5 + [anywhere] * 7 + [vmem] * 5,
        out_specs=[anywhere] * len(OUTPUTS),
        scratch_shapes=list(scratch.values()),
        compiler_params=pltpu.CompilerParams(
            collective_id=0, has_side_effects=True, vmem_limit_bytes=63 * 2 ** 20),
        name="layer",
    )(
        tokens, memory, cotangent, segments, padding,
        self_project, self_output, cross_query, cross_memory, cross_output, feed_in, feed_out,
        feed_in_bias.reshape(1, ff), feed_out_bias.reshape(1, d), norm_gain, norm_bias, residual_scale,
    )

    def hand_on(*refs):
        count = len(shapes)
        sources, results, held, sems = refs[:count], refs[count:2 * count], refs[2 * count:-1], refs[-1]
        into = [pltpu.make_async_copy(a, b, sems.at[0, j]) for j, (a, b) in enumerate(zip(sources, held))]
        out = [pltpu.make_async_copy(a, b, sems.at[1, j]) for j, (a, b) in enumerate(zip(held, results))]
        for copy in into:
            copy.start()
        for one, two in zip(into, out):
            one.wait()
            two.start()
        for copy in out:
            copy.wait()

    outcome = pl.pallas_call(
        hand_on,
        out_shape=shapes,
        in_specs=[anywhere] * len(shapes),
        out_specs=[anywhere] * len(shapes),
        scratch_shapes=[pltpu.VMEM(one.shape, one.dtype) for one in shapes] + [
            pltpu.SemaphoreType.DMA((2, len(shapes)))],
        name="results",
    )(*outcome)
    (out, dx, dm, g_sp, g_so, g_cq, g_cm, g_co, g_fi, g_fo,
     in_bias, out_bias, gain, bias, scale) = outcome
    return (
        out, dx, dm, g_sp, g_so, g_cq, g_cm, g_co, g_fi, in_bias.reshape(ff // n),
        g_fo, out_bias.reshape(d // n), gain, bias, scale,
    )


def solution(mesh):
    in_specs = (
        P("seq", "rows", None), P("seq", "rows", None), P("rows", "seq"), P("rows", "seq"),
        P("seq", "rows", None),
    ) + (P(),) * 12
    out_specs = (P("seq", "rows", None),) * 3 + (
        P("seq", None), P("seq", None), P("seq", None), P("seq", None), P("seq", None),
        P("seq", None), P("seq"), P("seq", None), P("seq"),
        P(None, "seq"), P(None, "seq"), P(None, "seq"),
    )
    shape = (mesh.shape["seq"], mesh.shape["rows"])
    return jax.shard_map(
        functools.partial(on_device, shape),
        mesh=mesh, in_specs=in_specs, out_specs=out_specs, check_vma=False,
    )
```

```python
import functools
import math

import jax
import jax.numpy as jnp
from jax import lax
from jax.experimental import pallas as pl
from jax.experimental.pallas import tpu as pltpu
from jax.sharding import PartitionSpec as P

HEADS = 8
EPSILON = 1e-05
NEGATIVE = -1e30
BF = jnp.bfloat16
F32 = jnp.float32
I32 = jnp.int32
MESH = pl.DeviceIdType.MESH
GELU_A = math.sqrt(2.0 / math.pi)
GELU_B = 0.044715


def nn(a, b):
    return jnp.dot(a, b, preferred_element_type=F32)


def nt(a, b):
    return lax.dot_general(a, b, (((1,), (1,)), ((), ())), preferred_element_type=F32)


def tn(a, b):
    return lax.dot_general(a, b, (((0,), (0,)), ((), ())), preferred_element_type=F32)


def log2(value):
    return int(value).bit_length() - 1


def reverse_static(index, bits):
    return sum(((index >> k) & 1) << (bits - 1 - k) for k in range(bits))


class Sizes:
    def __init__(self, n, rows, t, mt, d, ff):
        self.n, self.rows, self.t, self.mt, self.d, self.ff = n, rows, t, mt, d, ff
        self.bits, self.row_bits = log2(n), log2(rows)
        self.split = n // HEADS
        self.hd = d // HEADS
        self.halo = t // 2
        self.mhalo = mt // 2
        self.sums = {
            "fo0": (ff // n, d // 2, "far first", "fo", 0),
            "fo1": (ff // n, d // 2, "rows second", "fo", d // 2),
            "fi0": (d // n, ff // 2, "rows third", "fi", 0),
            "fi1": (d // n, ff // 2, "far first", "fi", ff // 2),
            "co": (d // n, d, "rows second", "co", 0),
            "cq": (d // n, d, "rows third", "cq", 0),
            "mk": (mt, d, "seq alone", "mk", 0),
            "cm": (d // n, 2 * d, "rows second", "cm", 0),
            "so": (d // n, d, "rows second", "so", 0),
            "sp": (d // n, 3 * d, "rows second", "sp", 0),
            "sm": (16, 128, "rows last", "sm", 0),
        }
        self.types = {"sm": F32}

    def seq_bits(self, name):
        if self.sums[name][2] == "far first":
            return [0, 2, 1] + list(range(3, self.bits))
        return list(range(self.bits))

    def steps(self, name):
        order = self.sums[name][2]
        seq = [("seq", k) for k in self.seq_bits(name)]
        rows = [("exchange", k) for k in range(self.row_bits)]
        if order == "seq alone":
            return seq
        at = self.halving(name)
        if at is not None:
            return seq[:at] + [("halve", 0)] + seq[at:] + rows[1:] + [("gather", 0)]
        return seq + rows

    def halving(self, name):
        return {"rows second": 1, "rows third": 2}.get(self.sums[name][2])

    def parts(self, name):
        return 1 if self.halving(name) is None else 2

    def received(self, name):
        held, first, spans = self.n * self.parts(name), 0, []
        for kind, _ in self.steps(name):
            held = held // 2 if kind in ("seq", "halve") else held
            spans.append((first, held))
            first += held
        return spans, first

    def scratch(self):
        n, t, mt, d, ff, hd, split = self.n, self.t, self.mt, self.d, self.ff, self.hd, self.split
        v, dma = pltpu.VMEM, pltpu.SemaphoreType.DMA
        spec = dict(
            w_so=v((d, d), BF), w_cq=v((d, d), BF), w_cm=v((d, 2 * d), BF),
            w_co=v((d, d), BF), w_fi=v((d, ff), BF), w_fo=v((ff, d), BF),
            x=v((2 * t, d), BF), mem=v((2 * mt, d), BF), cot=v((2 * t, d), BF),
            dx=v((2 * t, d), F32), codes=v((8, t), I32),
            xg=v((n, t, d), BF), mg=v((n, mt, d), BF), mkv=v((n, mt, 2 * d), BF),
            qkvt=v((HEADS, 3 * hd, t), BF), kv=v((split, HEADS, 2 * hd, t), BF),
            qt=v((HEADS, hd, t), BF), kts=v((hd, n * t), BF), vts=v((hd, n * t), BF),
            ots=v((HEADS, hd, t), BF), otr=v((HEADS, hd, t), BF), of=v((HEADS, t, hd), F32),
            dos=v((HEADS, hd, t), BF), dor=v((HEADS, hd, t), BF), dqr=v((HEADS, hd, t), BF),
            dwt=v((3 * hd, d), F32),
            kvst=v((HEADS, split, 2 * hd, t), BF), kvsib=v((HEADS, split, 2 * hd, t), BF),
            kvfin=v((HEADS, 2 * hd, t), BF), dkvr=v((HEADS, 2 * hd, t), BF),
            dws=v((split, n // split, d // n, 4 * hd), BF), dwsib=v((split, n // split, d // n, 4 * hd), BF),
            dwr=v((HEADS, d // n, 4 * hd), BF),
            dsh=v((d // n, 3 * d), BF), dshr=v((self.row_bits, d // n, 3 * d), BF),
            xw=v((t + self.halo, d), BF), mw=v((2 * mt, d), BF),
            qp=v((t, d), BF), ps=v((t + self.halo, 2 * d), BF), pm=v((2 * mt, 2 * d), BF),
            cp=v((8, t), I32), cn=v((8, t), I32),
            lse=v((t, 4 * HEADS), F32),
            op=v((t, d), F32), co32=v((2 * t, d), F32),
            hss=v((self.halo, d), BF), hsr=v((self.halo, d), BF),
            hms=v((mt, d), BF), hmr=v((mt, d), BF),
            att=v((2 * t, d), BF), catt=v((2 * t, d), BF), cqv=v((2 * t, d), BF),
            tmp=v((2 * t, d), F32), n1=v((2 * t, d), F32), n2=v((2 * t, d), F32),
            i1=v((2 * t, 1), F32), i2=v((2 * t, 1), F32),
            h1b=v((2 * t, d), BF), h2b=v((2 * t, d), BF),
            act=v((2 * t, ff), BF), dg=v((2 * t, ff), F32),
            dtb=v((2 * t, d), BF), dc=v((2 * t, d), BF), dcq=v((2 * t, d), BF),
            dself=v((t, d), BF), dproj=v((t, 3 * d), BF),
            o_out=v((t, 2, d), BF), o_dx=v((t, 2, d), F32), o_dm=v((mt, 2, d), F32),
            o_sp=v((d // n, 3 * d), F32), o_so=v((d // n, d), F32), o_cq=v((d // n, d), F32),
            o_cm=v((d // n, 2 * d), F32), o_co=v((d // n, d), F32),
            o_fi=v((d // n, ff), F32), o_fo=v((ff // n, d), F32),
            sm=v((16, d), F32), o_sm=v((16, 128), F32),
            o_bfi=v((1, ff // n), F32), o_bfo=v((1, d // n), F32),
            o_bgain=v((3, d // n), F32), o_bbias=v((3, d // n), F32), o_bscale=v((3, d // n), F32),
        )
        for name, (r, c, _, _, _) in self.sums.items():
            parts = self.parts(name)
            if name != "mk":
                spec["a_" + name] = v((n * parts, r, c // parts), self.types.get(name, BF))
            spec["r_" + name] = v((self.received(name)[1], r, c // parts), self.types.get(name, BF))
            spec["ss_" + name] = dma
            spec["rs_" + name] = dma((len(self.steps(name)),))
        spec.update(
            wsem=dma((6,)), xgs=dma((4,)), xgr=dma((n,)), mgs=dma((4,)), mgr=dma((n,)),
            hs=dma((8,)), hr=dma((8,)),
            kv_s=dma, kv_r=dma, kw_s=dma((split,)), kw_r=dma((split,)),
            q_s=dma, q_r=dma, o_s=dma, o_r=dma, do_s=dma, do_r=dma,
            dq_s=dma, dq_r=dma, kf_s=dma, kf_r=dma,
            sib_s=dma, sib_r=dma((HEADS, split - 1)),
            ds_s=dma((split,)), ds_r=dma((split,)), dw_s=dma, dw_r=dma,
            outs=dma((len(self.sums) + 8,)), dy_s=dma((self.row_bits,)), dy_r=dma((self.row_bits,)),
        )
        return spec


ORDER = (
    "fo_mm", "fo0", "dpre", "fi_mm", "fi0", "fi1", "fo0", "sb", "fi0", "co_mm", "dc", "co", "xd0", "out",
    "fi1", "xd1", "xp", "co", "fo0", "xd2", "xd3", "fo1", "fi0", "fb", "som", "fo1", "xg3", "smm", "sm",
    "cqm", "cq", "fi1", "so", "psb", "fi0", "spm", "sp", "fo0", "so", "cq", "cmm", "cm", "co", "sm", "fi1",
    "dmp", "sp", "sd7", "co", "fi0", "so", "sm", "sd5", "fo1", "co", "cq", "sd3", "sd1", "sp", "cm", "mkm",
    "so", "dwm", "mk", "dwo", "cm", "co", "fo1", "sm", "sp", "fi0", "mk", "dxp", "fo1", "cq", "sp", "cm",
    "fo0", "sm", "cq", "mk", "sp", "fi0", "cm", "co", "fo1", "so", "fi1", "fin2", "sm", "cq", "mk", "fin1",
    "fo0", "fo1", "cm", "so", "cm", "sp", "cq", "so", "fi1", "mk",
)


class Refs:
    def __init__(self, names, refs):
        for name, ref in zip(names, refs):
            setattr(self, name, ref)


INPUTS = (
    "x_in", "mem_in", "cot_in", "seg_in", "pad_in",
    "h_sp", "h_so", "h_cq", "h_cm", "h_co", "h_fi", "h_fo",
    "fi_b", "fo_b", "gain", "bias", "scale",
)
OUTPUTS = (
    "out", "dx_out", "dm_out", "g_sp", "g_so", "g_cq", "g_cm", "g_co", "g_fi", "g_fo",
    "b_fi", "b_fo", "b_gain", "b_bias", "b_scale",
)


def layer_kernel(z, names, *refs):
    g = Refs(names, refs)
    g.w_sp = g.h_sp
    g.dxp, g.dmp = g.co32.at[pl.ds(0, z.t + z.halo)], g.n2.at[pl.ds(0, 2 * z.mt)]
    n, t, mt, d, ff, hd, split = z.n, z.t, z.mt, z.d, z.ff, z.hd, z.split
    half = 2 * hd
    pairs = d // half
    softmax_scale = 1.0 / math.sqrt(hd)
    s = lax.axis_index("seq")
    r = lax.axis_index("rows")

    def bit_of(index, k):
        return lax.rem(lax.div(index, 2 ** k), 2)

    def seq_partner(k):
        return s + (1 - 2 * bit_of(s, k)) * 2 ** k

    def row_partner(k):
        return r + (1 - 2 * bit_of(r, k)) * 2 ** k

    def place_of(index):
        return sum(bit_of(index, k) * 2 ** (z.bits - 1 - k) for k in range(z.bits))

    nxt = lax.rem(s + 1, n)
    prv = lax.rem(s + n - 1, n)
    my_head = lax.div(s, split)
    my_part = lax.rem(s, split)
    own_turn = lax.div(s, split)
    own_rest = lax.rem(s, split)
    own_part = own_rest + lax.rem(own_turn, 2) * (split - 1 - 2 * own_rest)

    barrier = pltpu.get_barrier_semaphore()
    for step in range(1, n):
        pl.semaphore_signal(barrier, inc=1, device_id=(lax.rem(s + step, n), r), device_id_type=MESH)
    for k in range(z.row_bits):
        pl.semaphore_signal(barrier, inc=1, device_id=(s, row_partner(k)), device_id_type=MESH)

    loads = {
        name: pltpu.make_async_copy(getattr(g, "h_" + name), getattr(g, "w_" + name), g.wsem.at[j])
        for j, name in enumerate(("cm", "so", "cq", "co", "fi", "fo"))
    }

    def remote(src, dst, ssem, rsem, dev):
        return pltpu.make_async_remote_copy(
            src_ref=src, dst_ref=dst, send_sem=ssem, recv_sem=rsem,
            device_id=dev, device_id_type=MESH,
        )

    class Spread:
        def __init__(self, src, dst, ssem, rsem, dest):
            self.dest = dest
            self.far = remote(src, dst, ssem, rsem, (dest, r))
            self.near = pltpu.make_async_copy(src, dst, rsem)

        def start(self):
            @pl.when(self.dest != s)
            def _():
                self.far.start()

            @pl.when(self.dest == s)
            def _():
                self.near.start()

    def wait_whole(ref, sem):
        pltpu.make_async_copy(ref, ref, sem).wait()

    def wait_sent(ref, sem, own):
        count = ref.shape[0]

        @pl.when(own)
        def _():
            wait_whole(ref.at[pl.ds(0, count - 1)], sem)

        @pl.when(jnp.logical_not(own))
        def _():
            wait_whole(ref, sem)

    class Chain:
        def __init__(self, buf, send, recv):
            self.buf, self.send, self.recv = buf, send, recv
            self.line = n // 4
            self.zz, self.xx, self.core = lax.div(s, 4), bit_of(s, 1), bit_of(s, 0)

        def copy(self, way, origin):
            dev = (s + 4, s - 4, s + 2 - 4 * self.xx, s + 1 - 2 * self.core)[way]
            at = place_of(origin)
            block = self.buf.at[at]
            return remote(block, block, self.send.at[way], self.recv.at[at], (dev, r))

        def arrive(self, origin):
            at = place_of(origin)
            wait_whole(self.buf.at[at], self.recv.at[at])

        def pass_on(self, zz, ahead, back):
            origin = s + 4 * (zz - self.zz)
            if ahead:
                @pl.when(self.zz < self.line - 1)
                def _():
                    self.copy(0, origin).start()
            if back:
                @pl.when(self.zz > 0)
                def _():
                    self.copy(1, origin).start()
            self.copy(2, origin).start()
            self.copy(3, origin).start()

        def start(self):
            self.pass_on(self.zz, True, True)

        def step(self, j):
            low, high = self.zz - 1 - j, self.zz + 1 + j

            @pl.when(low >= 0)
            def _():
                self.arrive(s + 4 * (low - self.zz))
                self.pass_on(low, True, False)

            @pl.when(high < self.line)
            def _():
                self.arrive(s + 4 * (high - self.zz))
                self.pass_on(high, False, True)

        def cross_step(self, j):
            other = s + 2 - 4 * self.xx
            for sign in ((1,) if j == 0 else (-1, 1)):
                zz = self.zz + sign * j

                @pl.when((zz >= 0) & (zz < self.line))
                def _():
                    origin = other + 4 * (zz - self.zz)
                    self.arrive(origin)
                    self.copy(3, origin).start()

        def finish(self):
            other = s + 1 - 2 * self.core
            for k in range(2 * self.line):
                self.arrive(lax.rem(other, 2) + 2 * k)

        def drain(self):
            for zz in range(self.line):
                for way, count in ((0, zz + 1 if zz < self.line - 1 else 0), (1, self.line - zz if zz else 0)):
                    if count:
                        @pl.when(self.zz == zz)
                        def _():
                            wait_whole(self.buf.at[pl.ds(0, count)], self.send.at[way])
            wait_whole(self.buf.at[pl.ds(0, self.line)], self.send.at[2])
            wait_whole(self.buf.at[pl.ds(0, 2 * self.line)], self.send.at[3])

    class Sum:
        def __init__(self, name, number):
            self.name, self.number = name, number
            self.share, self.columns, _, target, self.offset = z.sums[name]
            self.out, self.result_at = getattr(g, "o_" + target, None), getattr(g, "g_" + target, None)
            self.a = g.mg if name == "mk" else getattr(g, "a_" + name)
            self.r = getattr(g, "r_" + name)
            self.ss, self.rs = getattr(g, "ss_" + name), getattr(g, "rs_" + name)
            self.steps, self.parts = z.steps(name), z.parts(name)
            self.spans = z.received(name)[0]
            self.copies = {}
            self.at = -1

        def held(self, i):
            if i == 0:
                return self.a, 0, n * self.parts
            return (self.r,) + self.spans[i - 1]

        def bit(self, i):
            kind, k = self.steps[i]
            return bit_of(s, k) if kind == "seq" else bit_of(r, k)

        def start(self, i):
            ref, first, blocks = self.held(i)
            into, into_first, count = self.held(i + 1)
            kind, k = self.steps[i]
            src = ref.at[pl.ds(first + (1 - self.bit(i)) * count, count)] if blocks > count else (
                ref.at[pl.ds(first, count)])
            dev = (seq_partner(k), r) if kind == "seq" else (s, row_partner(k))
            self.copies[i] = remote(src, into.at[pl.ds(into_first, count)], self.ss, self.rs.at[i], dev)
            self.copies[i].start()

        def finish(self, i):
            self.copies[i].wait()
            ref, first, blocks = self.held(i)
            into, into_first, count = self.held(i + 1)
            kind, k = self.steps[i]
            last = i + 1 == len(self.steps)
            if kind == "gather":
                width = self.columns // 2
                mine, theirs = bit_of(r, 0) * width, (1 - bit_of(r, 0)) * width
                self.out[:, pl.ds(pl.multiple_of(self.offset + mine, 128), width)] = ref[first].astype(F32)
                self.out[:, pl.ds(pl.multiple_of(self.offset + theirs, 128), width)] = (
                    into[into_first].astype(F32))
                return
            if last and self.out is not None:
                self.out[:, self.offset:self.offset + self.columns] = (
                    into[into_first].astype(F32) + ref[first].astype(F32))
                return
            base = first + self.bit(i) * count if blocks > count else first
            if count <= 2:
                for j in range(count):
                    into[into_first + j] = into[into_first + j] + ref[base + j]
            else:
                def add(j, carry):
                    into[into_first + j] = into[into_first + j] + ref[base + j]
                    return carry
                lax.fori_loop(0, count, add, 0)

        def output(self):
            cols = pl.ds(self.offset, self.columns)
            return pltpu.make_async_copy(
                self.out.at[:, cols], self.result_at.at[:, cols], g.outs.at[self.number])

        def over(self):
            return self.at == len(self.steps)

        def advance(self):
            if self.over():
                return
            if self.at >= 0:
                self.finish(self.at)
            self.at += 1
            if not self.over():
                self.start(self.at)
            elif self.out is not None and self.name not in ("sp", "sm"):
                self.output().start()

        def result(self):
            ref, first, _ = self.held(len(self.steps))
            return ref[first]

        def put(self, owner, value, first_column):
            width = self.columns // self.parts
            position = sum(
                ((owner >> k) & 1) << (z.bits - 1 - j) for j, k in enumerate(z.seq_bits(self.name)))
            below = n >> (z.halving(self.name) or 0)
            above, rest = position // below, position % below
            for part in range(self.parts):
                start = self.offset + part * width
                low, high = max(first_column, start), min(first_column + value.shape[1], start + width)
                if low < high:
                    where = (above * self.parts + part) * below + rest
                    self.a[where, :, low - start:high - start] = (
                        value[:, low - first_column:high - first_column])

    sums = {name: Sum(name, j) for j, name in enumerate(z.sums)}

    def put_rows(target, value, first_column=0, first_owner=0):
        value = value.astype(BF)
        for name, (share, _, _, output, _) in z.sums.items():
            if output == target:
                for j in range(value.shape[0] // share):
                    sums[name].put(first_owner + j, value[j * share:(j + 1) * share], first_column)

    def over_rows(count, size, step):
        def one(j, carry):
            step(pl.ds(pl.multiple_of(j * size, size), size))
            return carry
        lax.fori_loop(0, count // size, one, 0)

    def mean(value):
        return jnp.sum(value, -1, keepdims=True) * (1.0 / d)

    def norm_forward(total):
        centred = total - mean(total)
        inverse = lax.rsqrt(mean(centred * centred) + EPSILON)
        return centred * inverse, inverse

    def norm_backward(grad, normed, inverse, gain_row, which):
        scaled = grad * gain_row
        result = inverse * (scaled - mean(scaled) - normed * mean(scaled * normed))
        g.sm[which:which + 1, :] += jnp.sum(grad * normed, 0, keepdims=True)
        g.sm[3 + which:4 + which, :] += jnp.sum(grad, 0, keepdims=True)
        return result

    lane = lax.broadcasted_iota(I32, (t, half), 1)

    def only(value, which):
        keep = (lane < hd) if which == 0 else (lane >= hd)
        return jnp.where(keep, value, jnp.zeros_like(value))

    def both(first, second):
        return jnp.where(lane < hd, first, second)

    def pair_cols(p, offset=0):
        return slice(offset + p * half, offset + (p + 1) * half)

    def keep_lse(index, value):
        g.lse[:, index:index + 1] = value

    def kept_lse(index):
        return g.lse[:, index:index + 1]

    SELF_PACKED, CROSS_PACKED, CROSS_DOC, SELF_DOC = (k * HEADS for k in range(4))

    tokens_all = Chain(g.xg, g.xgs, g.xgr)
    memory_all = Chain(g.mg, g.mgs, g.mgr)
    place = place_of(s)
    other_seg = g.seg_in[1:2, :]
    swap = jnp.min(other_seg, -1, keepdims=True) == jnp.max(other_seg, -1, keepdims=True)

    def ordered(ref, into):
        first, second, count = ref[:, 0, :], ref[:, 1, :], ref.shape[0]
        into[0:count, :] = jnp.where(swap, second, first)
        into[count:, :] = jnp.where(swap, first, second)

    def restored(first, second, ref):
        ref[:, 0, :] = jnp.where(swap, second, first)
        ref[:, 1, :] = jnp.where(swap, first, second)

    ordered(g.x_in, g.x)
    for load in loads.values():
        load.start()

    for part in range(3):
        made = nn(g.x[0:t, :], g.w_sp[:, part * d:(part + 1) * d]).astype(BF)
        g.qkvt[:, part * hd:(part + 1) * hd, :] = made.T.reshape(HEADS, hd, t)
    pl.semaphore_wait(barrier, n - 1 + z.row_bits)
    for h in range(HEADS):
        Spread(g.qkvt.at[h, pl.ds(hd, 2 * hd)], g.kv.at[my_part, own_turn], g.kv_s, g.kv_r,
               h * split + my_part).start()
    for h in range(HEADS):
        Spread(g.qkvt.at[h, pl.ds(0, hd)], g.qt.at[own_turn], g.q_s, g.q_r, h * split + own_part).start()
    ordered(g.mem_in, g.mem)
    seg = jnp.where(swap, g.seg_in[0:1, :], other_seg)
    pad = jnp.where(swap, g.pad_in[0:1, :], g.pad_in[1:2, :])
    q_at = lax.broadcasted_iota(I32, (t, t), 0)
    k_at = lax.broadcasted_iota(I32, (t, t), 1)
    seg_q = jnp.sum(jnp.where(q_at == k_at, seg.astype(F32), 0.0), -1, keepdims=True).astype(I32)
    pick = (q_at == 2 * lax.rem(k_at + z.mhalo, mt)).astype(F32)
    mem_seg = jnp.dot(
        jnp.broadcast_to(seg.astype(F32), (8, t)), pick,
        precision=lax.Precision.HIGHEST, preferred_element_type=F32).astype(I32)
    g.codes[0:1, :] = seg
    g.codes[1:2, :] = pad
    g.codes[2:3, :] = pltpu.roll(seg, z.halo, 1)
    g.codes[3:4, :] = pltpu.roll(pad, z.halo, 1)
    g.codes[4:8, :] = mem_seg[0:4]
    g.xg[place] = g.x[0:t, :]
    g.mg[place] = g.mem[0:mt, :]
    g.xw[0:t, :] = g.x[t:, :]
    g.mw[z.mhalo:z.mhalo + mt, :] = g.mem[mt:, :]
    halo_copies = [
        remote(g.codes, g.cn, g.hs.at[0], g.hr.at[0], (prv, r)),
        remote(g.codes, g.cp, g.hs.at[1], g.hr.at[1], (nxt, r)),
        remote(g.x.at[pl.ds(2 * t - z.halo, z.halo)], g.xw.at[pl.ds(t, z.halo)],
               g.hs.at[2], g.hr.at[2], (nxt, r)),
        remote(g.mem.at[pl.ds(mt, z.mhalo)], g.mw.at[pl.ds(z.mhalo + mt, z.mhalo)],
               g.hs.at[3], g.hr.at[3], (prv, r)),
        remote(g.mem.at[pl.ds(2 * mt - z.mhalo, z.mhalo)], g.mw.at[pl.ds(0, z.mhalo)],
               g.hs.at[4], g.hr.at[4], (nxt, r)),
    ]
    for copy in halo_copies:
        copy.start()

    memory_all.start()

    g.qp[...] = nn(g.xw[0:t, :], g.w_sp[:, :d]).astype(BF)
    ordered(g.cot_in, g.cot)
    g.sm[...] = jnp.zeros_like(g.sm)

    def self_mask():
        seg_k, pad_k = g.codes[0:1, :], g.codes[1:2, :]
        own = (seg_q == seg_k) & (k_at <= q_at) & ((pad_k == 1) | (k_at == q_at))
        prev = (seg_q == g.cp[2:3, :]) & (g.cp[3:4, :] == 1)
        return own, prev[:, :z.halo]

    def cross_mask():
        at = lax.broadcasted_iota(I32, (1, 2 * mt), 1)
        seg_k = jnp.where(
            at < z.mhalo, g.cp[4:5, :],
            jnp.where(at < z.mhalo + mt, g.codes[4:5, :], g.cn[4:5, :]))
        return seg_q == seg_k

    def softmax_parts(scores):
        top = functools.reduce(jnp.maximum, [jnp.max(b, -1, keepdims=True) for b in scores])
        weights = [jnp.exp(b - top) for b in scores]
        total = functools.reduce(jnp.add, [jnp.sum(w, -1, keepdims=True) for w in weights])
        return weights, total, top + jnp.log(total)

    def hand_over(f):
        return remote(g.kv.at[my_part], g.kv.at[my_part], g.kw_s.at[f], g.kw_r.at[my_part],
                      (my_head * split + f, r))

    wait_whole(g.kv.at[my_part], g.kv_r)
    for f in range(split):
        @pl.when(my_part != f)
        def _():
            hand_over(f).start()
    wait_whole(g.qt, g.q_r)
    for f in range(split):
        @pl.when(my_part != f)
        def _():
            wait_whole(g.kv.at[f], g.kw_r.at[f])
    for b in range(n):
        g.kts[:, b * t:(b + 1) * t] = g.kv[b % split, b // split, 0:hd]
        g.vts[:, b * t:(b + 1) * t] = g.kv[b % split, b // split, hd:]

    wide = split * t
    diag_q = lax.broadcasted_iota(I32, (t, wide), 0)
    diag_k = lax.broadcasted_iota(I32, (t, wide), 1)

    def turn_rest(i):
        return my_part if i % 2 == 0 else split - 1 - my_part

    def diag_mask(i):
        return diag_k <= diag_q + turn_rest(i) * t

    def attend_document(i):
        q = g.qt[i].T
        low = i * wide
        blocks = []
        if low:
            blocks.append(nn(q, g.kts[:, :low]) * softmax_scale)
        blocks.append(jnp.where(
            diag_mask(i), nn(q, g.kts[:, low:low + wide]) * softmax_scale, NEGATIVE))
        weights, total, lse = softmax_parts(blocks)
        keep_lse(SELF_DOC + i, lse)
        o = nt(weights[-1].astype(BF), g.vts[:, low:low + wide])
        if low:
            o = o + nt(weights[0].astype(BF), g.vts[:, :low])
        o = o / total
        g.of[i] = o
        g.ots[i] = o.T.astype(BF)

    for turns in ((0, 1, 2, 3), (4, 5), (6, 7)):
        for i in turns:
            attend_document(i)
        if turns[0] == 0:
            memory_all.step(0)
        for i in turns:
            Spread(g.ots.at[i], g.otr.at[my_head], g.o_s, g.o_r, i * split + turn_rest(i)).start()
    memory_all.cross_step(0)

    for copy in halo_copies:
        copy.wait()
    g.ps[...] = nn(g.xw[...], g.w_sp[:, d:]).astype(BF)
    loads["cm"].wait()
    g.pm[...] = nn(g.mw[...], g.w_cm[...]).astype(BF)
    for j in range(1, n // 4 - 2):
        memory_all.step(j)

    own_mask, prev_mask = self_mask()
    for p in range(pairs):
        q, k, v = g.qp[:, pair_cols(p)], g.ps[:, pair_cols(p)], g.ps[:, pair_cols(p, d)]
        outs = []
        for w in range(2):
            sc = nt(only(q, w), k) * softmax_scale
            blocks = [jnp.where(own_mask, sc[:, :t], NEGATIVE), jnp.where(prev_mask, sc[:, t:], NEGATIVE)]
            weights, total, lse = softmax_parts(blocks)
            keep_lse(SELF_PACKED + 2 * p + w, lse)
            o = nn(weights[0].astype(BF), v[:t]) + nn(weights[1].astype(BF), v[t:])
            outs.append(o / total)
        o = both(*outs)
        g.op[:, pair_cols(p)] = o
        g.att[t:, pair_cols(p)] = o.astype(BF)

    for j in range(1, n // 4 - 2):
        memory_all.cross_step(j)
    memory_all.step(n // 4 - 2)

    loads["so"].wait()
    wait_whole(g.otr, g.o_r)
    g.att[0:t, :] = g.otr[...].reshape(d, t).T
    g.tmp[...] = nn(g.att[...], g.w_so[...])

    def first_norm(rows):
        total = g.x[rows, :].astype(F32) * g.scale[0:1, :] + g.tmp[rows, :]
        normed, inverse = norm_forward(total)
        g.n1[rows, :] = normed
        g.i1[rows, :] = inverse
        g.h1b[rows, :] = (normed * g.gain[0:1, :] + g.bias[0:1, :]).astype(BF)

    over_rows(2 * t, 128, first_norm)
    memory_all.cross_step(n // 4 - 2)
    tokens_all.start()
    loads["cq"].wait()
    g.cqv[...] = nn(g.h1b[...], g.w_cq[...]).astype(BF)

    seen = cross_mask()
    for p in range(pairs):
        q, k, v = g.cqv[t:, pair_cols(p)], g.pm[:, pair_cols(p)], g.pm[:, pair_cols(p, d)]
        outs = []
        for w in range(2):
            sc = jnp.where(seen, nt(only(q, w), k) * softmax_scale, NEGATIVE)
            (weights,), total, lse = softmax_parts([sc])
            keep_lse(CROSS_PACKED + 2 * p + w, lse)
            outs.append(nn(weights.astype(BF), v) / total)
        o = both(*outs)
        g.co32[t:, pair_cols(p)] = o
        g.catt[t:, pair_cols(p)] = o.astype(BF)
    memory_all.cross_step(n // 4 - 1)
    memory_all.finish()

    for part in range(2):
        cols = slice(part * d, (part + 1) * d)
        g.mkv[:, :, cols] = nn(g.mg[...].reshape(n * mt, d), g.w_cm[:, cols]).astype(BF).reshape(n, mt, d)

    tokens_all.step(0)
    tokens_all.cross_step(0)

    for p in range(pairs):
        q = g.cqv[0:t, pair_cols(p)]
        k = g.mkv[:, :, pair_cols(p)].reshape(n * mt, half)
        v = g.mkv[:, :, pair_cols(p, d)].reshape(n * mt, half)
        outs = []
        for w in range(2):
            sc = nt(only(q, w), k) * softmax_scale
            (weights,), total, lse = softmax_parts([sc])
            keep_lse(CROSS_DOC + 2 * p + w, lse)
            outs.append(nn(weights.astype(BF), v) / total)
        o = both(*outs)
        g.co32[0:t, pair_cols(p)] = o
        g.catt[0:t, pair_cols(p)] = o.astype(BF)
    stays = own_part == my_part
    wait_whole(g.kvfin.at[pl.ds(0, HEADS - 1)], g.kv_s)
    wait_sent(g.qt, g.q_s, stays)
    wait_sent(g.ots, g.o_s, stays)
    for f in range(split):
        @pl.when(my_part != f)
        def _():
            hand_over(f).wait_send()
    memory_all.drain()

    loads["co"].wait()
    g.tmp[...] = nn(g.catt[...], g.w_co[...])

    def second_norm(rows):
        hidden1 = g.n1[rows, :] * g.gain[0:1, :] + g.bias[0:1, :]
        normed, inverse = norm_forward(hidden1 * g.scale[1:2, :] + g.tmp[rows, :])
        g.n2[rows, :] = normed
        g.i2[rows, :] = inverse
        g.h2b[rows, :] = (normed * g.gain[1:2, :] + g.bias[1:2, :]).astype(BF)

    over_rows(2 * t, 128, second_norm)

    loads["fi"].wait()
    chunks = ff // d
    for c in range(chunks):
        cols = slice(c * d, (c + 1) * d)
        pre = nn(g.h2b[...], g.w_fi[:, cols]) + g.fi_b[0:1, cols]
        square = pre * pre
        bent = jnp.tanh(GELU_A * pre * (1.0 + GELU_B * square))
        g.act[:, cols] = (0.5 * pre * (1.0 + bent)).astype(BF)
        g.dg[:, cols] = 0.5 * (1.0 + bent) + 0.5 * pre * (1.0 - bent * bent) * (
            GELU_A * (1.0 + 3.0 * GELU_B * square))
    tokens_all.step(1)
    loads["fo"].wait()
    g.tmp[...] = nn(g.act[...], g.w_fo[...])

    def third_norm(rows):
        hidden2 = g.n2[rows, :] * g.gain[1:2, :] + g.bias[1:2, :]
        total = hidden2 * g.scale[2:3, :] + (g.tmp[rows, :] + g.fo_b[0:1, :])
        normed, inverse = norm_forward(total)
        grad = g.cot[rows, :].astype(F32)
        g.cot[rows, :] = (normed * g.gain[2:3, :] + g.bias[2:3, :]).astype(BF)
        back = norm_backward(grad, normed, inverse, g.gain[2:3, :], 2)
        g.sm[8:9, :] += jnp.sum(back * hidden2, 0, keepdims=True)
        g.dx[rows, :] = back
        low = back.astype(BF)
        g.dtb[rows, :] = low
        g.sm[9:10, :] += jnp.sum(low.astype(F32), 0, keepdims=True)

    over_rows(2 * t, 128, third_norm)
    tokens_all.cross_step(1)
    tokens_all.step(2)

    for j in range(3, n // 4 - 1):
        tokens_all.step(j)
        tokens_all.cross_step(j)

    def feed_out_grads():
        for c in range(chunks):
            cols = slice(c * d, (c + 1) * d)
            put_rows("fo", nn(g.act[:, cols].T, g.dtb[...]), 0, c * d // z.sums["fo0"][0])

    def before_gelu():
        for c in range(chunks):
            cols = slice(c * d, (c + 1) * d)
            back = (nt(g.dtb[...], g.w_fo[cols, :]) * g.dg[:, cols]).astype(BF)
            g.act[:, cols] = back
            g.sm[10 + c:11 + c, :] = jnp.sum(back.astype(F32), 0, keepdims=True)

    def feed_in_grads():
        h2t = g.h2b[...].T
        for c in range(chunks):
            cols = slice(c * d, (c + 1) * d)
            put_rows("fi", nn(h2t, g.act[:, cols]), c * d)

    def second_norm_back():
        g.tmp[...] = nt(g.act[...], g.w_fi[...])

        def second_back(rows):
            grad = g.dx[rows, :] * g.scale[2:3, :] + g.tmp[rows, :]
            back = norm_backward(grad, g.n2[rows, :], g.i2[rows, :], g.gain[1:2, :], 1)
            hidden1 = g.n1[rows, :] * g.gain[0:1, :] + g.bias[0:1, :]
            g.sm[7:8, :] += jnp.sum(back * hidden1, 0, keepdims=True)
            g.dx[rows, :] = back
            g.dtb[rows, :] = back.astype(BF)

        over_rows(2 * t, 128, second_back)

    def cross_output_back():
        g.dc[...] = nt(g.dtb[...], g.w_co[...]).astype(BF)

    def cross_output_grads():
        put_rows("co", nn(g.catt[...].T, g.dtb[...]))

    def result_out():
        restored(g.cot[0:t, :], g.cot[t:, :], g.o_out)
        pltpu.make_async_copy(g.o_out, g.out, g.outs.at[len(z.sums)]).start()

    def cross_document(p):
        q, go, o = g.cqv[0:t, pair_cols(p)], g.dc[0:t, pair_cols(p)], g.co32[0:t, pair_cols(p)]
        qt, gt = q.T, go.T
        k = g.mkv[:, :, pair_cols(p)].reshape(n * mt, half)
        v = g.mkv[:, :, pair_cols(p, d)].reshape(n * mt, half)
        dqs, dks, dvs = [], [], []
        for w in range(2):
            qm, gm = only(q, w), only(go, w)
            weights = jnp.exp(nt(qm, k) * softmax_scale - kept_lse(CROSS_DOC + 2 * p + w))
            delta = jnp.sum(gm.astype(F32) * o, -1, keepdims=True)
            ds = (weights * (nt(gm, v) - delta)).astype(BF)
            dqs.append(nn(ds, k))
            dks.append(nn(qt[w * hd:(w + 1) * hd], ds))
            dvs.append(nn(gt[w * hd:(w + 1) * hd], weights.astype(BF)))
        g.dcq[0:t, pair_cols(p)] = (both(*dqs) * softmax_scale).astype(BF)
        dk = (jnp.concatenate(dks, 0) * softmax_scale).astype(BF).T
        dv = jnp.concatenate(dvs, 0).astype(BF).T
        g.mkv[:, :, pair_cols(p)] = dk.reshape(n, mt, half)
        g.mkv[:, :, pair_cols(p, d)] = dv.reshape(n, mt, half)

    def cross_packed():
        for p in range(pairs):
            q, k, v = g.cqv[t:, pair_cols(p)], g.pm[:, pair_cols(p)], g.pm[:, pair_cols(p, d)]
            go, o = g.dc[t:, pair_cols(p)], g.co32[t:, pair_cols(p)]
            dqs, dk, dv = [], 0.0, 0.0
            for w in range(2):
                qm, gm = only(q, w), only(go, w)
                weights = jnp.where(
                    seen, jnp.exp(nt(qm, k) * softmax_scale - kept_lse(CROSS_PACKED + 2 * p + w)), 0.0)
                delta = jnp.sum(gm.astype(F32) * o, -1, keepdims=True)
                ds = (weights * (nt(gm, v) - delta)).astype(BF)
                dqs.append(nn(ds, k))
                dk = dk + tn(ds, qm)
                dv = dv + tn(weights.astype(BF), gm)
            g.dcq[t:, pair_cols(p)] = (both(*dqs) * softmax_scale).astype(BF)
            g.pm[:, pair_cols(p)] = (dk * softmax_scale).astype(BF)
            g.pm[:, pair_cols(p, d)] = dv.astype(BF)

    late = {}

    def first_norm_back():
        g.tmp[...] = nt(g.dcq[...], g.w_cq[...])

        def first_back(rows):
            grad = g.dx[rows, :] * g.scale[1:2, :] + g.tmp[rows, :]
            back = norm_backward(grad, g.n1[rows, :], g.i1[rows, :], g.gain[0:1, :], 0)
            g.sm[6:7, :] += jnp.sum(back * g.x[rows, :].astype(F32), 0, keepdims=True)
            g.dx[rows, :] = back
            g.dtb[rows, :] = back.astype(BF)

        over_rows(2 * t, 128, first_back)
        d_self = nt(g.dtb[...], g.w_so[...]).astype(BF)
        g.dself[...] = d_self[t:]
        g.dos[...] = d_self[:t].T.reshape(HEADS, hd, t)
        for h in range(HEADS):
            Spread(g.dos.at[h], g.dor.at[own_turn], g.do_s, g.do_r, h * split + own_part).start()

    def small_sums():
        share, bias_share = d // n, ff // n
        for o in range(n):
            first, bias_first = o * share, o * bias_share
            row = 10 + bias_first // d
            tile = g.sm[:, first // 128 * 128:first // 128 * 128 + 128]
            if first % 128:
                tile = pltpu.roll(tile, 128 - first % 128, 1)
            bias = g.sm[row:row + 1, bias_first % d // 128 * 128:bias_first % d // 128 * 128 + 128]
            if bias_first % 128:
                bias = pltpu.roll(bias, 128 - bias_first % 128, 1)
            sums["sm"].put(o, jnp.concatenate([tile[0:10], bias, tile[11:16]], 0), 0)

    def cross_memory_grads():
        mem_t = g.mg[...].reshape(n * mt, d).T
        win_t = g.mw[...].T
        for part in range(2):
            cols = slice(part * d, (part + 1) * d)
            doc_kv = g.mkv[:, :, cols].reshape(n * mt, d)
            put_rows("cm", nn(mem_t, doc_kv) + nn(win_t, g.pm[:, cols]), part * d)

    def memory_back():
        g.mg[...] = nt(g.mkv[...].reshape(n * mt, 2 * d), g.w_cm[...]).astype(BF).reshape(n, mt, d)

    def memory_halo():
        g.dmp[...] = nt(g.pm[...], g.w_cm[...])
        g.hms[0:z.mhalo, :] = g.dmp[0:z.mhalo, :].astype(BF)
        g.hms[z.mhalo:, :] = g.dmp[z.mhalo + mt:, :].astype(BF)
        late["memory"] = [
            remote(g.hms.at[pl.ds(0, z.mhalo)], g.hmr.at[pl.ds(z.mhalo, z.mhalo)],
                   g.hs.at[5], g.hr.at[5], (prv, r)),
            remote(g.hms.at[pl.ds(z.mhalo, z.mhalo)], g.hmr.at[pl.ds(0, z.mhalo)],
                   g.hs.at[6], g.hr.at[6], (nxt, r)),
        ]
        for copy in late["memory"]:
            copy.start()

    def cross_query_grads():
        put_rows("cq", nn(g.h1b[...].T, g.dcq[...]))

    def self_output_grads():
        put_rows("so", nn(g.att[...].T, g.dtb[...]))

    def self_packed():
        for p in range(pairs):
            q, k, v = g.qp[:, pair_cols(p)], g.ps[:, pair_cols(p)], g.ps[:, pair_cols(p, d)]
            go, o = g.dself[:, pair_cols(p)], g.op[:, pair_cols(p)]
            dqs, dk, dv = [], 0.0, 0.0
            for w in range(2):
                qm, gm = only(q, w), only(go, w)
                sc = nt(qm, k) * softmax_scale - kept_lse(SELF_PACKED + 2 * p + w)
                weights = jnp.concatenate(
                    [jnp.where(own_mask, jnp.exp(sc[:, :t]), 0.0),
                     jnp.where(prev_mask, jnp.exp(sc[:, t:]), 0.0)], 1)
                delta = jnp.sum(gm.astype(F32) * o, -1, keepdims=True)
                ds = (weights * (nt(gm, v) - delta)).astype(BF)
                dqs.append(nn(ds, k))
                dk = dk + tn(ds, qm)
                dv = dv + tn(weights.astype(BF), gm)
            g.qp[:, pair_cols(p)] = (both(*dqs) * softmax_scale).astype(BF)
            g.ps[:, pair_cols(p)] = (dk * softmax_scale).astype(BF)
            g.ps[:, pair_cols(p, d)] = dv.astype(BF)

    def self_project_grads():
        window_t = g.xw[...].T
        put_rows("sp", nn(window_t[:, :t], g.qp[...]), 0)
        put_rows("sp", nn(window_t, g.ps[:, :d]), d)
        put_rows("sp", nn(window_t, g.ps[:, d:]), 2 * d)

    def tokens_halo():
        g.dxp[...] = nt(g.ps[...], g.w_sp[:, d:])
        g.hss[...] = g.dxp[t:, :].astype(BF)
        late["tokens"] = remote(g.hss, g.hsr, g.hs.at[7], g.hr.at[7], (prv, r))
        late["tokens"].start()
        g.tmp[t:, :] = nt(g.qp[...], g.w_sp[:, :d]) + g.dxp[0:t, :]

    chunk = min(512, n * t)

    def kept(which, first, last):
        row, column = first // ff * 2 * hd + which * hd, first % ff
        return slice(row, row + hd), slice(column, column + last - first)

    def sibling(i, f):
        return remote(
            g.kvst.at[i, f], g.kvsib.at[i, my_part], g.sib_s,
            g.sib_r.at[i, lax.rem(my_part - f + split, split) - 1], (my_head * split + f, r))

    def to_siblings(action):
        for f in range(split):
            @pl.when(my_part != f)
            def _():
                action(f)

    def close_kv(i):
        g.kvfin[i] = g.kvst[i, my_part]

        def add(f):
            wait_whole(g.kvsib.at[i, f], g.sib_r.at[i, lax.rem(f - my_part + split, split) - 1])
            g.kvfin[i] = g.kvfin[i] + g.kvsib[i, f]

        to_siblings(add)
        Spread(g.kvfin.at[i], g.dkvr.at[my_head], g.kf_s, g.kf_r, i * split + my_part).start()

    def attend_document_back(i):
        b = i * split + turn_rest(i)
        qt, gt = g.qt[i], g.dor[i]
        q, go = qt.T, gt.T
        delta = jnp.sum(go.astype(F32) * g.of[i], -1, keepdims=True)
        lse = kept_lse(SELF_DOC + i)
        low = i * wide
        spans = [(a, min(a + chunk, low), False) for a in range(0, low, chunk)]
        spans.append((low, low + wide, True))
        dq = 0.0
        for first, last, masked in spans:
            k, v = g.kts[:, first:last], g.vts[:, first:last]
            weights = jnp.exp(nn(q, k) * softmax_scale - lse)
            if masked:
                weights = jnp.where(diag_mask(i), weights, 0.0)
            ds = (weights * (nn(go, v) - delta)).astype(BF)
            dq = dq + nt(ds, k)
            g.dg[kept(0, first, last)] += nn(qt, ds)
            g.dg[kept(1, first, last)] += nn(gt, weights.astype(BF))
        dqt = (dq * softmax_scale).T.astype(BF)
        g.ots[i] = dqt
        for f in range(split):
            first = (i * split + f) * t
            g.kvst[i, f, 0:hd] = (g.dg[kept(0, first, first + t)] * softmax_scale).astype(BF)
            g.kvst[i, f, hd:] = g.dg[kept(1, first, first + t)].astype(BF)
        g.dwt[0:hd, :] += nn(dqt, g.xg[place_of(b)])
        for f in range(split):
            g.dwt[hd:, :] += nn(g.kvst[i, f], g.xg[reverse_static(i * split + f, z.bits)])

    def self_document(turns):
        if turns[0] == HEADS - 1:
            tokens_all.finish()
            tokens_all.drain()
            wait_whole(g.dor, g.do_r)
            g.dg[...] = jnp.zeros_like(g.dg)
            g.dwt[...] = jnp.zeros_like(g.dwt)
        for i in turns:
            attend_document_back(i)
        for i in turns:
            Spread(g.ots.at[i], g.dqr.at[my_head], g.dq_s, g.dq_r, i * split + turn_rest(i)).start()
            to_siblings(lambda f: sibling(i, f).start())
        for i in late.get("turns", ()):
            close_kv(i)
        late["turns"] = turns

    def head_parts(f):
        return remote(g.dws.at[f], g.dwsib.at[my_part], g.ds_s.at[f], g.ds_r.at[my_part],
                      (my_head * split + f, r))

    def head_grads():
        whole = jnp.concatenate([g.dwt[...], jnp.zeros((hd, d), F32)], 0).T.astype(BF)
        share = d // n
        for o in range(n):
            g.dws[o % split, o // split] = whole[o * share:(o + 1) * share]
        to_siblings(lambda f: head_parts(f).start())

    def head_owners():
        for i in late["turns"]:
            close_kv(i)

        def add(f):
            wait_whole(g.dwsib.at[f], g.ds_r.at[f])
            g.dws[my_part] = g.dws[my_part] + g.dwsib[f]

        to_siblings(add)
        for j in range(HEADS):
            Spread(g.dws.at[my_part, j], g.dwr.at[my_head], g.dw_s, g.dw_r, j * split + my_part).start()

    def tokens_back():
        wait_whole(g.dqr, g.dq_r)
        g.dproj[:, 0:d] = g.dqr[...].reshape(d, t).T
        wait_whole(g.dkvr, g.kf_r)
        for part in range(2):
            g.dproj[:, (part + 1) * d:(part + 2) * d] = (
                g.dkvr[:, part * hd:(part + 1) * hd, :].reshape(d, t).T)
        g.tmp[0:t, :] = nt(g.dproj[...], g.w_sp[...])
        late["tokens"].wait()
        g.tmp[2 * t - z.halo:, :] += g.hsr[...].astype(F32)

        def last(rows):
            g.dx[rows, :] = g.dx[rows, :] * g.scale[0:1, :] + g.tmp[rows, :]

        over_rows(2 * t, 128, last)
        restored(g.dx[0:t, :], g.dx[t:, :], g.o_dx)
        pltpu.make_async_copy(g.o_dx, g.dx_out, g.outs.at[len(z.sums) + 1]).start()

    def shares(k):
        return remote(g.dsh, g.dshr.at[k], g.dy_s.at[k], g.dy_r.at[k], (s, row_partner(k)))

    def head_shares():
        wait_whole(g.dwr, g.dw_r)
        for p in range(pairs):
            left, right = g.dwr[2 * p], g.dwr[2 * p + 1]
            for part in range(3):
                cols = slice(part * hd, (part + 1) * hd)
                g.dsh[:, pair_cols(p, part * d)] = jnp.concatenate([left[:, cols], right[:, cols]], 1)
        shares(0).start()

    def rest_of_tokens():
        tokens_all.cross_step(2)
        tokens_all.cross_step(n // 4 - 1)

    pieces = dict(
        fo_mm=feed_out_grads, dpre=before_gelu, fi_mm=feed_in_grads, sb=second_norm_back,
        dc=cross_output_back, co_mm=cross_output_grads, out=result_out, xp=cross_packed,
        fb=first_norm_back, cmm=cross_memory_grads, mkm=memory_back, dmp=memory_halo,
        cqm=cross_query_grads, smm=small_sums, som=self_output_grads, psb=self_packed, spm=self_project_grads,
        dxp=tokens_halo, dwm=head_grads, dwo=head_owners, fin1=tokens_back, fin2=head_shares,
        xg3=rest_of_tokens,
    )
    for p in range(pairs):
        pieces["xd%d" % p] = functools.partial(cross_document, p)
    for i in range(1, HEADS, 2):
        pieces["sd%d" % i] = functools.partial(self_document, (i, i - 1))
    for name in ORDER:
        if name in pieces:
            pieces[name]()
        else:
            sums[name].advance()

    for k in range(z.row_bits - 1):
        shares(k).wait()
        g.dsh[...] = g.dsh[...] + g.dshr[k]
        shares(k + 1).start()
    while not all(one.over() for one in sums.values()):
        for one in sums.values():
            one.advance()
    for copy in late["memory"]:
        copy.wait()
    restored(sums["mk"].result().astype(F32),
             g.dmp[z.mhalo:z.mhalo + mt, :] + g.hmr[...].astype(F32), g.o_dm)
    pltpu.make_async_copy(g.o_dm, g.dm_out, g.outs.at[len(z.sums) + 2]).start()
    small = g.o_sm[...]
    g.o_bgain[...] = small[0:3, :d // n]
    g.o_bbias[...] = small[3:6, :d // n]
    g.o_bscale[...] = small[6:9, :d // n]
    g.o_bfo[...] = small[9:10, :d // n]
    g.o_bfi[...] = small[10:11, :ff // n]
    small_copies = [
        pltpu.make_async_copy(src, dst, g.outs.at[len(z.sums) + 3 + j])
        for j, (src, dst) in enumerate((
            (g.o_bgain, g.b_gain), (g.o_bbias, g.b_bias), (g.o_bscale, g.b_scale),
            (g.o_bfo, g.b_fo), (g.o_bfi, g.b_fi)))
    ]
    for copy in small_copies:
        copy.start()
    shares(z.row_bits - 1).wait()
    g.o_sp[...] = g.o_sp[...] + (g.dsh[...].astype(F32) + g.dshr[z.row_bits - 1].astype(F32))
    sums["sp"].output().start()
    wait_sent(g.dos, g.do_s, stays)
    wait_sent(g.ots, g.dq_s, stays)
    wait_whole(g.kvfin.at[pl.ds(0, HEADS - 1)], g.kf_s)
    wait_whole(g.dws.at[0, pl.ds(0, HEADS - 1)], g.dw_s)
    wait_whole(g.kvst.at[:, pl.ds(0, split - 1)], g.sib_s)
    to_siblings(lambda f: head_parts(f).wait_send())

    for copy in small_copies:
        copy.wait()
    for one in sums.values():
        if one.out is not None and one.name != "sm":
            one.output().wait()
    for j, (src, dst) in enumerate(((g.o_out, g.out), (g.o_dx, g.dx_out), (g.o_dm, g.dm_out))):
        pltpu.make_async_copy(src, dst, g.outs.at[len(z.sums) + j]).wait()


def on_device(
    mesh_shape,
    tokens, memory, segments, padding, cotangent,
    self_project, self_output, cross_query, cross_memory, cross_output,
    feed_in, feed_in_bias, feed_out, feed_out_bias, norm_gain, norm_bias, residual_scale,
):
    t, _, d = tokens.shape
    mt = memory.shape[0]
    ff = feed_in.shape[1]
    n, rows = mesh_shape
    z = Sizes(n, rows, t, mt, d, ff)

    scratch = z.scratch()
    names = INPUTS + OUTPUTS + tuple(scratch)
    vmem, anywhere = pl.BlockSpec(memory_space=pltpu.VMEM), pl.BlockSpec(memory_space=pl.ANY)
    shapes = [
        jax.ShapeDtypeStruct((t, 2, d), BF),
        jax.ShapeDtypeStruct((t, 2, d), F32),
        jax.ShapeDtypeStruct((mt, 2, d), F32),
    ] + [
        jax.ShapeDtypeStruct(shape, F32)
        for shape in (
            (d // n, 3 * d), (d // n, d), (d // n, d), (d // n, 2 * d), (d // n, d), (d // n, ff), (ff // n, d))
    ] + [
        jax.ShapeDtypeStruct((1, ff // n), F32), jax.ShapeDtypeStruct((1, d // n), F32),
    ] + [jax.ShapeDtypeStruct((3, d // n), F32)] * 3
    outcome = pl.pallas_call(
        functools.partial(layer_kernel, z, names),
        out_shape=shapes,
        in_specs=[vmem] * 6 + [anywhere] * 6 + [vmem] * 5,
        out_specs=[anywhere] * len(OUTPUTS),
        scratch_shapes=list(scratch.values()),
        compiler_params=pltpu.CompilerParams(
            collective_id=0, has_side_effects=True, vmem_limit_bytes=63 * 2 ** 20),
        name="layer",
    )(
        tokens, memory, cotangent, segments, padding,
        self_project, self_output, cross_query, cross_memory, cross_output, feed_in, feed_out,
        feed_in_bias.reshape(1, ff), feed_out_bias.reshape(1, d), norm_gain, norm_bias, residual_scale,
    )

    def hand_on(*refs):
        count = len(shapes)
        sources, results, held, sems = refs[:count], refs[count:2 * count], refs[2 * count:-1], refs[-1]
        into = [pltpu.make_async_copy(a, b, sems.at[0, j]) for j, (a, b) in enumerate(zip(sources, held))]
        out = [pltpu.make_async_copy(a, b, sems.at[1, j]) for j, (a, b) in enumerate(zip(held, results))]
        for copy in into:
            copy.start()
        for one, two in zip(into, out):
            one.wait()
            two.start()
        for copy in out:
            copy.wait()

    outcome = pl.pallas_call(
        hand_on,
        out_shape=shapes,
        in_specs=[anywhere] * len(shapes),
        out_specs=[anywhere] * len(shapes),
        scratch_shapes=[pltpu.VMEM(one.shape, one.dtype) for one in shapes] + [
            pltpu.SemaphoreType.DMA((2, len(shapes)))],
        name="results",
    )(*outcome)
    (out, dx, dm, g_sp, g_so, g_cq, g_cm, g_co, g_fi, g_fo,
     in_bias, out_bias, gain, bias, scale) = outcome
    return (
        out, dx, dm, g_sp, g_so, g_cq, g_cm, g_co, g_fi, in_bias.reshape(ff // n),
        g_fo, out_bias.reshape(d // n), gain, bias, scale,
    )


def solution(mesh):
    in_specs = (
        P("seq", "rows", None), P("seq", "rows", None), P("rows", "seq"), P("rows", "seq"),
        P("seq", "rows", None),
    ) + (P(),) * 12
    out_specs = (P("seq", "rows", None),) * 3 + (
        P("seq", None), P("seq", None), P("seq", None), P("seq", None), P("seq", None),
        P("seq", None), P("seq"), P("seq", None), P("seq"),
        P(None, "seq"), P(None, "seq"), P(None, "seq"),
    )
    shape = (mesh.shape["seq"], mesh.shape["rows"])
    return jax.shard_map(
        functools.partial(on_device, shape),
        mesh=mesh, in_specs=in_specs, out_specs=out_specs, check_vma=False,
    )
```

```python
import functools
import math

import jax
import jax.numpy as jnp
from jax import lax
from jax.experimental import pallas as pl
from jax.experimental.pallas import tpu as pltpu
from jax.sharding import PartitionSpec as P

HEADS = 8
EPSILON = 1e-05
NEGATIVE = -1e30
BF = jnp.bfloat16
F32 = jnp.float32
I32 = jnp.int32
MESH = pl.DeviceIdType.MESH
GELU_A = math.sqrt(2.0 / math.pi)
GELU_B = 0.044715


def nn(a, b):
    return jnp.dot(a, b, preferred_element_type=F32)


def nt(a, b):
    return lax.dot_general(a, b, (((1,), (1,)), ((), ())), preferred_element_type=F32)


def tn(a, b):
    return lax.dot_general(a, b, (((0,), (0,)), ((), ())), preferred_element_type=F32)


def log2(value):
    return int(value).bit_length() - 1


def reverse_static(index, bits):
    return sum(((index >> k) & 1) << (bits - 1 - k) for k in range(bits))


class Sizes:
    def __init__(self, n, rows, t, mt, d, ff):
        self.n, self.rows, self.t, self.mt, self.d, self.ff = n, rows, t, mt, d, ff
        self.bits, self.row_bits = log2(n), log2(rows)
        self.split = n // HEADS
        self.hd = d // HEADS
        self.halo = t // 2
        self.mhalo = mt // 2
        self.sums = {
            "fo0": (ff // n, d // 2, "far first", "fo", 0),
            "fo1": (ff // n, d // 2, "rows second", "fo", d // 2),
            "fi0": (d // n, ff // 2, "rows third", "fi", 0),
            "fi1": (d // n, ff // 2, "far first", "fi", ff // 2),
            "co": (d // n, d, "rows second", "co", 0),
            "cq": (d // n, d, "rows third", "cq", 0),
            "mk": (mt, d, "seq alone", "mk", 0),
            "cm": (d // n, 2 * d, "rows second", "cm", 0),
            "so": (d // n, d, "rows second", "so", 0),
            "sp": (d // n, 3 * d, "rows second", "sp", 0),
            "sm": (16, 128, "rows last", "sm", 0),
        }
        self.types = {"sm": F32}

    def seq_bits(self, name):
        if self.sums[name][2] == "far first":
            return [0, 2, 1] + list(range(3, self.bits))
        return list(range(self.bits))

    def steps(self, name):
        order = self.sums[name][2]
        seq = [("seq", k) for k in self.seq_bits(name)]
        rows = [("exchange", k) for k in range(self.row_bits)]
        if order == "seq alone":
            return seq
        at = self.halving(name)
        if at is not None:
            return seq[:at] + [("halve", 0)] + seq[at:] + rows[1:] + [("gather", 0)]
        return seq + rows

    def halving(self, name):
        return {"rows second": 1, "rows third": 2}.get(self.sums[name][2])

    def parts(self, name):
        return 1 if self.halving(name) is None else 2

    def received(self, name):
        held, first, spans = self.n * self.parts(name), 0, []
        for kind, _ in self.steps(name):
            held = held // 2 if kind in ("seq", "halve") else held
            spans.append((first, held))
            first += held
        return spans, first

    def scratch(self):
        n, t, mt, d, ff, hd, split = self.n, self.t, self.mt, self.d, self.ff, self.hd, self.split
        v, dma = pltpu.VMEM, pltpu.SemaphoreType.DMA
        spec = dict(
            w_so=v((d, d), BF), w_cq=v((d, d), BF), w_cm=v((d, 2 * d), BF),
            w_co=v((d, d), BF), w_fi=v((d, ff), BF), w_fo=v((ff, d), BF),
            x=v((2 * t, d), BF), mem=v((2 * mt, d), BF), cot=v((2 * t, d), BF),
            dx=v((2 * t, d), F32), codes=v((8, t), I32),
            xg=v((n, t, d), BF), mg=v((n, mt, d), BF), mkv=v((n, mt, 2 * d), BF),
            qkvt=v((HEADS, 3 * hd, t), BF), kv=v((split, HEADS, 2 * hd, t), BF),
            qt=v((HEADS, hd, t), BF), kts=v((hd, n * t), BF), vts=v((hd, n * t), BF),
            ots=v((HEADS, hd, t), BF), otr=v((HEADS, hd, t), BF), of=v((HEADS, t, hd), F32),
            dos=v((HEADS, hd, t), BF), dor=v((HEADS, hd, t), BF), dqr=v((HEADS, hd, t), BF),
            dwt=v((3 * hd, d), F32),
            kvst=v((HEADS, split, 2 * hd, t), BF), kvsib=v((HEADS, split, 2 * hd, t), BF),
            kvfin=v((HEADS, 2 * hd, t), BF), dkvr=v((HEADS, 2 * hd, t), BF),
            dws=v((split, n // split, d // n, 4 * hd), BF), dwsib=v((split, n // split, d // n, 4 * hd), BF),
            dwr=v((HEADS, d // n, 4 * hd), BF),
            dsh=v((d // n, 3 * d), BF), dshr=v((self.row_bits, d // n, 3 * d), BF),
            xw=v((t + self.halo, d), BF), mw=v((2 * mt, d), BF),
            qp=v((t, d), BF), ps=v((t + self.halo, 2 * d), BF), pm=v((2 * mt, 2 * d), BF),
            cp=v((8, t), I32), cn=v((8, t), I32),
            lse=v((t, 4 * HEADS), F32),
            op=v((t, d), F32), co32=v((2 * t, d), F32),
            hss=v((self.halo, d), BF), hsr=v((self.halo, d), BF),
            hms=v((mt, d), BF), hmr=v((mt, d), BF),
            att=v((2 * t, d), BF), catt=v((2 * t, d), BF), cqv=v((2 * t, d), BF),
            tmp=v((2 * t, d), F32), n1=v((2 * t, d), F32), n2=v((2 * t, d), F32),
            i1=v((2 * t, 1), F32), i2=v((2 * t, 1), F32),
            h1b=v((2 * t, d), BF), h2b=v((2 * t, d), BF),
            act=v((2 * t, ff), BF), dg=v((2 * t, ff), F32),
            dtb=v((2 * t, d), BF), dc=v((2 * t, d), BF), dcq=v((2 * t, d), BF),
            dself=v((t, d), BF), dproj=v((t, 3 * d), BF),
            o_out=v((t, 2, d), BF), o_dx=v((t, 2, d), F32), o_dm=v((mt, 2, d), F32),
            o_sp=v((d // n, 3 * d), F32), o_so=v((d // n, d), F32), o_cq=v((d // n, d), F32),
            o_cm=v((d // n, 2 * d), F32), o_co=v((d // n, d), F32),
            o_fi=v((d // n, ff), F32), o_fo=v((ff // n, d), F32),
            sm=v((16, d), F32), o_sm=v((16, 128), F32),
            o_bfi=v((1, ff // n), F32), o_bfo=v((1, d // n), F32),
            o_bgain=v((3, d // n), F32), o_bbias=v((3, d // n), F32), o_bscale=v((3, d // n), F32),
        )
        for name, (r, c, _, _, _) in self.sums.items():
            parts = self.parts(name)
            if name != "mk":
                spec["a_" + name] = v((n * parts, r, c // parts), self.types.get(name, BF))
            spec["r_" + name] = v((self.received(name)[1], r, c // parts), self.types.get(name, BF))
            spec["ss_" + name] = dma
            spec["rs_" + name] = dma((len(self.steps(name)),))
        spec.update(
            wsem=dma((6,)), xgs=dma((4,)), xgr=dma((n,)), mgs=dma((4,)), mgr=dma((n,)),
            hs=dma((8,)), hr=dma((8,)),
            kv_s=dma, kv_r=dma, kw_s=dma((split,)), kw_r=dma((split,)),
            q_s=dma, q_r=dma, o_s=dma, o_r=dma, do_s=dma, do_r=dma,
            dq_s=dma, dq_r=dma, kf_s=dma, kf_r=dma,
            sib_s=dma, sib_r=dma((HEADS, split - 1)),
            ds_s=dma((split,)), ds_r=dma((split,)), dw_s=dma, dw_r=dma,
            outs=dma((len(self.sums) + 8,)), dy_s=dma((self.row_bits,)), dy_r=dma((self.row_bits,)),
        )
        return spec


ORDER = (
    "fo_mm", "fo0", "dpre", "fi_mm", "fi0", "fi1", "fo0", "sb", "fi0", "co_mm", "dc", "co", "xd0", "out",
    "fi1", "xd1", "xp", "co", "fo0", "xd2", "xd3", "fo1", "fi0", "fb", "som", "fo1", "xg3", "smm", "sm",
    "cqm", "cq", "fi1", "so", "psb", "fi0", "spm", "sp", "fo0", "so", "cq", "cmm", "cm", "co", "sm", "fi1",
    "dmp", "sp", "sd7", "co", "fi0", "so", "sm", "sd5", "fo1", "co", "cq", "sd3", "sd1", "sp", "cm", "mkm",
    "so", "dwm", "mk", "dwo", "cm", "co", "fo1", "sm", "sp", "fi0", "mk", "dxp", "fo1", "cq", "sp", "cm",
    "fo0", "sm", "cq", "mk", "sp", "fi0", "cm", "co", "fo1", "so", "fi1", "fin2", "sm", "cq", "mk", "fin1",
    "fo0", "fo1", "cm", "so", "cm", "sp", "cq", "so", "fi1", "mk",
)


class Refs:
    def __init__(self, names, refs):
        for name, ref in zip(names, refs):
            setattr(self, name, ref)


INPUTS = (
    "x_in", "mem_in", "cot_in", "seg_in", "pad_in",
    "h_sp", "h_so", "h_cq", "h_cm", "h_co", "h_fi", "h_fo",
    "fi_b", "fo_b", "gain", "bias", "scale",
)
OUTPUTS = (
    "out", "dx_out", "dm_out", "g_sp", "g_so", "g_cq", "g_cm", "g_co", "g_fi", "g_fo",
    "b_fi", "b_fo", "b_gain", "b_bias", "b_scale",
)


def layer_kernel(z, names, *refs):
    g = Refs(names, refs)
    g.w_sp = g.h_sp
    g.dxp, g.dmp = g.co32.at[pl.ds(0, z.t + z.halo)], g.n2.at[pl.ds(0, 2 * z.mt)]
    n, t, mt, d, ff, hd, split = z.n, z.t, z.mt, z.d, z.ff, z.hd, z.split
    half = 2 * hd
    pairs = d // half
    softmax_scale = 1.0 / math.sqrt(hd)
    s = lax.axis_index("seq")
    r = lax.axis_index("rows")

    def bit_of(index, k):
        return lax.rem(lax.div(index, 2 ** k), 2)

    def seq_partner(k):
        return s + (1 - 2 * bit_of(s, k)) * 2 ** k

    def row_partner(k):
        return r + (1 - 2 * bit_of(r, k)) * 2 ** k

    def place_of(index):
        return sum(bit_of(index, k) * 2 ** (z.bits - 1 - k) for k in range(z.bits))

    nxt = lax.rem(s + 1, n)
    prv = lax.rem(s + n - 1, n)
    my_head = lax.div(s, split)
    my_part = lax.rem(s, split)
    own_turn = lax.div(s, split)
    own_rest = lax.rem(s, split)
    own_part = own_rest + lax.rem(own_turn, 2) * (split - 1 - 2 * own_rest)

    barrier = pltpu.get_barrier_semaphore()
    for step in range(1, n):
        pl.semaphore_signal(barrier, inc=1, device_id=(lax.rem(s + step, n), r), device_id_type=MESH)
    for k in range(z.row_bits):
        pl.semaphore_signal(barrier, inc=1, device_id=(s, row_partner(k)), device_id_type=MESH)

    loads = {
        name: pltpu.make_async_copy(getattr(g, "h_" + name), getattr(g, "w_" + name), g.wsem.at[j])
        for j, name in enumerate(("cm", "so", "cq", "co", "fi", "fo"))
    }

    def remote(src, dst, ssem, rsem, dev):
        return pltpu.make_async_remote_copy(
            src_ref=src, dst_ref=dst, send_sem=ssem, recv_sem=rsem,
            device_id=dev, device_id_type=MESH,
        )

    class Spread:
        def __init__(self, src, dst, ssem, rsem, dest):
            self.dest = dest
            self.far = remote(src, dst, ssem, rsem, (dest, r))
            self.near = pltpu.make_async_copy(src, dst, rsem)

        def start(self):
            @pl.when(self.dest != s)
            def _():
                self.far.start()

            @pl.when(self.dest == s)
            def _():
                self.near.start()

    def wait_whole(ref, sem):
        pltpu.make_async_copy(ref, ref, sem).wait()

    def wait_sent(ref, sem, own):
        count = ref.shape[0]

        @pl.when(own)
        def _():
            wait_whole(ref.at[pl.ds(0, count - 1)], sem)

        @pl.when(jnp.logical_not(own))
        def _():
            wait_whole(ref, sem)

    class Chain:
        def __init__(self, buf, send, recv):
            self.buf, self.send, self.recv = buf, send, recv
            self.line = n // 4
            self.zz, self.xx, self.core = lax.div(s, 4), bit_of(s, 1), bit_of(s, 0)

        def copy(self, way, origin):
            dev = (s + 4, s - 4, s + 2 - 4 * self.xx, s + 1 - 2 * self.core)[way]
            at = place_of(origin)
            block = self.buf.at[at]
            return remote(block, block, self.send.at[way], self.recv.at[at], (dev, r))

        def arrive(self, origin):
            at = place_of(origin)
            wait_whole(self.buf.at[at], self.recv.at[at])

        def pass_on(self, zz, ahead, back):
            origin = s + 4 * (zz - self.zz)
            if ahead:
                @pl.when(self.zz < self.line - 1)
                def _():
                    self.copy(0, origin).start()
            if back:
                @pl.when(self.zz > 0)
                def _():
                    self.copy(1, origin).start()
            self.copy(2, origin).start()
            self.copy(3, origin).start()

        def start(self):
            self.pass_on(self.zz, True, True)

        def step(self, j):
            low, high = self.zz - 1 - j, self.zz + 1 + j

            @pl.when(low >= 0)
            def _():
                self.arrive(s + 4 * (low - self.zz))
                self.pass_on(low, True, False)

            @pl.when(high < self.line)
            def _():
                self.arrive(s + 4 * (high - self.zz))
                self.pass_on(high, False, True)

        def cross_step(self, j):
            other = s + 2 - 4 * self.xx
            for sign in ((1,) if j == 0 else (-1, 1)):
                zz = self.zz + sign * j

                @pl.when((zz >= 0) & (zz < self.line))
                def _():
                    origin = other + 4 * (zz - self.zz)
                    self.arrive(origin)
                    self.copy(3, origin).start()

        def finish(self):
            other = s + 1 - 2 * self.core
            for k in range(2 * self.line):
                self.arrive(lax.rem(other, 2) + 2 * k)

        def drain(self):
            for zz in range(self.line):
                for way, count in ((0, zz + 1 if zz < self.line - 1 else 0), (1, self.line - zz if zz else 0)):
                    if count:
                        @pl.when(self.zz == zz)
                        def _():
                            wait_whole(self.buf.at[pl.ds(0, count)], self.send.at[way])
            wait_whole(self.buf.at[pl.ds(0, self.line)], self.send.at[2])
            wait_whole(self.buf.at[pl.ds(0, 2 * self.line)], self.send.at[3])

    class Sum:
        def __init__(self, name, number):
            self.name, self.number = name, number
            self.share, self.columns, _, target, self.offset = z.sums[name]
            self.out, self.result_at = getattr(g, "o_" + target, None), getattr(g, "g_" + target, None)
            self.a = g.mg if name == "mk" else getattr(g, "a_" + name)
            self.r = getattr(g, "r_" + name)
            self.ss, self.rs = getattr(g, "ss_" + name), getattr(g, "rs_" + name)
            self.steps, self.parts = z.steps(name), z.parts(name)
            self.spans = z.received(name)[0]
            self.copies = {}
            self.at = -1

        def held(self, i):
            if i == 0:
                return self.a, 0, n * self.parts
            return (self.r,) + self.spans[i - 1]

        def bit(self, i):
            kind, k = self.steps[i]
            return bit_of(s, k) if kind == "seq" else bit_of(r, k)

        def start(self, i):
            ref, first, blocks = self.held(i)
            into, into_first, count = self.held(i + 1)
            kind, k = self.steps[i]
            src = ref.at[pl.ds(first + (1 - self.bit(i)) * count, count)] if blocks > count else (
                ref.at[pl.ds(first, count)])
            dev = (seq_partner(k), r) if kind == "seq" else (s, row_partner(k))
            self.copies[i] = remote(src, into.at[pl.ds(into_first, count)], self.ss, self.rs.at[i], dev)
            self.copies[i].start()

        def finish(self, i):
            self.copies[i].wait()
            ref, first, blocks = self.held(i)
            into, into_first, count = self.held(i + 1)
            kind, k = self.steps[i]
            last = i + 1 == len(self.steps)
            if kind == "gather":
                width = self.columns // 2
                mine, theirs = bit_of(r, 0) * width, (1 - bit_of(r, 0)) * width
                self.out[:, pl.ds(pl.multiple_of(self.offset + mine, 128), width)] = ref[first].astype(F32)
                self.out[:, pl.ds(pl.multiple_of(self.offset + theirs, 128), width)] = (
                    into[into_first].astype(F32))
                return
            if last and self.out is not None:
                self.out[:, self.offset:self.offset + self.columns] = (
                    into[into_first].astype(F32) + ref[first].astype(F32))
                return
            base = first + self.bit(i) * count if blocks > count else first
            if count <= 2:
                for j in range(count):
                    into[into_first + j] = into[into_first + j] + ref[base + j]
            else:
                def add(j, carry):
                    into[into_first + j] = into[into_first + j] + ref[base + j]
                    return carry
                lax.fori_loop(0, count, add, 0)

        def output(self):
            cols = pl.ds(self.offset, self.columns)
            return pltpu.make_async_copy(
                self.out.at[:, cols], self.result_at.at[:, cols], g.outs.at[self.number])

        def over(self):
            return self.at == len(self.steps)

        def advance(self):
            if self.over():
                return
            if self.at >= 0:
                self.finish(self.at)
            self.at += 1
            if not self.over():
                self.start(self.at)
            elif self.out is not None and self.name not in ("sp", "sm"):
                self.output().start()

        def result(self):
            ref, first, _ = self.held(len(self.steps))
            return ref[first]

        def put(self, owner, value, first_column):
            width = self.columns // self.parts
            position = sum(
                ((owner >> k) & 1) << (z.bits - 1 - j) for j, k in enumerate(z.seq_bits(self.name)))
            below = n >> (z.halving(self.name) or 0)
            above, rest = position // below, position % below
            for part in range(self.parts):
                start = self.offset + part * width
                low, high = max(first_column, start), min(first_column + value.shape[1], start + width)
                if low < high:
                    where = (above * self.parts + part) * below + rest
                    self.a[where, :, low - start:high - start] = (
                        value[:, low - first_column:high - first_column])

    sums = {name: Sum(name, j) for j, name in enumerate(z.sums)}

    def put_rows(target, value, first_column=0, first_owner=0):
        value = value.astype(BF)
        for name, (share, _, _, output, _) in z.sums.items():
            if output == target:
                for j in range(value.shape[0] // share):
                    sums[name].put(first_owner + j, value[j * share:(j + 1) * share], first_column)

    def over_rows(count, size, step):
        def one(j, carry):
            step(pl.ds(pl.multiple_of(j * size, size), size))
            return carry
        lax.fori_loop(0, count // size, one, 0)

    def mean(value):
        return jnp.sum(value, -1, keepdims=True) * (1.0 / d)

    def norm_forward(total):
        centred = total - mean(total)
        inverse = lax.rsqrt(mean(centred * centred) + EPSILON)
        return centred * inverse, inverse

    def norm_backward(grad, normed, inverse, gain_row, which):
        scaled = grad * gain_row
        result = inverse * (scaled - mean(scaled) - normed * mean(scaled * normed))
        g.sm[which:which + 1, :] += jnp.sum(grad * normed, 0, keepdims=True)
        g.sm[3 + which:4 + which, :] += jnp.sum(grad, 0, keepdims=True)
        return result

    lane = lax.broadcasted_iota(I32, (t, half), 1)

    def only(value, which):
        keep = (lane < hd) if which == 0 else (lane >= hd)
        return jnp.where(keep, value, jnp.zeros_like(value))

    def both(first, second):
        return jnp.where(lane < hd, first, second)

    def pair_cols(p, offset=0):
        return slice(offset + p * half, offset + (p + 1) * half)

    def keep_lse(index, value):
        g.lse[:, index:index + 1] = value

    def kept_lse(index):
        return g.lse[:, index:index + 1]

    SELF_PACKED, CROSS_PACKED, CROSS_DOC, SELF_DOC = (k * HEADS for k in range(4))

    tokens_all = Chain(g.xg, g.xgs, g.xgr)
    memory_all = Chain(g.mg, g.mgs, g.mgr)
    place = place_of(s)
    other_seg = g.seg_in[1:2, :]
    swap = jnp.min(other_seg, -1, keepdims=True) == jnp.max(other_seg, -1, keepdims=True)

    def ordered(ref, into):
        first, second, count = ref[:, 0, :], ref[:, 1, :], ref.shape[0]
        into[0:count, :] = jnp.where(swap, second, first)
        into[count:, :] = jnp.where(swap, first, second)

    def restored(first, second, ref):
        ref[:, 0, :] = jnp.where(swap, second, first)
        ref[:, 1, :] = jnp.where(swap, first, second)

    ordered(g.x_in, g.x)
    for load in loads.values():
        load.start()

    for part in range(3):
        made = nn(g.x[0:t, :], g.w_sp[:, part * d:(part + 1) * d]).astype(BF)
        g.qkvt[:, part * hd:(part + 1) * hd, :] = made.T.reshape(HEADS, hd, t)
    pl.semaphore_wait(barrier, n - 1 + z.row_bits)
    for h in range(HEADS):
        Spread(g.qkvt.at[h, pl.ds(hd, 2 * hd)], g.kv.at[my_part, own_turn], g.kv_s, g.kv_r,
               h * split + my_part).start()
    for h in range(HEADS):
        Spread(g.qkvt.at[h, pl.ds(0, hd)], g.qt.at[own_turn], g.q_s, g.q_r, h * split + own_part).start()
    ordered(g.mem_in, g.mem)
    seg = jnp.where(swap, g.seg_in[0:1, :], other_seg)
    pad = jnp.where(swap, g.pad_in[0:1, :], g.pad_in[1:2, :])
    q_at = lax.broadcasted_iota(I32, (t, t), 0)
    k_at = lax.broadcasted_iota(I32, (t, t), 1)
    seg_q = jnp.sum(jnp.where(q_at == k_at, seg.astype(F32), 0.0), -1, keepdims=True).astype(I32)
    pick = (q_at == 2 * lax.rem(k_at + z.mhalo, mt)).astype(F32)
    mem_seg = jnp.dot(
        jnp.broadcast_to(seg.astype(F32), (8, t)), pick,
        precision=lax.Precision.HIGHEST, preferred_element_type=F32).astype(I32)
    g.codes[0:1, :] = seg
    g.codes[1:2, :] = pad
    g.codes[2:3, :] = pltpu.roll(seg, z.halo, 1)
    g.codes[3:4, :] = pltpu.roll(pad, z.halo, 1)
    g.codes[4:8, :] = mem_seg[0:4]
    g.xg[place] = g.x[0:t, :]
    g.mg[place] = g.mem[0:mt, :]
    g.xw[0:t, :] = g.x[t:, :]
    g.mw[z.mhalo:z.mhalo + mt, :] = g.mem[mt:, :]
    halo_copies = [
        remote(g.codes, g.cn, g.hs.at[0], g.hr.at[0], (prv, r)),
        remote(g.codes, g.cp, g.hs.at[1], g.hr.at[1], (nxt, r)),
        remote(g.x.at[pl.ds(2 * t - z.halo, z.halo)], g.xw.at[pl.ds(t, z.halo)],
               g.hs.at[2], g.hr.at[2], (nxt, r)),
        remote(g.mem.at[pl.ds(mt, z.mhalo)], g.mw.at[pl.ds(z.mhalo + mt, z.mhalo)],
               g.hs.at[3], g.hr.at[3], (prv, r)),
        remote(g.mem.at[pl.ds(2 * mt - z.mhalo, z.mhalo)], g.mw.at[pl.ds(0, z.mhalo)],
               g.hs.at[4], g.hr.at[4], (nxt, r)),
    ]
    for copy in halo_copies:
        copy.start()

    memory_all.start()

    g.qp[...] = nn(g.xw[0:t, :], g.w_sp[:, :d]).astype(BF)
    ordered(g.cot_in, g.cot)
    g.sm[...] = jnp.zeros_like(g.sm)

    def self_mask():
        seg_k, pad_k = g.codes[0:1, :], g.codes[1:2, :]
        own = (seg_q == seg_k) & (k_at <= q_at) & ((pad_k == 1) | (k_at == q_at))
        prev = (seg_q == g.cp[2:3, :]) & (g.cp[3:4, :] == 1)
        return own, prev[:, :z.halo]

    def cross_mask():
        at = lax.broadcasted_iota(I32, (1, 2 * mt), 1)
        seg_k = jnp.where(
            at < z.mhalo, g.cp[4:5, :],
            jnp.where(at < z.mhalo + mt, g.codes[4:5, :], g.cn[4:5, :]))
        return seg_q == seg_k

    def softmax_parts(scores):
        top = functools.reduce(jnp.maximum, [jnp.max(b, -1, keepdims=True) for b in scores])
        weights = [jnp.exp(b - top) for b in scores]
        total = functools.reduce(jnp.add, [jnp.sum(w, -1, keepdims=True) for w in weights])
        return weights, total, top + jnp.log(total)

    def hand_over(f):
        return remote(g.kv.at[my_part], g.kv.at[my_part], g.kw_s.at[f], g.kw_r.at[my_part],
                      (my_head * split + f, r))

    wait_whole(g.kv.at[my_part], g.kv_r)
    for f in range(split):
        @pl.when(my_part != f)
        def _():
            hand_over(f).start()
    wait_whole(g.qt, g.q_r)
    for f in range(split):
        @pl.when(my_part != f)
        def _():
            wait_whole(g.kv.at[f], g.kw_r.at[f])
    for b in range(n):
        g.kts[:, b * t:(b + 1) * t] = g.kv[b % split, b // split, 0:hd]
        g.vts[:, b * t:(b + 1) * t] = g.kv[b % split, b // split, hd:]

    wide = split * t
    diag_q = lax.broadcasted_iota(I32, (t, wide), 0)
    diag_k = lax.broadcasted_iota(I32, (t, wide), 1)

    def turn_rest(i):
        return my_part if i % 2 == 0 else split - 1 - my_part

    def diag_mask(i):
        return diag_k <= diag_q + turn_rest(i) * t

    def attend_document(i):
        q = g.qt[i].T
        low = i * wide
        blocks = []
        if low:
            blocks.append(nn(q, g.kts[:, :low]) * softmax_scale)
        blocks.append(jnp.where(
            diag_mask(i), nn(q, g.kts[:, low:low + wide]) * softmax_scale, NEGATIVE))
        weights, total, lse = softmax_parts(blocks)
        keep_lse(SELF_DOC + i, lse)
        o = nt(weights[-1].astype(BF), g.vts[:, low:low + wide])
        if low:
            o = o + nt(weights[0].astype(BF), g.vts[:, :low])
        o = o / total
        g.of[i] = o
        g.ots[i] = o.T.astype(BF)

    for turns in ((0, 1, 2, 3), (4, 5), (6, 7)):
        for i in turns:
            attend_document(i)
        if turns[0] == 0:
            memory_all.step(0)
        for i in turns:
            Spread(g.ots.at[i], g.otr.at[my_head], g.o_s, g.o_r, i * split + turn_rest(i)).start()
    memory_all.cross_step(0)

    for copy in halo_copies:
        copy.wait()
    g.ps[...] = nn(g.xw[...], g.w_sp[:, d:]).astype(BF)
    loads["cm"].wait()
    g.pm[...] = nn(g.mw[...], g.w_cm[...]).astype(BF)
    for j in range(1, n // 4 - 2):
        memory_all.step(j)

    own_mask, prev_mask = self_mask()
    for p in range(pairs):
        q, k, v = g.qp[:, pair_cols(p)], g.ps[:, pair_cols(p)], g.ps[:, pair_cols(p, d)]
        outs = []
        for w in range(2):
            sc = nt(only(q, w), k) * softmax_scale
            blocks = [jnp.where(own_mask, sc[:, :t], NEGATIVE), jnp.where(prev_mask, sc[:, t:], NEGATIVE)]
            weights, total, lse = softmax_parts(blocks)
            keep_lse(SELF_PACKED + 2 * p + w, lse)
            o = nn(weights[0].astype(BF), v[:t]) + nn(weights[1].astype(BF), v[t:])
            outs.append(o / total)
        o = both(*outs)
        g.op[:, pair_cols(p)] = o
        g.att[t:, pair_cols(p)] = o.astype(BF)

    for j in range(1, n // 4 - 2):
        memory_all.cross_step(j)
    memory_all.step(n // 4 - 2)

    loads["so"].wait()
    wait_whole(g.otr, g.o_r)
    g.att[0:t, :] = g.otr[...].reshape(d, t).T
    g.tmp[...] = nn(g.att[...], g.w_so[...])

    def first_norm(rows):
        total = g.x[rows, :].astype(F32) * g.scale[0:1, :] + g.tmp[rows, :]
        normed, inverse = norm_forward(total)
        g.n1[rows, :] = normed
        g.i1[rows, :] = inverse
        g.h1b[rows, :] = (normed * g.gain[0:1, :] + g.bias[0:1, :]).astype(BF)

    over_rows(2 * t, 256, first_norm)
    memory_all.cross_step(n // 4 - 2)
    tokens_all.start()
    loads["cq"].wait()
    g.cqv[...] = nn(g.h1b[...], g.w_cq[...]).astype(BF)

    seen = cross_mask()
    for p in range(pairs):
        q, k, v = g.cqv[t:, pair_cols(p)], g.pm[:, pair_cols(p)], g.pm[:, pair_cols(p, d)]
        outs = []
        for w in range(2):
            sc = jnp.where(seen, nt(only(q, w), k) * softmax_scale, NEGATIVE)
            (weights,), total, lse = softmax_parts([sc])
            keep_lse(CROSS_PACKED + 2 * p + w, lse)
            outs.append(nn(weights.astype(BF), v) / total)
        o = both(*outs)
        g.co32[t:, pair_cols(p)] = o
        g.catt[t:, pair_cols(p)] = o.astype(BF)
    memory_all.cross_step(n // 4 - 1)
    memory_all.finish()

    for part in range(2):
        cols = slice(part * d, (part + 1) * d)
        g.mkv[:, :, cols] = nn(g.mg[...].reshape(n * mt, d), g.w_cm[:, cols]).astype(BF).reshape(n, mt, d)

    tokens_all.step(0)
    tokens_all.cross_step(0)

    for p in range(pairs):
        q = g.cqv[0:t, pair_cols(p)]
        k = g.mkv[:, :, pair_cols(p)].reshape(n * mt, half)
        v = g.mkv[:, :, pair_cols(p, d)].reshape(n * mt, half)
        outs = []
        for w in range(2):
            sc = nt(only(q, w), k) * softmax_scale
            (weights,), total, lse = softmax_parts([sc])
            keep_lse(CROSS_DOC + 2 * p + w, lse)
            outs.append(nn(weights.astype(BF), v) / total)
        o = both(*outs)
        g.co32[0:t, pair_cols(p)] = o
        g.catt[0:t, pair_cols(p)] = o.astype(BF)
    stays = own_part == my_part
    wait_whole(g.kvfin.at[pl.ds(0, HEADS - 1)], g.kv_s)
    wait_sent(g.qt, g.q_s, stays)
    wait_sent(g.ots, g.o_s, stays)
    for f in range(split):
        @pl.when(my_part != f)
        def _():
            hand_over(f).wait_send()
    memory_all.drain()

    loads["co"].wait()
    g.tmp[...] = nn(g.catt[...], g.w_co[...])

    def second_norm(rows):
        hidden1 = g.n1[rows, :] * g.gain[0:1, :] + g.bias[0:1, :]
        normed, inverse = norm_forward(hidden1 * g.scale[1:2, :] + g.tmp[rows, :])
        g.n2[rows, :] = normed
        g.i2[rows, :] = inverse
        g.h2b[rows, :] = (normed * g.gain[1:2, :] + g.bias[1:2, :]).astype(BF)

    over_rows(2 * t, 256, second_norm)

    loads["fi"].wait()
    chunks = ff // d
    for c in range(chunks):
        cols = slice(c * d, (c + 1) * d)
        pre = nn(g.h2b[...], g.w_fi[:, cols]) + g.fi_b[0:1, cols]
        square = pre * pre
        bent = jnp.tanh(GELU_A * pre * (1.0 + GELU_B * square))
        g.act[:, cols] = (0.5 * pre * (1.0 + bent)).astype(BF)
        g.dg[:, cols] = 0.5 * (1.0 + bent) + 0.5 * pre * (1.0 - bent * bent) * (
            GELU_A * (1.0 + 3.0 * GELU_B * square))
    tokens_all.step(1)
    loads["fo"].wait()
    g.tmp[...] = nn(g.act[...], g.w_fo[...])

    def third_norm(rows):
        hidden2 = g.n2[rows, :] * g.gain[1:2, :] + g.bias[1:2, :]
        total = hidden2 * g.scale[2:3, :] + (g.tmp[rows, :] + g.fo_b[0:1, :])
        normed, inverse = norm_forward(total)
        grad = g.cot[rows, :].astype(F32)
        g.cot[rows, :] = (normed * g.gain[2:3, :] + g.bias[2:3, :]).astype(BF)
        back = norm_backward(grad, normed, inverse, g.gain[2:3, :], 2)
        g.sm[8:9, :] += jnp.sum(back * hidden2, 0, keepdims=True)
        g.dx[rows, :] = back
        low = back.astype(BF)
        g.dtb[rows, :] = low
        g.sm[9:10, :] += jnp.sum(low.astype(F32), 0, keepdims=True)

    over_rows(2 * t, 128, third_norm)
    tokens_all.cross_step(1)
    tokens_all.step(2)

    for j in range(3, n // 4 - 1):
        tokens_all.step(j)
        tokens_all.cross_step(j)

    def feed_out_grads():
        for c in range(chunks):
            cols = slice(c * d, (c + 1) * d)
            put_rows("fo", nn(g.act[:, cols].T, g.dtb[...]), 0, c * d // z.sums["fo0"][0])

    def before_gelu():
        for c in range(chunks):
            cols = slice(c * d, (c + 1) * d)
            back = (nt(g.dtb[...], g.w_fo[cols, :]) * g.dg[:, cols]).astype(BF)
            g.act[:, cols] = back
            g.sm[10 + c:11 + c, :] = jnp.sum(back.astype(F32), 0, keepdims=True)

    def feed_in_grads():
        h2t = g.h2b[...].T
        for c in range(chunks):
            cols = slice(c * d, (c + 1) * d)
            put_rows("fi", nn(h2t, g.act[:, cols]), c * d)

    def second_norm_back():
        g.tmp[...] = nt(g.act[...], g.w_fi[...])

        def second_back(rows):
            grad = g.dx[rows, :] * g.scale[2:3, :] + g.tmp[rows, :]
            back = norm_backward(grad, g.n2[rows, :], g.i2[rows, :], g.gain[1:2, :], 1)
            hidden1 = g.n1[rows, :] * g.gain[0:1, :] + g.bias[0:1, :]
            g.sm[7:8, :] += jnp.sum(back * hidden1, 0, keepdims=True)
            g.dx[rows, :] = back
            g.dtb[rows, :] = back.astype(BF)

        over_rows(2 * t, 128, second_back)

    def cross_output_back():
        g.dc[...] = nt(g.dtb[...], g.w_co[...]).astype(BF)

    def cross_output_grads():
        put_rows("co", nn(g.catt[...].T, g.dtb[...]))

    def result_out():
        restored(g.cot[0:t, :], g.cot[t:, :], g.o_out)
        pltpu.make_async_copy(g.o_out, g.out, g.outs.at[len(z.sums)]).start()

    def cross_document(p):
        q, go, o = g.cqv[0:t, pair_cols(p)], g.dc[0:t, pair_cols(p)], g.co32[0:t, pair_cols(p)]
        qt, gt = q.T, go.T
        k = g.mkv[:, :, pair_cols(p)].reshape(n * mt, half)
        v = g.mkv[:, :, pair_cols(p, d)].reshape(n * mt, half)
        dqs, dks, dvs = [], [], []
        for w in range(2):
            qm, gm = only(q, w), only(go, w)
            weights = jnp.exp(nt(qm, k) * softmax_scale - kept_lse(CROSS_DOC + 2 * p + w))
            delta = jnp.sum(gm.astype(F32) * o, -1, keepdims=True)
            ds = (weights * (nt(gm, v) - delta)).astype(BF)
            dqs.append(nn(ds, k))
            dks.append(nn(qt[w * hd:(w + 1) * hd], ds))
            dvs.append(nn(gt[w * hd:(w + 1) * hd], weights.astype(BF)))
        g.dcq[0:t, pair_cols(p)] = (both(*dqs) * softmax_scale).astype(BF)
        dk = (jnp.concatenate(dks, 0) * softmax_scale).astype(BF).T
        dv = jnp.concatenate(dvs, 0).astype(BF).T
        g.mkv[:, :, pair_cols(p)] = dk.reshape(n, mt, half)
        g.mkv[:, :, pair_cols(p, d)] = dv.reshape(n, mt, half)

    def cross_packed():
        for p in range(pairs):
            q, k, v = g.cqv[t:, pair_cols(p)], g.pm[:, pair_cols(p)], g.pm[:, pair_cols(p, d)]
            go, o = g.dc[t:, pair_cols(p)], g.co32[t:, pair_cols(p)]
            dqs, dk, dv = [], 0.0, 0.0
            for w in range(2):
                qm, gm = only(q, w), only(go, w)
                weights = jnp.where(
                    seen, jnp.exp(nt(qm, k) * softmax_scale - kept_lse(CROSS_PACKED + 2 * p + w)), 0.0)
                delta = jnp.sum(gm.astype(F32) * o, -1, keepdims=True)
                ds = (weights * (nt(gm, v) - delta)).astype(BF)
                dqs.append(nn(ds, k))
                dk = dk + tn(ds, qm)
                dv = dv + tn(weights.astype(BF), gm)
            g.dcq[t:, pair_cols(p)] = (both(*dqs) * softmax_scale).astype(BF)
            g.pm[:, pair_cols(p)] = (dk * softmax_scale).astype(BF)
            g.pm[:, pair_cols(p, d)] = dv.astype(BF)

    late = {}

    def first_norm_back():
        g.tmp[...] = nt(g.dcq[...], g.w_cq[...])

        def first_back(rows):
            grad = g.dx[rows, :] * g.scale[1:2, :] + g.tmp[rows, :]
            back = norm_backward(grad, g.n1[rows, :], g.i1[rows, :], g.gain[0:1, :], 0)
            g.sm[6:7, :] += jnp.sum(back * g.x[rows, :].astype(F32), 0, keepdims=True)
            g.dx[rows, :] = back
            g.dtb[rows, :] = back.astype(BF)

        over_rows(2 * t, 128, first_back)
        d_self = nt(g.dtb[...], g.w_so[...]).astype(BF)
        g.dself[...] = d_self[t:]
        g.dos[...] = d_self[:t].T.reshape(HEADS, hd, t)
        for h in range(HEADS):
            Spread(g.dos.at[h], g.dor.at[own_turn], g.do_s, g.do_r, h * split + own_part).start()

    def small_sums():
        share, bias_share = d // n, ff // n
        for o in range(n):
            first, bias_first = o * share, o * bias_share
            row = 10 + bias_first // d
            tile = g.sm[:, first // 128 * 128:first // 128 * 128 + 128]
            if first % 128:
                tile = pltpu.roll(tile, 128 - first % 128, 1)
            bias = g.sm[row:row + 1, bias_first % d // 128 * 128:bias_first % d // 128 * 128 + 128]
            if bias_first % 128:
                bias = pltpu.roll(bias, 128 - bias_first % 128, 1)
            sums["sm"].put(o, jnp.concatenate([tile[0:10], bias, tile[11:16]], 0), 0)

    def cross_memory_grads():
        mem_t = g.mg[...].reshape(n * mt, d).T
        win_t = g.mw[...].T
        for part in range(2):
            cols = slice(part * d, (part + 1) * d)
            doc_kv = g.mkv[:, :, cols].reshape(n * mt, d)
            put_rows("cm", nn(mem_t, doc_kv) + nn(win_t, g.pm[:, cols]), part * d)

    def memory_back():
        g.mg[...] = nt(g.mkv[...].reshape(n * mt, 2 * d), g.w_cm[...]).astype(BF).reshape(n, mt, d)

    def memory_halo():
        g.dmp[...] = nt(g.pm[...], g.w_cm[...])
        g.hms[0:z.mhalo, :] = g.dmp[0:z.mhalo, :].astype(BF)
        g.hms[z.mhalo:, :] = g.dmp[z.mhalo + mt:, :].astype(BF)
        late["memory"] = [
            remote(g.hms.at[pl.ds(0, z.mhalo)], g.hmr.at[pl.ds(z.mhalo, z.mhalo)],
                   g.hs.at[5], g.hr.at[5], (prv, r)),
            remote(g.hms.at[pl.ds(z.mhalo, z.mhalo)], g.hmr.at[pl.ds(0, z.mhalo)],
                   g.hs.at[6], g.hr.at[6], (nxt, r)),
        ]
        for copy in late["memory"]:
            copy.start()

    def cross_query_grads():
        put_rows("cq", nn(g.h1b[...].T, g.dcq[...]))

    def self_output_grads():
        put_rows("so", nn(g.att[...].T, g.dtb[...]))

    def self_packed():
        for p in range(pairs):
            q, k, v = g.qp[:, pair_cols(p)], g.ps[:, pair_cols(p)], g.ps[:, pair_cols(p, d)]
            go, o = g.dself[:, pair_cols(p)], g.op[:, pair_cols(p)]
            dqs, dk, dv = [], 0.0, 0.0
            for w in range(2):
                qm, gm = only(q, w), only(go, w)
                sc = nt(qm, k) * softmax_scale - kept_lse(SELF_PACKED + 2 * p + w)
                weights = jnp.concatenate(
                    [jnp.where(own_mask, jnp.exp(sc[:, :t]), 0.0),
                     jnp.where(prev_mask, jnp.exp(sc[:, t:]), 0.0)], 1)
                delta = jnp.sum(gm.astype(F32) * o, -1, keepdims=True)
                ds = (weights * (nt(gm, v) - delta)).astype(BF)
                dqs.append(nn(ds, k))
                dk = dk + tn(ds, qm)
                dv = dv + tn(weights.astype(BF), gm)
            g.qp[:, pair_cols(p)] = (both(*dqs) * softmax_scale).astype(BF)
            g.ps[:, pair_cols(p)] = (dk * softmax_scale).astype(BF)
            g.ps[:, pair_cols(p, d)] = dv.astype(BF)

    def self_project_grads():
        window_t = g.xw[...].T
        put_rows("sp", nn(window_t[:, :t], g.qp[...]), 0)
        put_rows("sp", nn(window_t, g.ps[:, :d]), d)
        put_rows("sp", nn(window_t, g.ps[:, d:]), 2 * d)

    def tokens_halo():
        g.dxp[...] = nt(g.ps[...], g.w_sp[:, d:])
        g.hss[...] = g.dxp[t:, :].astype(BF)
        late["tokens"] = remote(g.hss, g.hsr, g.hs.at[7], g.hr.at[7], (prv, r))
        late["tokens"].start()
        g.tmp[t:, :] = nt(g.qp[...], g.w_sp[:, :d]) + g.dxp[0:t, :]

    chunk = min(512, n * t)

    def kept(which, first, last):
        row, column = first // ff * 2 * hd + which * hd, first % ff
        return slice(row, row + hd), slice(column, column + last - first)

    def sibling(i, f):
        return remote(
            g.kvst.at[i, f], g.kvsib.at[i, my_part], g.sib_s,
            g.sib_r.at[i, lax.rem(my_part - f + split, split) - 1], (my_head * split + f, r))

    def to_siblings(action):
        for f in range(split):
            @pl.when(my_part != f)
            def _():
                action(f)

    def close_kv(i):
        g.kvfin[i] = g.kvst[i, my_part]

        def add(f):
            wait_whole(g.kvsib.at[i, f], g.sib_r.at[i, lax.rem(f - my_part + split, split) - 1])
            g.kvfin[i] = g.kvfin[i] + g.kvsib[i, f]

        to_siblings(add)
        Spread(g.kvfin.at[i], g.dkvr.at[my_head], g.kf_s, g.kf_r, i * split + my_part).start()

    def attend_document_back(i):
        b = i * split + turn_rest(i)
        qt, gt = g.qt[i], g.dor[i]
        q, go = qt.T, gt.T
        delta = jnp.sum(go.astype(F32) * g.of[i], -1, keepdims=True)
        lse = kept_lse(SELF_DOC + i)
        low = i * wide
        spans = [(a, min(a + chunk, low), False) for a in range(0, low, chunk)]
        spans.append((low, low + wide, True))
        dq = 0.0
        for first, last, masked in spans:
            k, v = g.kts[:, first:last], g.vts[:, first:last]
            weights = jnp.exp(nn(q, k) * softmax_scale - lse)
            if masked:
                weights = jnp.where(diag_mask(i), weights, 0.0)
            ds = (weights * (nn(go, v) - delta)).astype(BF)
            dq = dq + nt(ds, k)
            g.dg[kept(0, first, last)] += nn(qt, ds)
            g.dg[kept(1, first, last)] += nn(gt, weights.astype(BF))
        dqt = (dq * softmax_scale).T.astype(BF)
        g.ots[i] = dqt
        for f in range(split):
            first = (i * split + f) * t
            g.kvst[i, f, 0:hd] = (g.dg[kept(0, first, first + t)] * softmax_scale).astype(BF)
            g.kvst[i, f, hd:] = g.dg[kept(1, first, first + t)].astype(BF)
        g.dwt[0:hd, :] += nn(dqt, g.xg[place_of(b)])
        for f in range(split):
            g.dwt[hd:, :] += nn(g.kvst[i, f], g.xg[reverse_static(i * split + f, z.bits)])

    def self_document(turns):
        if turns[0] == HEADS - 1:
            tokens_all.finish()
            tokens_all.drain()
            wait_whole(g.dor, g.do_r)
            g.dg[...] = jnp.zeros_like(g.dg)
            g.dwt[...] = jnp.zeros_like(g.dwt)
        for i in turns:
            attend_document_back(i)
        for i in turns:
            Spread(g.ots.at[i], g.dqr.at[my_head], g.dq_s, g.dq_r, i * split + turn_rest(i)).start()
            to_siblings(lambda f: sibling(i, f).start())
        for i in late.get("turns", ()):
            close_kv(i)
        late["turns"] = turns

    def head_parts(f):
        return remote(g.dws.at[f], g.dwsib.at[my_part], g.ds_s.at[f], g.ds_r.at[my_part],
                      (my_head * split + f, r))

    def head_grads():
        whole = jnp.concatenate([g.dwt[...], jnp.zeros((hd, d), F32)], 0).T.astype(BF)
        share = d // n
        for o in range(n):
            g.dws[o % split, o // split] = whole[o * share:(o + 1) * share]
        to_siblings(lambda f: head_parts(f).start())

    def head_owners():
        for i in late["turns"]:
            close_kv(i)

        def add(f):
            wait_whole(g.dwsib.at[f], g.ds_r.at[f])
            g.dws[my_part] = g.dws[my_part] + g.dwsib[f]

        to_siblings(add)
        for j in range(HEADS):
            Spread(g.dws.at[my_part, j], g.dwr.at[my_head], g.dw_s, g.dw_r, j * split + my_part).start()

    def tokens_back():
        wait_whole(g.dqr, g.dq_r)
        g.dproj[:, 0:d] = g.dqr[...].reshape(d, t).T
        wait_whole(g.dkvr, g.kf_r)
        for part in range(2):
            g.dproj[:, (part + 1) * d:(part + 2) * d] = (
                g.dkvr[:, part * hd:(part + 1) * hd, :].reshape(d, t).T)
        g.tmp[0:t, :] = nt(g.dproj[...], g.w_sp[...])
        late["tokens"].wait()
        g.tmp[2 * t - z.halo:, :] += g.hsr[...].astype(F32)

        def last(rows):
            g.dx[rows, :] = g.dx[rows, :] * g.scale[0:1, :] + g.tmp[rows, :]

        over_rows(2 * t, 128, last)
        restored(g.dx[0:t, :], g.dx[t:, :], g.o_dx)
        pltpu.make_async_copy(g.o_dx, g.dx_out, g.outs.at[len(z.sums) + 1]).start()

    def shares(k):
        return remote(g.dsh, g.dshr.at[k], g.dy_s.at[k], g.dy_r.at[k], (s, row_partner(k)))

    def head_shares():
        wait_whole(g.dwr, g.dw_r)
        for p in range(pairs):
            left, right = g.dwr[2 * p], g.dwr[2 * p + 1]
            for part in range(3):
                cols = slice(part * hd, (part + 1) * hd)
                g.dsh[:, pair_cols(p, part * d)] = jnp.concatenate([left[:, cols], right[:, cols]], 1)
        shares(0).start()

    def rest_of_tokens():
        tokens_all.cross_step(2)
        tokens_all.cross_step(n // 4 - 1)

    pieces = dict(
        fo_mm=feed_out_grads, dpre=before_gelu, fi_mm=feed_in_grads, sb=second_norm_back,
        dc=cross_output_back, co_mm=cross_output_grads, out=result_out, xp=cross_packed,
        fb=first_norm_back, cmm=cross_memory_grads, mkm=memory_back, dmp=memory_halo,
        cqm=cross_query_grads, smm=small_sums, som=self_output_grads, psb=self_packed, spm=self_project_grads,
        dxp=tokens_halo, dwm=head_grads, dwo=head_owners, fin1=tokens_back, fin2=head_shares,
        xg3=rest_of_tokens,
    )
    for p in range(pairs):
        pieces["xd%d" % p] = functools.partial(cross_document, p)
    for i in range(1, HEADS, 2):
        pieces["sd%d" % i] = functools.partial(self_document, (i, i - 1))
    for name in ORDER:
        if name in pieces:
            pieces[name]()
        else:
            sums[name].advance()

    for k in range(z.row_bits - 1):
        shares(k).wait()
        g.dsh[...] = g.dsh[...] + g.dshr[k]
        shares(k + 1).start()
    while not all(one.over() for one in sums.values()):
        for one in sums.values():
            one.advance()
    for copy in late["memory"]:
        copy.wait()
    restored(sums["mk"].result().astype(F32),
             g.dmp[z.mhalo:z.mhalo + mt, :] + g.hmr[...].astype(F32), g.o_dm)
    pltpu.make_async_copy(g.o_dm, g.dm_out, g.outs.at[len(z.sums) + 2]).start()
    small = g.o_sm[...]
    g.o_bgain[...] = small[0:3, :d // n]
    g.o_bbias[...] = small[3:6, :d // n]
    g.o_bscale[...] = small[6:9, :d // n]
    g.o_bfo[...] = small[9:10, :d // n]
    g.o_bfi[...] = small[10:11, :ff // n]
    small_copies = [
        pltpu.make_async_copy(src, dst, g.outs.at[len(z.sums) + 3 + j])
        for j, (src, dst) in enumerate((
            (g.o_bgain, g.b_gain), (g.o_bbias, g.b_bias), (g.o_bscale, g.b_scale),
            (g.o_bfo, g.b_fo), (g.o_bfi, g.b_fi)))
    ]
    for copy in small_copies:
        copy.start()
    shares(z.row_bits - 1).wait()
    g.o_sp[...] = g.o_sp[...] + (g.dsh[...].astype(F32) + g.dshr[z.row_bits - 1].astype(F32))
    sums["sp"].output().start()
    wait_sent(g.dos, g.do_s, stays)
    wait_sent(g.ots, g.dq_s, stays)
    wait_whole(g.kvfin.at[pl.ds(0, HEADS - 1)], g.kf_s)
    wait_whole(g.dws.at[0, pl.ds(0, HEADS - 1)], g.dw_s)
    wait_whole(g.kvst.at[:, pl.ds(0, split - 1)], g.sib_s)
    to_siblings(lambda f: head_parts(f).wait_send())

    for copy in small_copies:
        copy.wait()
    for one in sums.values():
        if one.out is not None and one.name != "sm":
            one.output().wait()
    for j, (src, dst) in enumerate(((g.o_out, g.out), (g.o_dx, g.dx_out), (g.o_dm, g.dm_out))):
        pltpu.make_async_copy(src, dst, g.outs.at[len(z.sums) + j]).wait()


def on_device(
    mesh_shape,
    tokens, memory, segments, padding, cotangent,
    self_project, self_output, cross_query, cross_memory, cross_output,
    feed_in, feed_in_bias, feed_out, feed_out_bias, norm_gain, norm_bias, residual_scale,
):
    t, _, d = tokens.shape
    mt = memory.shape[0]
    ff = feed_in.shape[1]
    n, rows = mesh_shape
    z = Sizes(n, rows, t, mt, d, ff)

    scratch = z.scratch()
    names = INPUTS + OUTPUTS + tuple(scratch)
    vmem, anywhere = pl.BlockSpec(memory_space=pltpu.VMEM), pl.BlockSpec(memory_space=pl.ANY)
    shapes = [
        jax.ShapeDtypeStruct((t, 2, d), BF),
        jax.ShapeDtypeStruct((t, 2, d), F32),
        jax.ShapeDtypeStruct((mt, 2, d), F32),
    ] + [
        jax.ShapeDtypeStruct(shape, F32)
        for shape in (
            (d // n, 3 * d), (d // n, d), (d // n, d), (d // n, 2 * d), (d // n, d), (d // n, ff), (ff // n, d))
    ] + [
        jax.ShapeDtypeStruct((1, ff // n), F32), jax.ShapeDtypeStruct((1, d // n), F32),
    ] + [jax.ShapeDtypeStruct((3, d // n), F32)] * 3
    outcome = pl.pallas_call(
        functools.partial(layer_kernel, z, names),
        out_shape=shapes,
        in_specs=[vmem] * 6 + [anywhere] * 6 + [vmem] * 5,
        out_specs=[anywhere] * len(OUTPUTS),
        scratch_shapes=list(scratch.values()),
        compiler_params=pltpu.CompilerParams(
            collective_id=0, has_side_effects=True, vmem_limit_bytes=63 * 2 ** 20),
        name="layer",
    )(
        tokens, memory, cotangent, segments, padding,
        self_project, self_output, cross_query, cross_memory, cross_output, feed_in, feed_out,
        feed_in_bias.reshape(1, ff), feed_out_bias.reshape(1, d), norm_gain, norm_bias, residual_scale,
    )

    def hand_on(*refs):
        count = len(shapes)
        sources, results, held, sems = refs[:count], refs[count:2 * count], refs[2 * count:-1], refs[-1]
        into = [pltpu.make_async_copy(a, b, sems.at[0, j]) for j, (a, b) in enumerate(zip(sources, held))]
        out = [pltpu.make_async_copy(a, b, sems.at[1, j]) for j, (a, b) in enumerate(zip(held, results))]
        for copy in into:
            copy.start()
        for one, two in zip(into, out):
            one.wait()
            two.start()
        for copy in out:
            copy.wait()

    outcome = pl.pallas_call(
        hand_on,
        out_shape=shapes,
        in_specs=[anywhere] * len(shapes),
        out_specs=[anywhere] * len(shapes),
        scratch_shapes=[pltpu.VMEM(one.shape, one.dtype) for one in shapes] + [
            pltpu.SemaphoreType.DMA((2, len(shapes)))],
        name="results",
    )(*outcome)
    (out, dx, dm, g_sp, g_so, g_cq, g_cm, g_co, g_fi, g_fo,
     in_bias, out_bias, gain, bias, scale) = outcome
    return (
        out, dx, dm, g_sp, g_so, g_cq, g_cm, g_co, g_fi, in_bias.reshape(ff // n),
        g_fo, out_bias.reshape(d // n), gain, bias, scale,
    )


def solution(mesh):
    in_specs = (
        P("seq", "rows", None), P("seq", "rows", None), P("rows", "seq"), P("rows", "seq"),
        P("seq", "rows", None),
    ) + (P(),) * 12
    out_specs = (P("seq", "rows", None),) * 3 + (
        P("seq", None), P("seq", None), P("seq", None), P("seq", None), P("seq", None),
        P("seq", None), P("seq"), P("seq", None), P("seq"),
        P(None, "seq"), P(None, "seq"), P(None, "seq"),
    )
    shape = (mesh.shape["seq"], mesh.shape["rows"])
    return jax.shard_map(
        functools.partial(on_device, shape),
        mesh=mesh, in_specs=in_specs, out_specs=out_specs, check_vma=False,
    )
```
